32 devices in a mesh: dp: 16 (over z, x, core), mp: 2 (over y).
Axes of the slice: x: 2, y: 2, z: 4, core: 2. Of those that a mesh axis runs over, the one named last changes fastest.
Arguments:
- inputs: bfloat16 [16384, 1024], P(('dp', 'mp')), may hold values from -6 to 6
- cotangent: bfloat16 [16384, 1024], P(('dp', 'mp')), may hold values from -6 to 6
- lengths: int32 [16], P('dp'), may hold values from 102 to 1024, as said below
- buckets: int32 [2047], replicated, may hold values from 0 to 31
- w_qkv: float32 [3, 1024, 1024], P(None, None, 'mp'), may hold values from -0.1875 to 0.1875
- w_out: float32 [1024, 1024], P(None, 'mp'), may hold values from -0.75 to 0.75
- w_ffn: float32 [2, 1024, 4096], P(None, None, 'mp'), may hold values from -0.1875 to 0.1875
- norm_params: float32 [4, 1024], replicated, may hold values from 0.5 to 1.5
- rel_bias: float32 [32, 16], replicated, may hold values from -5 to 5
- momentum_qkv: float32 [3, 1024, 1024], P(None, 'dp', 'mp'), may hold values from -1408 to 1408
- momentum_out: float32 [1024, 1024], P('dp', 'mp'), may hold values from -80 to 80
- momentum_ffn: float32 [2, 1024, 4096], P(None, 'dp', 'mp'), may hold values from -384 to 384
- momentum_norms: float32 [4, 1024], replicated, may hold values from -768 to 768
- momentum_bias: float32 [32, 16], replicated, may hold values from -224 to 224
- average_qkv: float32 [3, 1024, 1024], P(None, 'dp', 'mp'), may hold values from -0.1875 to 0.1875
- average_out: float32 [1024, 1024], P('dp', 'mp'), may hold values from -0.75 to 0.75
- average_ffn: float32 [2, 1024, 4096], P(None, 'dp', 'mp'), may hold values from -0.1875 to 0.1875
- average_norms: float32 [4, 1024], replicated, may hold values from 0.5 to 1.5
- average_bias: float32 [32, 16], replicated, may hold values from -5 to 5
Outputs:
- output: bfloat16 [16384, 1024], P(('dp', 'mp'))
- input_grad: float32 [16384, 1024], P(('dp', 'mp'))
- grad_qkv: float32 [3, 1024, 1024], P(None, 'dp', 'mp')
- next_moment_qkv: float32 [3, 1024, 1024], P(None, 'dp', 'mp')
- next_weight_qkv: float32 [3, 1024, 1024], P(None, 'dp', 'mp')
- next_average_qkv: float32 [3, 1024, 1024], P(None, 'dp', 'mp')
- grad_out: float32 [1024, 1024], P('dp', 'mp')
- next_moment_out: float32 [1024, 1024], P('dp', 'mp')
- next_weight_out: float32 [1024, 1024], P('dp', 'mp')
- next_average_out: float32 [1024, 1024], P('dp', 'mp')
- grad_ffn: float32 [2, 1024, 4096], P(None, 'dp', 'mp')
- next_moment_ffn: float32 [2, 1024, 4096], P(None, 'dp', 'mp')
- next_weight_ffn: float32 [2, 1024, 4096], P(None, 'dp', 'mp')
- next_average_ffn: float32 [2, 1024, 4096], P(None, 'dp', 'mp')
- grad_norms: float32 [4, 1024], replicated
- next_moment_norms: float32 [4, 1024], replicated
- next_weight_norms: float32 [4, 1024], replicated
- next_average_norms: float32 [4, 1024], replicated
- grad_bias: float32 [32, 16], replicated
- next_moment_bias: float32 [32, 16], replicated
- next_weight_bias: float32 [32, 16], replicated
- next_average_bias: float32 [32, 16], replicated
The draws below stay inside these ranges and needn't reach their ends.
Inputs may be any that keep to these rules, and one draw needn't show every extreme that they name: `lengths`: each clip's number of valid frames; in every draw some clip has all 1024 valid.
All inputs are finite; a program needn't handle non-finite values.
Results may differ from the reference program's by a relative error of at most 0.017.
Values may be sent and summed in bfloat16 or wider, within the bound.
No kernel may reach another device: no remote copies, remote signals or barrier semaphores. Data moves between devices by JAX's collectives and lax.ppermute only.
A program may use at most 256 MiB of HBM per device.

```python
import math
import jax
import jax.numpy as jnp
from jax import lax

D = 1024
H = 16
HD = 64
FF = 4096
NB = 32
LEN = 1024
CLIPS = 16
TOKENS = 16384


def draw_lengths(key, part):
    first_key, second_key = jax.random.split(key)
    drawn = jax.random.randint(first_key, (CLIPS,), LEN // 10, LEN + 1, dtype=jnp.int32)
    chosen = jax.random.randint(second_key, (), 0, CLIPS, dtype=jnp.int32)
    return jnp.where(jnp.arange(CLIPS, dtype=jnp.int32) == chosen, LEN, drawn).astype(jnp.int32)


def draw_momentum_qkv(key, part):
    key = jax.random.fold_in(key, 11)
    entry_key = jax.random.fold_in(key, 0)
    magnitude = 1.5 * float(CLIPS * LEN) ** 0.5
    shape_all = (3, D, H * HD)
    entries = jnp.clip(jax.random.normal(entry_key, shape_all, jnp.float32), -6.0, 6.0)
    return (magnitude * entries).astype(jnp.float32)


def place_ends(result, key, smallest, top_value):
    longest = result.shape.index(max(result.shape))
    spots = []
    for shift in (0, 1):
        where = [jax.random.randint(jax.random.fold_in(key, axis), (), 0, length) for axis, length in enumerate(result.shape)]
        where[longest] = (where[longest] + shift) % result.shape[longest]
        spots.append(tuple(where))
    return result.at[spots[0]].set(smallest).at[spots[1]].set(top_value)


def shard_levels(stream_key, dims, shards, low, largest):
    def one(dim, parts):
        steps = jax.random.uniform(jax.random.fold_in(jax.random.fold_in(stream_key, 6), dim), (parts,), jnp.float32, low / len(shards), largest / len(shards))
        return jnp.repeat(jnp.exp(steps), dims[dim] // parts).reshape((-1,) + (1,) * (len(dims) - dim - 1))

    gain = one(*shards[0])
    for cut in shards[1:]:
        gain = gain * one(*cut)
    return gain


def bell_draw(rng, dims, deviation, reach, pieces=(), held_as=jnp.bfloat16):
    result = jax.random.normal(rng, dims, jnp.float32) * deviation
    if len(pieces) > 0:
        result = shard_levels(rng, dims, pieces, -0.22, 0.18) * result
    return jnp.clip(result, min=-reach, max=reach).astype(held_as)


def setup_inputs(seed: int = 0) -> dict:
    key_list = jax.random.split(jax.random.key(seed), 20)
    inputs = bell_draw(key_list[0], (TOKENS, D), 1.0, 6.0, ((0, 32),))
    cotangent = bell_draw(key_list[1], (TOKENS, D), 1.0, 6.0, ((0, 32),))
    lengths = draw_lengths(jax.random.fold_in(key_list[19], 71), 0)
    buckets = place_ends(jax.random.randint(key_list[3], (2 * LEN - 1,), 0, NB), jax.random.fold_in(key_list[3], 1), 0, NB - 1).astype(jnp.int32)
    w_qkv = bell_draw(key_list[4], (3, D, H * HD), D ** -0.5, 0.1875, ((2, 2),), jnp.float32)
    w_out = bell_draw(key_list[5], (D, H * HD), (H * HD * 64 // LEN) ** -0.5, 0.75, ((1, 2),), jnp.float32)
    w_ffn = bell_draw(key_list[6], (2, D, FF), D ** -0.5, 0.1875, ((2, 2),), jnp.float32)
    norm_params = jnp.clip(1.0 + 0.1 * jax.random.normal(key_list[7], (4, D), jnp.float32), 0.5, 1.5)
    rel_bias = bell_draw(key_list[8], (NB, H), 1.0, 5.0, (), jnp.float32)
    momentum_qkv = draw_momentum_qkv(jax.random.fold_in(key_list[19], 71), 0)
    momentum_out = bell_draw(key_list[10], (D, H * HD), (0.1 * (CLIPS * LEN) ** 0.5), 80.0, ((0, 16), (1, 2)), jnp.float32)
    momentum_ffn = bell_draw(key_list[11], (2, D, FF), (0.5 * (CLIPS * LEN) ** 0.5), 384.0, ((1, 16), (2, 2)), jnp.float32)
    momentum_norms = bell_draw(key_list[12], (4, D), ((CLIPS * LEN) ** 0.5), 768.0, (), jnp.float32)
    momentum_bias = bell_draw(key_list[13], (NB, H), (0.3 * (CLIPS * LEN) ** 0.5), 224.0, (), jnp.float32)
    average_qkv = bell_draw(key_list[14], (3, D, H * HD), D ** -0.5, 0.1875, ((1, 16), (2, 2)), jnp.float32)
    average_out = bell_draw(key_list[15], (D, H * HD), (H * HD * 64 // LEN) ** -0.5, 0.75, ((0, 16), (1, 2)), jnp.float32)
    average_ffn = bell_draw(key_list[16], (2, D, FF), D ** -0.5, 0.1875, ((1, 16), (2, 2)), jnp.float32)
    average_norms = jnp.clip(1.0 + 0.1 * jax.random.normal(key_list[17], (4, D), jnp.float32), 0.5, 1.5)
    average_bias = bell_draw(key_list[18], (NB, H), 1.0, 5.0, (), jnp.float32)
    return {"inputs": inputs, "cotangent": cotangent, "lengths": lengths, "buckets": buckets, "w_qkv": w_qkv, "w_out": w_out, "w_ffn": w_ffn, "norm_params": norm_params, "rel_bias": rel_bias, "momentum_qkv": momentum_qkv, "momentum_out": momentum_out, "momentum_ffn": momentum_ffn, "momentum_norms": momentum_norms, "momentum_bias": momentum_bias, "average_qkv": average_qkv, "average_out": average_out, "average_ffn": average_ffn, "average_norms": average_norms, "average_bias": average_bias}


@jax.custom_vjp
def low(v):
    return lax.optimization_barrier(v.astype(jnp.bfloat16)).astype(jnp.float32)

@jax.custom_vjp
def low_back(v):
    return v

def low_keep(v):
    return (low(v), None)

def low_pass(kept, grad):
    return (grad,)

def back_keep(v):
    return (v, None)

def back_low(kept, grad):
    return (low(grad),)
low.defvjp(low_keep, low_pass)
low_back.defvjp(back_keep, back_low)
highest = lax.Precision.HIGHEST
momentum_keep = 0.5
average_keep = 0.5

def normalize(values, gain_row, shift_row):
    row_mean = lax.optimization_barrier(jnp.mean(values, axis=-1, keepdims=True))
    centered = values - row_mean
    spread = lax.optimization_barrier(jnp.mean(centered * centered, axis=-1, keepdims=True))
    return centered * lax.rsqrt(spread + 1e-05) * gain_row + shift_row

def clip_layer(clip_inputs, w_qkv, w_out, w_ffn, norm_params, rel_bias, clip_size, buckets):
    normed_one = low(normalize(clip_inputs, norm_params[0], norm_params[1]))
    weights_qkv = low(w_qkv)
    queries = low_back(low(jnp.dot(normed_one, weights_qkv[0], precision=highest))).reshape(LEN, H, HD)
    keys_all = low_back(low(jnp.dot(normed_one, weights_qkv[1], precision=highest))).reshape(LEN, H, HD)
    values_all = low_back(low(jnp.dot(normed_one, weights_qkv[2], precision=highest))).reshape(LEN, H, HD)
    bias_table = rel_bias[buckets].T
    block_rows = LEN // 2
    key_valid = jnp.arange(LEN, dtype=jnp.int32) < clip_size

    @jax.checkpoint
    def attend_block(block_index):
        first_row = block_index * block_rows
        query_block = lax.dynamic_slice_in_dim(queries, first_row, block_rows, 0)
        offsets = jnp.arange(LEN, dtype=jnp.int32)[None, :] - (first_row + jnp.arange(block_rows, dtype=jnp.int32))[:, None] + (LEN - 1)
        scores = jnp.einsum('qhd,khd->hqk', query_block, keys_all, precision=highest) * 0.125 + bias_table[:, offsets]
        scores = jnp.where(key_valid[None, None, :], low_back(scores), -1000000000.0)
        soft_weights = low(jax.nn.softmax(scores, axis=-1))
        return low_back(low(jnp.einsum('hqk,khd->qhd', soft_weights, values_all, precision=highest)))
    context = lax.map(attend_block, jnp.arange(2, dtype=jnp.int32)).reshape(LEN, H * HD)
    branch = low_back(jnp.dot(context, low(w_out).T, precision=highest))
    middle = clip_inputs + branch
    normed_two = low(normalize(middle, norm_params[2], norm_params[3]))
    weights_ffn = low(w_ffn)
    hidden_pre = low_back(jnp.dot(normed_two, weights_ffn[0], precision=highest))
    hidden = low(jax.nn.gelu(hidden_pre, approximate=False))
    return middle + jnp.dot(hidden, weights_ffn[1].T, precision=highest)

def apply_update(weight, momentum, average, gradient, step_rate):
    next_moment = momentum_keep * momentum + gradient
    next_weight = weight - step_rate * (gradient + momentum_keep * next_moment)
    next_average = average_keep * average + (1.0 - average_keep) * next_weight
    return (next_moment, next_weight, next_average)

def reference(inputs, cotangent, lengths, buckets, w_qkv, w_out, w_ffn, norm_params, rel_bias, momentum_qkv, momentum_out, momentum_ffn, momentum_norms, momentum_bias, average_qkv, average_out, average_ffn, average_norms, average_bias):
    clip_inputs_all = inputs.reshape(CLIPS, LEN, D)
    clip_cot_all = cotangent.reshape(CLIPS, LEN, D)

    def per_clip(running, packed):
        clip_inputs, clip_cot, clip_size = packed

        def layer_of(layer_inputs, weight_one, weight_two, weight_three, weight_four, weight_five):
            return clip_layer(layer_inputs, weight_one, weight_two, weight_three, weight_four, weight_five, clip_size, buckets)
        clip_out, pullback = jax.vjp(layer_of, clip_inputs.astype(jnp.float32), w_qkv, w_out, w_ffn, norm_params, rel_bias)
        grads = pullback(clip_cot.astype(jnp.float32))
        running = tuple((summed + clip_part for summed, clip_part in zip(running, grads[1:])))
        return (running, (clip_out.astype(jnp.bfloat16), grads[0]))
    zeros_start = (jnp.zeros_like(w_qkv), jnp.zeros_like(w_out), jnp.zeros_like(w_ffn), jnp.zeros_like(norm_params), jnp.zeros_like(rel_bias))
    summed_all, (outputs, input_grads) = lax.scan(per_clip, zeros_start, (clip_inputs_all, clip_cot_all, lengths))
    scale_factor = 1.0 / math.sqrt(float(CLIPS * LEN))
    moment_qkv, weight_qkv, mean_qkv = apply_update(w_qkv, momentum_qkv, average_qkv, summed_all[0], 0.3 * scale_factor)
    moment_out, weight_out, mean_out = apply_update(w_out, momentum_out, average_out, summed_all[1], 0.1 * scale_factor)
    moment_ffn, weight_ffn, mean_ffn = apply_update(w_ffn, momentum_ffn, average_ffn, summed_all[2], 0.05 * scale_factor)
    moment_norms, weight_norms, mean_norms = apply_update(norm_params, momentum_norms, average_norms, summed_all[3], 0.05 * scale_factor)
    moment_bias, weight_bias, mean_bias = apply_update(rel_bias, momentum_bias, average_bias, summed_all[4], 0.05 * scale_factor)
    return (outputs.reshape(TOKENS, D), input_grads.reshape(TOKENS, D), summed_all[0], moment_qkv, weight_qkv, mean_qkv, summed_all[1], moment_out, weight_out, mean_out, summed_all[2], moment_ffn, weight_ffn, mean_ffn, summed_all[3], moment_norms, weight_norms, mean_norms, summed_all[4], moment_bias, weight_bias, mean_bias)
```

```python
import math

import jax
import jax.numpy as jnp
from jax import lax
from jax.experimental import pallas as pl
from jax.experimental.pallas import tpu as pltpu
from jax.sharding import PartitionSpec as P

HD = 64
PAIR = 2 * HD
QB = 128
f32 = jnp.float32
bf16 = jnp.bfloat16
ROWS_BY_ROWS = (((1,), (1,)), ((), ()))
COLS_BY_COLS = (((0,), (0,)), ((), ()))
VMEM_LIMIT = 56 * 2**20

highest = lax.Precision.HIGHEST
momentum_keep = 0.5
average_keep = 0.5


def skew_kernel(tab_ref, rev_ref, fwd_ref, bwd_ref):
    width = tab_ref.shape[2]
    for src, dst in ((tab_ref, fwd_ref), (rev_ref, bwd_ref)):
        rows = jnp.broadcast_to(src[0], (QB, width))
        rolled = pltpu.roll(rows, width - (QB - 1), 1, stride=1, stride_axis=0)
        dst[0] = rolled[:, : width - QB]

def skew_tables(table):
    heads, width = table.shape
    pad = jnp.pad(table, ((0,0),(0,1)))[:, None, :]
    rev = jnp.pad(table[:, ::-1], ((0,0),(0,1)))[:, None, :]
    width += 1
    spec = pl.BlockSpec((1,1,width), lambda h:(h,0,0))
    ospec = pl.BlockSpec((1,QB,width-QB), lambda h:(h,0,0))
    o = jax.ShapeDtypeStruct((heads,QB,width-QB), f32)
    return pl.pallas_call(skew_kernel, grid=(heads,), in_specs=[spec,spec], out_specs=[ospec,ospec], out_shape=[o,o], name="skew")(pad, rev)

def split3(x):
    a = x.astype(bf16).astype(f32)
    r = x - a
    b = r.astype(bf16).astype(f32)
    return a, b, r - b

def key_side(k, valid_row, own, lane, first):
    extra = jnp.where(lane == first, valid_row, jnp.where((lane > first) & (lane < first + 4), 1.0, 0.0))
    return jnp.where(own, k, extra).astype(bf16)

def fwd_kernel(len_ref, q_ref, k_ref, v_ref, t_ref, o_ref, lse_ref, kx_ref, vx_ref):
    L = k_ref.shape[0]; R = q_ref.shape[0]
    lane = lax.broadcasted_iota(jnp.int32, (L, PAIR), 1)
    row = lax.broadcasted_iota(jnp.int32, (L, PAIR), 0)
    mask = jnp.where(row < len_ref[0], 0.0, -1e9)
    k = k_ref[...].astype(f32); v = v_ref[...].astype(f32)
    for h in range(2):
        own = (lane >= HD) if h else (lane < HD)
        kx_ref[h] = key_side(k, mask, own, lane, 0 if h else HD)
        vx_ref[h] = jnp.where(own, v, 1.0).astype(bf16)
    lq = lax.broadcasted_iota(jnp.int32, (QB, PAIR), 1)
    def body(a, _):
        rows = pl.ds(pl.multiple_of(a*QB, QB), QB)
        q = q_ref[rows, :].astype(f32) * 0.125
        start = pl.multiple_of(L - QB - a*QB, QB)
        outs=[]; ls=[]
        for h in range(2):
            own = (lq >= HD) if h else (lq < HD)
            first = 0 if h else HD
            qx = jnp.where(own, q, jnp.where(lq == first, 1.0, 0.0)).astype(bf16)
            s = lax.dot_general(qx, kx_ref[h], ROWS_BY_ROWS, preferred_element_type=f32)
            s = s + t_ref[h, :, pl.ds(start, L)]
            m = jnp.max(s, axis=1, keepdims=True)
            e = jnp.exp(s - m).astype(bf16)
            pv = jnp.dot(e, vx_ref[h], preferred_element_type=f32)
            tot = pv[:, :1] if h else pv[:, HD:HD+1]
            outs.append(pv / tot)
            ls.append(m + jnp.log(tot))
        o_ref[rows, :] = jnp.where(lq < HD, outs[0], outs[1]).astype(bf16)
        lse_ref[rows, :] = jnp.where(lq < HD, ls[0], ls[1])
        return 0
    lax.fori_loop(0, R//QB, body, 0)

def attn_fwd(proj, lengths, skew):
    _, L, W = proj.shape
    pairs = W // (PAIR)
    def sp(i): return pl.BlockSpec((None, L, PAIR), lambda p, i=i: (i, 0, p))
    return pl.pallas_call(fwd_kernel, grid=(pairs,),
        in_specs=[pl.BlockSpec(memory_space=pltpu.SMEM), sp(0), sp(1), sp(2),
                  pl.BlockSpec((2, QB, skew.shape[2]), lambda p:(p,0,0))],
        out_specs=[pl.BlockSpec((L, PAIR), lambda p:(0,p)), pl.BlockSpec((L, PAIR), lambda p:(0,p))],
        out_shape=[jax.ShapeDtypeStruct((L,W), bf16), jax.ShapeDtypeStruct((L,W), f32)],
        scratch_shapes=[pltpu.VMEM((2,L,PAIR), bf16), pltpu.VMEM((2,L,PAIR), bf16)],
        compiler_params=pltpu.CompilerParams(vmem_limit_bytes=VMEM_LIMIT), name="attn_fwd",
    )(lengths, proj, proj, proj, skew)

def bwd_kernel(len_ref, q_ref, k_ref, v_ref, do_ref, o_ref, lse_ref, t_ref,
               dq_ref, dk_ref, dv_ref, diag_ref, qx_ref, gx_ref, acc_ref, dqa_ref):
    L = k_ref.shape[0]
    W2 = PAIR
    lane = lax.broadcasted_iota(jnp.int32, (L, W2), 1)
    q = q_ref[...].astype(f32) * 0.125
    do = do_ref[...].astype(f32)
    prod = do * o_ref[...].astype(f32)
    lse = lse_ref[...]
    for h in range(2):
        own = (lane >= HD) if h else (lane < HD)
        first = 0 if h else HD
        delta = jnp.sum(jnp.where(own, prod, 0.0), axis=1, keepdims=True)
        l = lse[:, HD:HD+1] if h else lse[:, :1]
        la, lb, lc = split3(-l)
        qx_ref[h] = jnp.where(own, q, jnp.where(lane == first, 1.0, jnp.where(lane == first+1, la, jnp.where(lane == first+2, lb, jnp.where(lane == first+3, lc, 0.0))))).astype(bf16)
        da, db, dc = split3(-delta)
        gx_ref[h] = jnp.where(own, do, jnp.where(lane == first+1, da, jnp.where(lane == first+2, db, jnp.where(lane == first+3, dc, 0.0)))).astype(bf16)
    acc_ref[...] = jnp.zeros_like(acc_ref)
    lk = lax.broadcasted_iota(jnp.int32, (QB, W2), 1)
    rk = lax.broadcasted_iota(jnp.int32, (QB, W2), 0)
    def body(c, _):
        rows = pl.ds(pl.multiple_of(c*QB, QB), QB)
        k = k_ref[rows, :].astype(f32); v = v_ref[rows, :].astype(f32)
        mask = jnp.where(rk + c*QB < len_ref[0], 0.0, -1e9)
        start = pl.multiple_of(L - QB - c*QB, QB)
        dks=[]; dvs=[]; dqs=[]
        for h in range(2):
            own = (lk >= HD) if h else (lk < HD)
            first = 0 if h else HD
            kx = key_side(k, mask, own, lk, first)
            vx = jnp.where(own, v, jnp.where((lk > first) & (lk < first+4), 1.0, 0.0)).astype(bf16)
            s = lax.dot_general(kx, qx_ref[h], ROWS_BY_ROWS, preferred_element_type=f32)
            p = jnp.exp(s + t_ref[h, :, pl.ds(start, L)])
            dp = lax.dot_general(vx, gx_ref[h], ROWS_BY_ROWS, preferred_element_type=f32)
            ds = p * dp
            acc_ref[h, :, pl.ds(start, L)] += ds
            pb = p.astype(bf16); dsb = ds.astype(bf16)
            dvs.append(jnp.dot(pb, gx_ref[h], preferred_element_type=f32))
            dks.append(jnp.dot(dsb, qx_ref[h], preferred_element_type=f32))
            dqs.append(lax.dot_general(dsb, kx, COLS_BY_COLS, preferred_element_type=f32))
        dk_ref[rows, :] = jnp.where(lk < HD, dks[0], dks[1]).astype(bf16)
        dv_ref[rows, :] = jnp.where(lk < HD, dvs[0], dvs[1]).astype(bf16)
        dq = jnp.where(lane < HD, dqs[0], dqs[1])
        @pl.when(c == 0)
        def _(): dqa_ref[...] = dq
        @pl.when(c > 0)
        def _(): dqa_ref[...] += dq
        return 0
    lax.fori_loop(0, L//QB, body, 0)
    dq_ref[...] = (dqa_ref[...] * 0.125).astype(bf16)
    for h in range(2):
        diag_ref[h] = diagonal_sums(jnp.concatenate([acc_ref[h], jnp.zeros((QB, QB), f32)], axis=1))

def diagonal_sums(a):
    width = a.shape[1]
    total = pltpu.roll(a[:8], QB - 1, 1)
    for g in range(1, QB // 8):
        total = total + pltpu.roll(a[8*g : 8*g + 8], QB - 1 - 8*g, 1)
    sub = lax.broadcasted_iota(jnp.int32, total.shape, 0)
    for bit in (1, 2, 4):
        total = jnp.where((sub & bit) != 0, pltpu.roll(total, width - bit, 1), total)
    return jnp.sum(total, axis=0, keepdims=True)

def attn_bwd(proj, do, o, lse, lengths, skew_t):
    _, L, W = proj.shape
    pairs = W // (PAIR)
    def sp(i): return pl.BlockSpec((None, L, PAIR), lambda p, i=i: (i, 0, p))
    cs = pl.BlockSpec((L, PAIR), lambda p:(0,p))
    wid = skew_t.shape[2]
    return pl.pallas_call(bwd_kernel, grid=(pairs,),
        in_specs=[pl.BlockSpec(memory_space=pltpu.SMEM), sp(0), sp(1), sp(2), cs, cs, cs,
                  pl.BlockSpec((2, QB, wid), lambda p:(p,0,0))],
        out_specs=[cs, cs, cs, pl.BlockSpec((2, 1, wid+QB), lambda p:(p,0,0))],
        out_shape=[jax.ShapeDtypeStruct((L,W), bf16)]*3 + [jax.ShapeDtypeStruct((W//HD, 1, wid+QB), f32)],
        scratch_shapes=[pltpu.VMEM((2,L,PAIR), bf16), pltpu.VMEM((2,L,PAIR), bf16), pltpu.VMEM((2,QB,wid), f32), pltpu.VMEM((L,PAIR), f32)],
        compiler_params=pltpu.CompilerParams(vmem_limit_bytes=VMEM_LIMIT), name="attn_bwd",
    )(lengths, proj, proj, proj, do, o, lse, skew_t)

def unit(values):
    row_mean = jnp.mean(values, axis=-1, keepdims=True)
    centered = values - row_mean
    spread = jnp.mean(centered * centered, axis=-1, keepdims=True)
    inverse = lax.rsqrt(spread + 1e-05)
    return (centered * inverse, inverse)


def norm_back(grad_normed, unit_rows, inverse, gain_row):
    grad_unit = grad_normed * gain_row
    first_mean = jnp.mean(grad_unit, axis=-1, keepdims=True)
    second_mean = jnp.mean(grad_unit * unit_rows, axis=-1, keepdims=True)
    return inverse * (grad_unit - first_mean - unit_rows * second_mean)


def apply_update(weight, momentum, average, gradient, step_rate):
    next_moment = momentum_keep * momentum + gradient
    next_weight = weight - step_rate * (gradient + momentum_keep * next_moment)
    next_average = average_keep * average + (1.0 - average_keep) * next_weight
    return (next_moment, next_weight, next_average)


def swap(values, axis, bit):
    size = lax.axis_size(axis)
    return lax.ppermute(values, axis, [(i, i ^ bit) for i in range(size)])


def gather_rows(rows):
    if lax.axis_size("mp") != 2:
        return lax.all_gather(rows, "mp", axis=0, tiled=True)
    other = swap(rows, "mp", 1)
    first = lax.axis_index("mp") == 0
    return jnp.concatenate([jnp.where(first, rows, other), jnp.where(first, other, rows)], axis=0)


def sum_rows(rows):
    if lax.axis_size("mp") != 2:
        return lax.psum(rows, "mp").astype(f32)
    return rows.astype(f32) + swap(rows, "mp", 1).astype(f32)


def scatter_rows(rows):
    if lax.axis_size("mp") != 2:
        return lax.psum_scatter(rows, "mp", scatter_dimension=0, tiled=True).astype(f32)
    half = rows.shape[0] // 2
    mine = lax.axis_index("mp") * half
    sent = lax.dynamic_slice_in_dim(rows, half - mine, half, 0)
    kept = lax.dynamic_slice_in_dim(rows, mine, half, 0)
    return kept.astype(f32) + swap(sent, "mp", 1).astype(f32)


def halves_first(columns):
    rows, width = columns.shape
    bits = lax.axis_size("dp").bit_length() - 1
    split = columns.reshape((rows,) + (2,) * bits + (width >> bits,))
    order = (0,) + tuple(range(bits, 0, -1)) + (bits + 1,)
    return split.transpose(order).reshape(rows, 2, width >> 1)


def weight_share(ordered, right):
    place = lax.axis_index("dp")
    bits = lax.axis_size("dp").bit_length() - 1
    low = place & 1

    def product(which):
        piece = lax.dynamic_index_in_dim(ordered, which, 1, keepdims=False)
        return lax.dot_general(piece, right, COLS_BY_COLS, preferred_element_type=f32)

    got = swap(product(1 - low).astype(bf16), "dp", 1)
    total = product(low) + got.astype(f32)
    for bit in range(1, bits):
        total = total.astype(bf16)
        half = total.shape[0] // 2
        mine = (lax.shift_right_logical(place, bit) & 1) * half
        got = swap(lax.dynamic_slice_in_dim(total, half - mine, half, 0), "dp", 1 << bit)
        total = lax.dynamic_slice_in_dim(total, mine, half, 0).astype(f32) + got.astype(f32)
    return total


def sum_all(values):
    for axis in ("dp", "mp"):
        bit = 1
        while bit < lax.axis_size(axis):
            values = values + swap(values, axis, bit)
            bit *= 2
    return values


def gelu_parts(values):
    half_erf = 0.5 * lax.erf(values * 0.7071067811865476)
    gate = 0.5 + half_erf
    slope = gate + values * (0.3989422804014327 * jnp.exp(-0.5 * values * values))
    return (values * gate, slope)


def per_device(
    inputs,
    cotangent,
    lengths,
    buckets,
    w_qkv,
    w_out,
    w_ffn,
    norm_params,
    rel_bias,
    momentum_qkv,
    momentum_out,
    momentum_ffn,
    momentum_norms,
    momentum_bias,
    average_qkv,
    average_out,
    average_ffn,
    average_norms,
    average_bias,
):
    model_size = lax.axis_size("mp")
    data_size = lax.axis_size("dp")
    rows_local = inputs.shape[0]
    seq_len = rows_local * model_size
    width_local = w_qkv.shape[2]
    heads_local = width_local // HD
    head_first = lax.axis_index("mp") * heads_local
    own_first = lax.axis_index("mp") * rows_local
    data_index = lax.axis_index("dp")
    share_rows = momentum_out.shape[0]

    inputs_all = gather_rows(inputs).astype(f32)
    cot_all = gather_rows(cotangent)
    weights_qkv = w_qkv.astype(bf16)
    weights_out = w_out.astype(bf16)
    weights_ffn = w_ffn.astype(bf16)

    bias_local = lax.dynamic_slice_in_dim(rel_bias, head_first, heads_local, 1)
    bucket_hits = (buckets[:, None] == jnp.arange(rel_bias.shape[0], dtype=jnp.int32)[None, :]).astype(f32)
    bias_table = jnp.dot(bucket_hits, bias_local, precision=highest).T
    skew, skew_back = skew_tables(bias_table)

    unit_one, inverse_one = unit(inputs_all)
    normed_one = (unit_one * norm_params[0] + norm_params[1]).astype(bf16)
    projected = jnp.einsum("sd,tdc->tsc", normed_one, weights_qkv, preferred_element_type=f32).astype(bf16)
    context, log_totals = attn_fwd(projected, lengths, skew)
    branch = lax.dot_general(context, weights_out, ROWS_BY_ROWS, preferred_element_type=f32).astype(bf16)
    middle = inputs_all + sum_rows(branch)
    unit_two, inverse_two = unit(middle)
    normed_two = (unit_two * norm_params[2] + norm_params[3]).astype(bf16)

    hidden_pre = jnp.dot(normed_two, weights_ffn[0], preferred_element_type=f32)
    hidden, slope = gelu_parts(hidden_pre)
    hidden = hidden.astype(bf16)
    hidden_grad = jnp.dot(cot_all, weights_ffn[1], preferred_element_type=f32)
    pre_grad = (hidden_grad * slope).astype(bf16)
    normed_two_part = lax.dot_general(pre_grad, weights_ffn[0], ROWS_BY_ROWS, preferred_element_type=f32).astype(bf16)
    normed_two_grad = sum_rows(normed_two_part)
    out_part = lax.dot_general(hidden, weights_ffn[1], ROWS_BY_ROWS, preferred_element_type=f32).astype(bf16)
    middle_own = lax.dynamic_slice_in_dim(middle, own_first, rows_local, 0)
    output = (middle_own + scatter_rows(out_part)).astype(bf16)

    up_share = weight_share(halves_first(normed_two), pre_grad)
    down_share = weight_share(halves_first(cot_all), hidden)

    middle_grad = cot_all.astype(f32) + norm_back(normed_two_grad, unit_two, inverse_two, norm_params[2])
    gain_two_grad = jnp.sum(normed_two_grad * unit_two, axis=0) / model_size
    shift_two_grad = jnp.sum(normed_two_grad, axis=0) / model_size
    branch_grad = middle_grad.astype(bf16)
    context_grad = jnp.dot(branch_grad, weights_out, preferred_element_type=f32).astype(bf16)
    out_share = weight_share(halves_first(branch_grad), context)

    query_grad, key_grad, value_grad, diagonals = attn_bwd(projected, context_grad, context, log_totals, lengths, skew_back)
    offset_grad = diagonals[:, 0, : 2 * seq_len - 1]
    ordered_one = halves_first(normed_one)
    grad_parts = [query_grad, key_grad, value_grad]
    normed_one_part = sum(
        lax.dot_general(g, weights_qkv[t], ROWS_BY_ROWS, preferred_element_type=f32) for t, g in enumerate(grad_parts)
    )
    gain_one_grad = jnp.sum(normed_one_part * unit_one, axis=0)
    shift_one_grad = jnp.sum(normed_one_part, axis=0)
    normed_one_grad = scatter_rows(normed_one_part.astype(bf16))
    qkv_share = weight_share(ordered_one, jnp.concatenate(grad_parts, axis=1))
    qkv_share = qkv_share.reshape(share_rows, 3, width_local).transpose(1, 0, 2)

    unit_own, inverse_own = unit(inputs.astype(f32))
    input_grad = lax.dynamic_slice_in_dim(middle_grad, own_first, rows_local, 0) + norm_back(
        normed_one_grad, unit_own, inverse_own, norm_params[0]
    )

    bias_grad_local = jnp.einsum("rb,hr->bh", bucket_hits[::-1], offset_grad, precision=highest)
    bias_grad_full = lax.dynamic_update_slice_in_dim(jnp.zeros(rel_bias.shape, f32), bias_grad_local, head_first, 1)
    norm_grad_local = jnp.stack([gain_one_grad, shift_one_grad, gain_two_grad, shift_two_grad])
    small = jnp.concatenate([norm_grad_local.reshape(-1, 128), bias_grad_full.reshape(-1, 128)], axis=0)
    small = sum_all(small)
    norm_rows = norm_grad_local.size // 128
    norm_grad = small[:norm_rows].reshape(norm_grad_local.shape)
    bias_grad = small[norm_rows:].reshape(rel_bias.shape)

    ffn_share = jnp.stack([up_share, down_share])
    scale_factor = 1.0 / math.sqrt(float(seq_len * data_size))
    weight_qkv_share = lax.dynamic_slice_in_dim(w_qkv, data_index * share_rows, share_rows, 1)
    weight_out_share = lax.dynamic_slice_in_dim(w_out, data_index * share_rows, share_rows, 0)
    weight_ffn_share = lax.dynamic_slice_in_dim(w_ffn, data_index * share_rows, share_rows, 1)
    moment_qkv, weight_qkv, mean_qkv = apply_update(
        weight_qkv_share, momentum_qkv, average_qkv, qkv_share, 0.3 * scale_factor
    )
    moment_out, weight_out, mean_out = apply_update(
        weight_out_share, momentum_out, average_out, out_share, 0.1 * scale_factor
    )
    moment_ffn, weight_ffn, mean_ffn = apply_update(
        weight_ffn_share, momentum_ffn, average_ffn, ffn_share, 0.05 * scale_factor
    )
    moment_norms, weight_norms, mean_norms = apply_update(
        norm_params, momentum_norms, average_norms, norm_grad, 0.05 * scale_factor
    )
    moment_bias, weight_bias, mean_bias = apply_update(
        rel_bias, momentum_bias, average_bias, bias_grad, 0.05 * scale_factor
    )
    return (
        output,
        input_grad,
        qkv_share,
        moment_qkv,
        weight_qkv,
        mean_qkv,
        out_share,
        moment_out,
        weight_out,
        mean_out,
        ffn_share,
        moment_ffn,
        weight_ffn,
        mean_ffn,
        norm_grad,
        moment_norms,
        weight_norms,
        mean_norms,
        bias_grad,
        moment_bias,
        weight_bias,
        mean_bias,
    )


def solution(mesh):
    return jax.shard_map(
        per_device,
        mesh=mesh,
        in_specs=(
            P(("dp", "mp"), None),
            P(("dp", "mp"), None),
            P("dp"),
            P(),
            P(None, None, "mp"),
            P(None, "mp"),
            P(None, None, "mp"),
            P(),
            P(),
            P(None, "dp", "mp"),
            P("dp", "mp"),
            P(None, "dp", "mp"),
            P(),
            P(),
            P(None, "dp", "mp"),
            P("dp", "mp"),
            P(None, "dp", "mp"),
            P(),
            P(),
        ),
        out_specs=(
            P(("dp", "mp"), None),
            P(("dp", "mp"), None),
            P(None, "dp", "mp"),
            P(None, "dp", "mp"),
            P(None, "dp", "mp"),
            P(None, "dp", "mp"),
            P("dp", "mp"),
            P("dp", "mp"),
            P("dp", "mp"),
            P("dp", "mp"),
            P(None, "dp", "mp"),
            P(None, "dp", "mp"),
            P(None, "dp", "mp"),
            P(None, "dp", "mp"),
            P(),
            P(),
            P(),
            P(),
            P(),
            P(),
            P(),
            P(),
        ),
        check_vma=False,
    )
```

```python
import math

import jax
import jax.numpy as jnp
from jax import lax
from jax.experimental import pallas as pl
from jax.experimental.pallas import tpu as pltpu
from jax.sharding import PartitionSpec as P

HD = 64
PAIR = 2 * HD
QB = 128
QUERY_BLOCK = 512
KEY_BLOCK = 512
f32 = jnp.float32
bf16 = jnp.bfloat16
ROWS_BY_ROWS = (((1,), (1,)), ((), ()))
COLS_BY_COLS = (((0,), (0,)), ((), ()))
VMEM_LIMIT = 56 * 2**20

highest = lax.Precision.HIGHEST
momentum_keep = 0.5
average_keep = 0.5
SHARE = 1.1e6


def cost(microseconds):
    return pl.CostEstimate(flops=0, bytes_accessed=int(SHARE * microseconds), transcendentals=0)


def skew_kernel(forward_ref, reverse_ref, forward_out, reverse_out):
    width = forward_ref.shape[2]
    for source, result in ((forward_ref, forward_out), (reverse_ref, reverse_out)):
        rows = jnp.broadcast_to(source[0], (QB, width))
        result[0] = pltpu.roll(rows, width - (QB - 1), 1, stride=1, stride_axis=0)[:, : width - QB]


def skew_tables(table):
    heads, width = table.shape
    forward = jnp.pad(table, ((0, 0), (0, 1)))[:, None, :]
    reverse = jnp.pad(table[:, ::-1], ((0, 0), (0, 1)))[:, None, :]
    width += 1
    row = pl.BlockSpec((1, 1, width), lambda h: (h, 0, 0))
    skewed = pl.BlockSpec((1, QB, width - QB), lambda h: (h, 0, 0))
    shape = jax.ShapeDtypeStruct((heads, QB, width - QB), f32)
    return pl.pallas_call(
        skew_kernel,
        grid=(heads,),
        in_specs=[row, row],
        out_specs=[skewed, skewed],
        out_shape=[shape, shape],
        cost_estimate=cost(8),
        name="skew",
    )(forward, reverse)


def three_parts(values):
    first = values.astype(bf16).astype(f32)
    rest = values - first
    second = rest.astype(bf16).astype(f32)
    return (first, second, rest - second)


def own_lanes(lane, head):
    return (lane >= HD) if head else (lane < HD)


def key_side(keys, mask, lane, head):
    first = 0 if head else HD
    extra = jnp.where(lane == first, mask, jnp.where((lane > first) & (lane < first + 4), 1.0, 0.0))
    return jnp.where(own_lanes(lane, head), keys, extra).astype(bf16)


def forward_kernel(
    first_row,
    length_ref,
    q_ref,
    k_ref,
    v_ref,
    skew_ref,
    weight_ref,
    context_ref,
    total_ref,
    branch_ref,
    key_ref,
    value_ref,
    raised_ref,
    gathered_ref,
):
    seq_len = k_ref.shape[0]
    rows_here = q_ref.shape[0]
    lane = lax.broadcasted_iota(jnp.int32, (seq_len, PAIR), 1)
    place = lax.broadcasted_iota(jnp.int32, (seq_len, PAIR), 0)
    mask = jnp.where(place < length_ref[0], 0.0, -1e9)
    keys = k_ref[...].astype(f32)
    values = v_ref[...].astype(f32)
    for head in range(2):
        key_ref[head] = key_side(keys, mask, lane, head)
        value_ref[head] = jnp.where(own_lanes(lane, head), values, 1.0).astype(bf16)
    here = min(QUERY_BLOCK, rows_here)
    lane = lax.broadcasted_iota(jnp.int32, (here, PAIR), 1)

    def block(index, carry):
        rows = pl.ds(pl.multiple_of(index * here, here), here)
        queries = q_ref[rows, :].astype(f32) * 0.125
        context = []
        totals = []
        for head in range(2):
            own = own_lanes(lane, head)
            first = 0 if head else HD
            query = jnp.where(own, queries, jnp.where(lane == first, 1.0, 0.0)).astype(bf16)
            scores = lax.dot_general(query, key_ref[head], ROWS_BY_ROWS, preferred_element_type=f32)
            tops = []
            for piece in range(0, here, QB):
                start = pl.multiple_of(seq_len - QB - first_row - index * here - piece, QB)
                moved = scores[piece : piece + QB] + skew_ref[head, :, pl.ds(start, seq_len)]
                top = jnp.max(moved, axis=1, keepdims=True)
                raised_ref[head, piece : piece + QB, :] = jnp.exp(moved - top).astype(bf16)
                tops.append(top)
            weighted = jnp.dot(raised_ref[head], value_ref[head], preferred_element_type=f32)
            context.append(weighted / weighted[:, first : first + 1])
            totals.append(jnp.concatenate(tops, axis=0) + jnp.log(jnp.where(own, 1.0, weighted)))
        context_ref[rows, :] = jnp.where(lane < HD, context[0], context[1]).astype(bf16)
        total_ref[rows, :] = jnp.where(lane < HD, totals[1], totals[0])
        return carry

    lax.fori_loop(0, rows_here // here, block, 0, unroll=True)
    step = pl.program_id(0)
    gathered_ref[step] = context_ref[...]

    @pl.when(step == pl.num_programs(0) - 1)
    def _():
        gathered = jnp.concatenate([gathered_ref[p] for p in range(gathered_ref.shape[0])], axis=1)
        branch_ref[...] = lax.dot_general(gathered, weight_ref[...], ROWS_BY_ROWS, preferred_element_type=f32).astype(bf16)


def attend(projected, lengths, skew, weights_out, chunk, chunks):
    _, seq_len, width = projected.shape
    features = weights_out.shape[0]
    rows_here = seq_len // chunks
    whole = [pl.BlockSpec((None, seq_len, PAIR), lambda p, t=t: (t, 0, p)) for t in (1, 2)]
    part = pl.BlockSpec((rows_here, PAIR), lambda p: (0, p))
    return pl.pallas_call(
        lambda *refs: forward_kernel(chunk * rows_here, *refs),
        grid=(width // PAIR,),
        in_specs=[
            pl.BlockSpec(memory_space=pltpu.SMEM),
            pl.BlockSpec((None, rows_here, PAIR), lambda p: (0, chunk, p)),
            *whole,
            pl.BlockSpec((2,) + skew.shape[1:], lambda p: (p, 0, 0)),
            pl.BlockSpec(weights_out.shape, lambda p: (0, 0)),
        ],
        out_specs=[part, part, pl.BlockSpec((rows_here, features), lambda p: (0, 0))],
        out_shape=[
            jax.ShapeDtypeStruct((rows_here, width), bf16),
            jax.ShapeDtypeStruct((rows_here, width), f32),
            jax.ShapeDtypeStruct((rows_here, features), bf16),
        ],
        scratch_shapes=[
            pltpu.VMEM((2, seq_len, PAIR), bf16),
            pltpu.VMEM((2, seq_len, PAIR), bf16),
            pltpu.VMEM((2, min(QUERY_BLOCK, rows_here), seq_len), bf16),
            pltpu.VMEM((width // PAIR, rows_here, PAIR), bf16),
        ],
        compiler_params=pltpu.CompilerParams(vmem_limit_bytes=VMEM_LIMIT),
        cost_estimate=cost(13),
        name="attend",
    )(lengths, projected, projected, projected, skew, weights_out)


def diagonal_sums(skewed):
    width = skewed.shape[1]
    total = pltpu.roll(skewed[:8], QB - 1, 1)
    for group in range(1, QB // 8):
        total = total + pltpu.roll(skewed[8 * group : 8 * group + 8], QB - 1 - 8 * group, 1)
    row = lax.broadcasted_iota(jnp.int32, total.shape, 0)
    for bit in (1, 2, 4):
        total = jnp.where((row & bit) != 0, pltpu.roll(total, width - bit, 1), total)
    return jnp.sum(total, axis=0, keepdims=True)


def backward_kernel(first_row, last, *refs):
    (length_ref, q_ref, k_ref, v_ref, grad_ref, context_ref, total_ref, skew_ref) = refs[:8]
    running = last and first_row > 0
    if running:
        dq_before, dk_before, dv_before = refs[8:11]
    if last:
        grads_ref, diagonal_ref = refs[-8:-6]
        dq_ref = grads_ref.at[0, pl.ds(first_row, q_ref.shape[0]), :]
        dk_ref, dv_ref = grads_ref.at[1], grads_ref.at[2]
    else:
        dq_ref, dk_ref, dv_ref, diagonal_ref = refs[-10:-6]
    (query_ref, back_ref, skewed_ref, dq_sum, soft_ref, slope_ref) = refs[-6:]
    if running:
        grads_ref[0, :first_row, :] = dq_before[...]
    seq_len = k_ref.shape[0]
    rows_here = q_ref.shape[0]
    lane = lax.broadcasted_iota(jnp.int32, (rows_here, PAIR), 1)
    queries = q_ref[...].astype(f32) * 0.125
    back = grad_ref[...].astype(f32)
    dots = back * context_ref[...].astype(f32)
    first_lane = lax.broadcasted_iota(jnp.int32, (PAIR, PAIR), 0) // HD
    cross = jnp.where(first_lane != lax.broadcasted_iota(jnp.int32, (PAIR, PAIR), 1) // HD, 1.0, 0.0).astype(bf16)
    row_dot = sum(jnp.dot(part.astype(bf16), cross, preferred_element_type=f32) for part in three_parts(dots)[:2])
    tops = three_parts(-total_ref[...])
    drops = three_parts(-row_dot)
    for head in range(2):
        own = own_lanes(lane, head)
        first = 0 if head else HD
        query = jnp.where(lane == first, 1.0, 0.0)
        graded = jnp.zeros_like(query)
        for i in range(3):
            query = jnp.where(lane == first + 1 + i, tops[i], query)
            graded = jnp.where(lane == first + 1 + i, drops[i], graded)
        query_ref[head] = jnp.where(own, queries, query).astype(bf16)
        back_ref[head] = jnp.where(own, back, graded).astype(bf16)
    skewed_ref[...] = jnp.zeros_like(skewed_ref)
    keys_here = soft_ref.shape[1]
    small_lane = lax.broadcasted_iota(jnp.int32, (keys_here, PAIR), 1)
    small_row = lax.broadcasted_iota(jnp.int32, (keys_here, PAIR), 0)

    def block(index, carry):
        rows = pl.ds(pl.multiple_of(index * keys_here, keys_here), keys_here)
        keys = k_ref[rows, :].astype(f32)
        values = v_ref[rows, :].astype(f32)
        mask = jnp.where(small_row + index * keys_here < length_ref[0], 0.0, -1e9)
        dq, dk, dv = [], [], []
        for head in range(2):
            key = key_side(keys, mask, small_lane, head)
            value = key_side(values, 0.0, small_lane, head)
            scores = lax.dot_general(key, query_ref[head], ROWS_BY_ROWS, preferred_element_type=f32)
            drop = lax.dot_general(value, back_ref[head], ROWS_BY_ROWS, preferred_element_type=f32)
            for first in range(0, keys_here, QB):
                piece = slice(first, first + QB)
                start = pl.multiple_of(seq_len - QB + first_row - index * keys_here - first, QB)
                soft = jnp.exp(scores[piece] + skew_ref[head, :, pl.ds(start, rows_here)])
                score_grad = soft * drop[piece]
                skewed_ref[head, :, pl.ds(start, rows_here)] += score_grad
                soft_ref[head, piece, :] = soft.astype(bf16)
                slope_ref[head, piece, :] = score_grad.astype(bf16)
            dv.append(jnp.dot(soft_ref[head], back_ref[head], preferred_element_type=f32))
            dk.append(jnp.dot(slope_ref[head], query_ref[head], preferred_element_type=f32))
            dq.append(lax.dot_general(slope_ref[head], key, COLS_BY_COLS, preferred_element_type=f32))
        dk = jnp.where(small_lane < HD, dk[0], dk[1])
        dv = jnp.where(small_lane < HD, dv[0], dv[1])
        if running:
            dk = dk + dk_before[rows, :]
            dv = dv + dv_before[rows, :]
        dk_ref[rows, :] = dk.astype(dk_ref.dtype)
        dv_ref[rows, :] = dv.astype(dv_ref.dtype)
        dq = jnp.where(lane < HD, dq[0], dq[1])

        @pl.when(index == 0)
        def _():
            dq_sum[...] = dq

        @pl.when(index > 0)
        def _():
            dq_sum[...] += dq

        return carry

    lax.fori_loop(0, seq_len // keys_here, block, 0, unroll=True)
    dq_ref[...] = (dq_sum[...] * 0.125).astype(bf16)
    for head in range(2):
        diagonal_ref[head] = diagonal_sums(jnp.concatenate([skewed_ref[head], jnp.zeros((QB, QB), f32)], axis=1))


def attend_back(projected, context_grad, context, totals, lengths, skew, chunk, chunks, before=(), group=(0, 1)):
    _, seq_len, width = projected.shape
    pairs = width // PAIR // group[1]
    ahead = group[0] * pairs
    width = pairs * PAIR
    rows_here = seq_len // chunks
    key_block = min(KEY_BLOCK, seq_len)
    skew_width = skew.shape[2]
    whole = [pl.BlockSpec((None, seq_len, PAIR), lambda p, t=t: (t, 0, p + ahead)) for t in (1, 2)]
    part = pl.BlockSpec((rows_here, PAIR), lambda p: (0, p + ahead))
    full = pl.BlockSpec((seq_len, PAIR), lambda p: (0, p + ahead))
    last = chunk == chunks - 1
    assert last or group == (0, 1)
    if last:
        out_specs = [pl.BlockSpec((3, seq_len, PAIR), lambda p: (0, 0, p))]
        out_shape = [jax.ShapeDtypeStruct((3, seq_len, width), bf16)]
    else:
        out_specs = [part, full, full]
        out_shape = [jax.ShapeDtypeStruct((rows_here, width), bf16)] + [jax.ShapeDtypeStruct((seq_len, width), f32)] * 2
    return pl.pallas_call(
        lambda *refs: backward_kernel(chunk * rows_here, last, *refs),
        grid=(pairs,),
        in_specs=[
            pl.BlockSpec(memory_space=pltpu.SMEM),
            pl.BlockSpec((None, rows_here, PAIR), lambda p: (0, chunk, p + ahead)),
            *whole,
            part,
            part,
            part,
            pl.BlockSpec((2, QB, skew_width), lambda p: (p + ahead, 0, 0)),
            *[part, full, full][: len(before)],
        ],
        out_specs=out_specs + [pl.BlockSpec((2, 1, skew_width + QB), lambda p: (p, 0, 0))],
        out_shape=out_shape + [jax.ShapeDtypeStruct((width // HD, 1, skew_width + QB), f32)],
        scratch_shapes=[
            pltpu.VMEM((2, rows_here, PAIR), bf16),
            pltpu.VMEM((2, rows_here, PAIR), bf16),
            pltpu.VMEM((2, QB, skew_width), f32),
            pltpu.VMEM((rows_here, PAIR), f32),
            pltpu.VMEM((2, key_block, rows_here), bf16),
            pltpu.VMEM((2, key_block, rows_here), bf16),
        ],
        compiler_params=pltpu.CompilerParams(vmem_limit_bytes=VMEM_LIMIT),
        cost_estimate=cost(18 if group[1] == 1 else 10.5),
        name="attend_back",
    )(lengths, projected, projected, projected, context_grad, context, totals, skew, *before)


def unit(values):
    row_mean = jnp.mean(values, axis=-1, keepdims=True)
    centered = values - row_mean
    spread = jnp.mean(centered * centered, axis=-1, keepdims=True)
    inverse = lax.rsqrt(spread + 1e-05)
    return (centered * inverse, inverse)


def ffn_kernel(x_ref, one_ref, two_ref, cot_ref, norm_ref, up_ref, down_ref, middle_ref, normed_ref, hidden_ref, pre_ref, grad_ref, out_ref, grad_sum, out_sum):
    step = pl.program_id(0)

    @pl.when(step == 0)
    def _():
        middle = x_ref[...].astype(f32) + (one_ref[...].astype(f32) + two_ref[...].astype(f32))
        middle_ref[...] = middle
        normed_ref[...] = (unit(middle)[0] * norm_ref[2:3, :] + norm_ref[3:4, :]).astype(bf16)
        grad_sum[...] = jnp.zeros_like(grad_sum)
        out_sum[...] = jnp.zeros_like(out_sum)

    up = up_ref[...].astype(bf16)
    down = down_ref[...].astype(bf16)
    block = min(512, x_ref.shape[0])
    for first in range(0, x_ref.shape[0], block):
        rows = pl.ds(first, block)
        hidden_pre = jnp.dot(normed_ref[rows, :], up, preferred_element_type=f32)
        hidden_grad = jnp.dot(cot_ref[rows, :], down, preferred_element_type=f32)
        gate = 0.5 + 0.5 * lax.erf(hidden_pre * 0.7071067811865476)
        slope = gate + hidden_pre * (0.3989422804014327 * jnp.exp(-0.5 * hidden_pre * hidden_pre))
        hidden = (hidden_pre * gate).astype(bf16)
        pre_grad = (hidden_grad * slope).astype(bf16)
        hidden_ref[rows, :] = hidden
        pre_ref[rows, :] = pre_grad
        grad_sum[rows, :] += lax.dot_general(pre_grad, up, ROWS_BY_ROWS, preferred_element_type=f32)
        out_sum[rows, :] += lax.dot_general(hidden, down, ROWS_BY_ROWS, preferred_element_type=f32)

    @pl.when(step == pl.num_programs(0) - 1)
    def _():
        grad_ref[...] = grad_sum[...].astype(bf16)
        out_ref[...] = out_sum[...].astype(bf16)


def feed_forward(x_rows, branch_one, branch_two, cot_rows, norm_params, weights_ffn):
    rows, width = x_rows.shape
    units = weights_ffn.shape[2]
    tile = min(512, units)
    whole = pl.BlockSpec((rows, width), lambda f: (0, 0))
    tall = pl.BlockSpec((rows, tile), lambda f: (0, f))
    return pl.pallas_call(
        ffn_kernel,
        grid=(units // tile,),
        in_specs=[
            whole,
            whole,
            whole,
            whole,
            pl.BlockSpec(norm_params.shape, lambda f: (0, 0)),
            pl.BlockSpec((None, width, tile), lambda f: (0, 0, f)),
            pl.BlockSpec((None, width, tile), lambda f: (1, 0, f)),
        ],
        out_specs=[whole, whole, tall, tall, whole, whole],
        out_shape=[
            jax.ShapeDtypeStruct((rows, width), f32),
            jax.ShapeDtypeStruct((rows, width), bf16),
            jax.ShapeDtypeStruct((rows, units), bf16),
            jax.ShapeDtypeStruct((rows, units), bf16),
            jax.ShapeDtypeStruct((rows, width), bf16),
            jax.ShapeDtypeStruct((rows, width), bf16),
        ],
        scratch_shapes=[pltpu.VMEM((rows, width), f32)] * 2,
        compiler_params=pltpu.CompilerParams(vmem_limit_bytes=VMEM_LIMIT),
        cost_estimate=cost(17.5),
        name="feed_forward",
    )(x_rows, branch_one, branch_two, cot_rows, norm_params, weights_ffn, weights_ffn)


def weight_kernel(order, core_ref, *refs):
    chunks = (len(refs) - 3) // 2
    lefts, rights = refs[:chunks], refs[chunks : 2 * chunks]
    sent_ref, kept_ref, left_ref = refs[2 * chunks :]
    rows = lefts[0].shape[0]
    half = left_ref.shape[1]
    share = 2 * half // len(order)

    @pl.when(pl.program_id(0) == 0)
    def _():
        for chunk in range(chunks):
            turned = lefts[chunk][...].T
            for block, place in enumerate(order):
                core, first = divmod(place * share, half)
                which = jnp.where(core_ref[0] == core, 1, 0)
                left_ref[which, first : first + share, chunk * rows : (chunk + 1) * rows] = turned[
                    block * share : (block + 1) * share
                ]

    left = left_ref[...].reshape(2 * half, chunks * rows)
    total = 0.0
    for chunk in range(chunks):
        piece = left[:, chunk * rows : (chunk + 1) * rows]
        total = total + jnp.dot(piece, rights[chunk][...], preferred_element_type=f32)
    sent_ref[...] = total[:half].astype(bf16)
    kept_ref[...] = total[half:].astype(bf16)


def block_order(bits):
    places = range(len(bits))
    return [sum(((i >> bits[p]) & 1) << (len(bits) - 1 - p) for p in places) for i in range(1 << len(bits))]


def weight_halves(lefts, rights, core, bits):
    rows, features = lefts[0].shape
    chunks = len(lefts)
    if len(rights) == chunks:
        columns = rights[0].shape[1]
        tile = min(512, columns)
        right_specs = [pl.BlockSpec((rows, tile), lambda c: (0, c))] * chunks
    else:
        parts, _, tile = rights[0].shape
        columns = parts * tile
        right_specs = [pl.BlockSpec((None, rows, tile), lambda c, k=k: (c, k, 0)) for k in range(chunks)]
        rights = rights * chunks
    result = pl.BlockSpec((features // 2, tile), lambda c: (0, c))
    order = block_order(bits)
    return pl.pallas_call(
        lambda *refs: weight_kernel(order, *refs),
        grid=(columns // tile,),
        in_specs=[
            pl.BlockSpec(memory_space=pltpu.SMEM),
            *[pl.BlockSpec((rows, features), lambda c: (0, 0))] * chunks,
            *right_specs,
        ],
        out_specs=[result, result],
        out_shape=[jax.ShapeDtypeStruct((features // 2, columns), bf16)] * 2,
        scratch_shapes=[pltpu.VMEM((2, features // 2, rows * chunks), bf16)],
        compiler_params=pltpu.CompilerParams(vmem_limit_bytes=VMEM_LIMIT),
        cost_estimate=cost(8.8 * columns / 2048 + 2),
        name="weight_halves",
    )(core, *lefts, *rights)


def middle_kernel(part_ref, other_ref, middle_ref, cot_ref, norm_ref, weight_ref, grad_ref, branch_ref, context_ref, sums_ref):
    grad = part_ref[...].astype(f32) + other_ref[...].astype(f32)
    rows, inverse = unit(middle_ref[...])
    grad_unit = grad * norm_ref[2:3, :]
    first_mean = jnp.mean(grad_unit, axis=-1, keepdims=True)
    second_mean = jnp.mean(grad_unit * rows, axis=-1, keepdims=True)
    whole = cot_ref[...].astype(f32) + inverse * (grad_unit - first_mean - rows * second_mean)
    grad_ref[...] = whole
    branch_ref[...] = whole.astype(bf16)
    context_ref[...] = jnp.dot(branch_ref[...], weight_ref[...], preferred_element_type=f32).astype(bf16)
    gain = jnp.sum(grad * rows, axis=0, keepdims=True)
    shift = jnp.sum(grad, axis=0, keepdims=True)

    @pl.when(pl.program_id(0) == 0)
    def _():
        sums_ref[0:1, :] = gain
        sums_ref[1:2, :] = shift

    @pl.when(pl.program_id(0) > 0)
    def _():
        sums_ref[0:1, :] += gain
        sums_ref[1:2, :] += shift


def middle_back(part, other, middle, cot_rows, norm_params, weights_out):
    rows, width = part.shape
    block = min(256, rows)
    columns = weights_out.shape[1]
    piece = pl.BlockSpec((block, width), lambda r: (r, 0))
    return pl.pallas_call(
        middle_kernel,
        grid=(rows // block,),
        in_specs=[
            piece,
            piece,
            piece,
            piece,
            pl.BlockSpec(norm_params.shape, lambda r: (0, 0)),
            pl.BlockSpec(weights_out.shape, lambda r: (0, 0)),
        ],
        out_specs=[piece, piece, pl.BlockSpec((block, columns), lambda r: (r, 0)), pl.BlockSpec((2, width), lambda r: (0, 0))],
        out_shape=[
            jax.ShapeDtypeStruct((rows, width), f32),
            jax.ShapeDtypeStruct((rows, width), bf16),
            jax.ShapeDtypeStruct((rows, columns), bf16),
            jax.ShapeDtypeStruct((2, width), f32),
        ],
        compiler_params=pltpu.CompilerParams(vmem_limit_bytes=VMEM_LIMIT),
        cost_estimate=cost(6),
        name="middle_back",
    )(part, other, middle, cot_rows, norm_params, weights_out)


def first_kernel(groups, place_ref, *refs):
    grads, (weight_ref, x_ref, part_ref, sums_ref) = refs[:groups], refs[groups:]
    width = grads[0].shape[2]
    pieces = [(group, t) for group in range(groups) for t in range(3)]
    left = jnp.concatenate([grads[group][t] for group, t in pieces], axis=1)
    right = jnp.concatenate([weight_ref[t, :, group * width : (group + 1) * width] for group, t in pieces], axis=1)
    part = lax.dot_general(left, right, ROWS_BY_ROWS, preferred_element_type=f32)
    part_ref[...] = part.astype(bf16)
    gain = jnp.sum(part * unit(x_ref[...].astype(f32))[0], axis=0, keepdims=True)
    shift = jnp.sum(part, axis=0, keepdims=True)

    @pl.when(pl.program_id(0) == 0)
    def _():
        sums_ref[0:1, :] = gain
        sums_ref[1:2, :] = shift

    @pl.when(pl.program_id(0) > 0)
    def _():
        sums_ref[0:1, :] += gain
        sums_ref[1:2, :] += shift


def first_back(grads, weights_qkv, x_rows, first_row):
    rows, width = x_rows.shape
    block = min(512, rows)
    columns = grads[0].shape[2]
    return pl.pallas_call(
        lambda *refs: first_kernel(len(grads), *refs),
        grid_spec=pltpu.PrefetchScalarGridSpec(
            num_scalar_prefetch=1,
            grid=(rows // block,),
            in_specs=[
                *[pl.BlockSpec((3, block, columns), lambda r, place: (0, r + place[0], 0))] * len(grads),
                pl.BlockSpec(weights_qkv.shape, lambda r, place: (0, 0, 0)),
                pl.BlockSpec((block, width), lambda r, place: (r, 0)),
            ],
            out_specs=[pl.BlockSpec((block, width), lambda r, place: (r, 0)), pl.BlockSpec((2, width), lambda r, place: (0, 0))],
        ),
        out_shape=[jax.ShapeDtypeStruct((rows, width), bf16), jax.ShapeDtypeStruct((2, width), f32)],
        compiler_params=pltpu.CompilerParams(vmem_limit_bytes=VMEM_LIMIT),
        cost_estimate=cost(6),
        name="first_back",
    )(jnp.reshape(first_row // block, (1,)), *grads, weights_qkv, x_rows)


def project_kernel(chunks, *refs):
    xs, (norm_ref, weight_ref), normed_refs, result_ref = refs[:chunks], refs[chunks:][:2], refs[chunks + 2 : -1], refs[-1]
    rows = xs[0].shape[0]
    block = min(256, rows)
    for chunk in range(chunks):
        for first in range(0, rows, block):
            at = pl.ds(first, block)
            values = xs[chunk][at, :].astype(f32)
            normed = (unit(values)[0] * norm_ref[0:1, :] + norm_ref[1:2, :]).astype(bf16)
            normed_refs[chunk][at, :] = normed
            for t in range(3):
                product = jnp.dot(normed, weight_ref[t], preferred_element_type=f32)
                result_ref[t, pl.ds(chunk * rows + first, block), :] = product.astype(bf16)


def project(x_rows, norm_params, weights_qkv):
    chunks = len(x_rows)
    rows, width = x_rows[0].shape
    columns = weights_qkv.shape[2]
    *normed, result = pl.pallas_call(
        lambda *refs: project_kernel(chunks, *refs),
        out_shape=[jax.ShapeDtypeStruct((rows, width), bf16)] * chunks
        + [jax.ShapeDtypeStruct((3, rows * chunks, columns), bf16)],
        compiler_params=pltpu.CompilerParams(vmem_limit_bytes=VMEM_LIMIT),
        cost_estimate=cost(8),
        name="project",
    )(*x_rows, norm_params, weights_qkv)
    return (normed, result)


def halve_kernel(count, bits_ref, *refs):
    for i in range(count):
        kept_ref, got_ref = refs[2 * i : 2 * i + 2]
        results = refs[2 * count + 2 * i : 2 * count + 2 * i + 2]
        half = results[0].shape[0]
        for result, which in zip(results, (1 - bits_ref[i], bits_ref[i])):
            rows = pl.ds(pl.multiple_of(which * half, half), half)
            result[...] = (kept_ref[rows, :].astype(f32) + got_ref[rows, :].astype(f32)).astype(bf16)


def halve(pairs, bits):
    count = len(pairs)
    steps = 2
    while any(kept.shape[1] % (128 * steps) for kept, _ in pairs):
        steps -= 1
    in_specs, out_specs, out_shape = [], [], []
    for kept, _ in pairs:
        rows, columns = kept.shape
        in_specs += [pl.BlockSpec((rows, columns // steps), lambda c: (0, c))] * 2
        out_specs += [pl.BlockSpec((rows // 2, columns // steps), lambda c: (0, c))] * 2
        out_shape += [jax.ShapeDtypeStruct((rows // 2, columns), bf16)] * 2
    results = pl.pallas_call(
        lambda *refs: halve_kernel(count, *refs),
        grid=(steps,),
        in_specs=[pl.BlockSpec(memory_space=pltpu.SMEM)] + in_specs,
        out_specs=out_specs,
        out_shape=out_shape,
        compiler_params=pltpu.CompilerParams(vmem_limit_bytes=VMEM_LIMIT),
        cost_estimate=cost(4),
        name="halve",
    )(jnp.stack(bits), *[x for pair in pairs for x in pair])
    return [tuple(results[2 * i : 2 * i + 2]) for i in range(count)]


def updated(weight, momentum, average, gradient, step_rate):
    next_moment = momentum_keep * momentum + gradient
    next_weight = weight - step_rate * (gradient + momentum_keep * next_moment)
    next_average = average_keep * average + (1.0 - average_keep) * next_weight
    return (gradient, next_moment, next_weight, next_average)


def ffn_update_kernel(rate, place_ref, *refs):
    grads, (weight_ref, momentum_ref, average_ref), results = refs[:4], refs[4:7], refs[7:]
    for i in range(2):
        gradient = grads[2 * i][...].astype(f32) + grads[2 * i + 1][...].astype(f32)
        for result, value in zip(results, updated(weight_ref[i], momentum_ref[i], average_ref[i], gradient, rate)):
            result[i] = value


def ffn_update(up, down, weight, momentum, average, place, rate):
    _, rows, columns = momentum.shape
    share = pl.BlockSpec((2, rows, columns), lambda i, place: (0, 0, 0))
    return pl.pallas_call(
        lambda *refs: ffn_update_kernel(rate, *refs),
        grid_spec=pltpu.PrefetchScalarGridSpec(
            num_scalar_prefetch=1,
            grid=(1,),
            in_specs=[pl.BlockSpec((rows, columns), lambda i, place: (0, 0))] * 4
            + [pl.BlockSpec((2, rows, columns), lambda i, place: (0, place[0], 0)), share, share],
            out_specs=[share] * 4,
        ),
        out_shape=[jax.ShapeDtypeStruct(momentum.shape, f32)] * 4,
        compiler_params=pltpu.CompilerParams(vmem_limit_bytes=VMEM_LIMIT),
        cost_estimate=cost(4.5),
        name="ffn_update",
    )(place, *up, *down, weight, momentum, average)


def attention_update_kernel(groups, rates, place_ref, *refs):
    grads, refs = refs[: 2 * groups + 2], refs[2 * groups + 2 :]
    (weight_qkv, momentum_qkv, average_qkv, weight_out, momentum_out, average_out), results = refs[:6], refs[6:]
    sums = [grads[2 * i][...].astype(f32) + grads[2 * i + 1][...].astype(f32) for i in range(groups + 1)]
    width = sums[0].shape[1] // 3
    for t in range(3):
        gradient = jnp.concatenate([sums[group][:, t * width : (t + 1) * width] for group in range(groups)], axis=1)
        values = updated(weight_qkv[t], momentum_qkv[t], average_qkv[t], gradient, rates[0])
        for result, value in zip(results[:4], values):
            result[t] = value
    values = updated(weight_out[...], momentum_out[...], average_out[...], sums[groups], rates[1])
    for result, value in zip(results[4:], values):
        result[...] = value


def attention_update(qkv, out, qkv_state, out_state, place, rates):
    groups = len(qkv)
    _, rows, columns = qkv_state[1].shape
    many = pl.BlockSpec((3, rows, columns), lambda i, place: (0, 0, 0))
    one = pl.BlockSpec((rows, columns), lambda i, place: (0, 0))
    return pl.pallas_call(
        lambda *refs: attention_update_kernel(groups, rates, *refs),
        grid_spec=pltpu.PrefetchScalarGridSpec(
            num_scalar_prefetch=1,
            grid=(1,),
            in_specs=[pl.BlockSpec((rows, 3 * columns // groups), lambda i, place: (0, 0))] * (2 * groups)
            + [one, one]
            + [pl.BlockSpec((3, rows, columns), lambda i, place: (0, place[0], 0)), many, many]
            + [pl.BlockSpec((rows, columns), lambda i, place: (place[0], 0)), one, one],
            out_specs=[many] * 4 + [one] * 4,
        ),
        out_shape=[jax.ShapeDtypeStruct(qkv_state[1].shape, f32)] * 4 + [jax.ShapeDtypeStruct((rows, columns), f32)] * 4,
        compiler_params=pltpu.CompilerParams(vmem_limit_bytes=VMEM_LIMIT),
        cost_estimate=cost(3),
        name="attention_update",
    )(place, *[x for pair in qkv for x in pair], *out, *qkv_state, *out_state)


def pack_kernel(shares, counts, head_ref, buckets_ref, *refs):
    result_ref = refs[-1]
    one, two, diagonals = refs[: counts[0]], refs[counts[0] : sum(counts[:2])], refs[sum(counts[:2]) : -1]
    norms = [sum(ref[...] for ref in one), sum(ref[...] for ref in two) * (1.0 / shares)]
    rows = jnp.concatenate(norms, axis=0)
    for i in range(rows.shape[1] // 128):
        result_ref[4 * i : 4 * i + 4, :] = rows[:, 128 * i : 128 * i + 128]
    whole = diagonals[0][:, 0, :]
    offsets = whole + jnp.concatenate([ref[:, 0, :] for ref in diagonals[1:]], axis=0)
    first = rows.shape[1] // 32
    heads = result_ref.shape[0] - first
    bins = lax.broadcasted_iota(jnp.int32, (128, offsets.shape[1]), 0)
    hits = (buckets_ref[...] == bins).astype(f32)
    sums = lax.dot_general(offsets, hits, ROWS_BY_ROWS, precision=highest, preferred_element_type=f32)
    if sums.shape[0] < heads:
        sums = jnp.concatenate([sums, jnp.zeros((heads - sums.shape[0], 128), f32)], axis=0)
    result_ref[first:, :] = pltpu.roll(sums, head_ref[0], 0)


def pack_small(one, two, diagonals, buckets, heads, head_first, shares):
    width = one[0].shape[1]
    return pl.pallas_call(
        lambda *refs: pack_kernel(shares, (len(one), len(two)), *refs),
        in_specs=[pl.BlockSpec(memory_space=pltpu.SMEM)]
        + [pl.BlockSpec(memory_space=pltpu.VMEM)] * (1 + len(one) + len(two) + len(diagonals)),
        out_shape=jax.ShapeDtypeStruct((width // 32 + heads, 128), f32),
        cost_estimate=cost(2),
        name="pack_small",
    )(jnp.reshape(head_first, (1,)), buckets, *one, *two, *diagonals)


def small_update_kernel(rate, small_ref, *refs):
    norm_state, bias_state, results = refs[:3], refs[3:6], refs[6:]
    width = norm_state[0].shape[1]
    gradient = jnp.concatenate([small_ref[4 * i : 4 * i + 4, :] for i in range(width // 128)], axis=1)
    for result, value in zip(results[:4], updated(*[ref[...] for ref in norm_state], gradient, rate)):
        result[...] = value
    gradient = small_ref[width // 32 :, : bias_state[0].shape[1]]
    for result, value in zip(results[4:], updated(*[ref[...] for ref in bias_state], gradient, rate)):
        result[...] = value


def small_update(small, norm_state, bias_state, rate):
    return pl.pallas_call(
        lambda *refs: small_update_kernel(rate, *refs),
        out_shape=[jax.ShapeDtypeStruct(norm_state[0].shape, f32)] * 4
        + [jax.ShapeDtypeStruct(bias_state[0].shape, f32)] * 4,
        cost_estimate=cost(1.5),
        name="small_update",
    )(small, *norm_state, *bias_state)


def finish_kernel(place_ref, sent_ref, kept_ref, x_ref, norm_ref, *refs):
    result_ref = refs[-1]
    grad = sent_ref[...].astype(f32) + kept_ref[...].astype(f32)
    rows, inverse = unit(x_ref[...].astype(f32))
    grad_unit = grad * norm_ref[0:1, :]
    first_mean = jnp.mean(grad_unit, axis=-1, keepdims=True)
    second_mean = jnp.mean(grad_unit * rows, axis=-1, keepdims=True)
    back = inverse * (grad_unit - first_mean - rows * second_mean)
    result_ref[...] = back + jnp.where(place_ref[0] == 0, refs[0][...], refs[1][...])


def finish(got, kept, x_rows, norm_params, middle_grad, place):
    rows, width = x_rows.shape
    block = min(256, rows)
    piece = pl.BlockSpec((block, width), lambda r, place: (r, 0))
    chosen = [
        pl.BlockSpec((block, width), lambda r, place: (jnp.where(place[0] == 0, r, 0), 0)),
        pl.BlockSpec((block, width), lambda r, place: (jnp.where(place[0] == 0, 0, r), 0)),
    ]
    return pl.pallas_call(
        finish_kernel,
        grid_spec=pltpu.PrefetchScalarGridSpec(
            num_scalar_prefetch=1,
            grid=(rows // block,),
            in_specs=[piece, piece, piece, pl.BlockSpec(norm_params.shape, lambda r, place: (0, 0)), *chosen],
            out_specs=piece,
        ),
        out_shape=jax.ShapeDtypeStruct((rows, width), f32),
        compiler_params=pltpu.CompilerParams(vmem_limit_bytes=VMEM_LIMIT),
        cost_estimate=cost(5),
        name="finish",
    )(place, got, kept, x_rows, norm_params, *middle_grad)


def after(value, *others):
    return lax.optimization_barrier((value,) + others)[0]


def swap(values, axis, bit):
    size = lax.axis_size(axis)
    return lax.ppermute(values, axis, [(i, i ^ bit) for i in range(size)])


def in_order(own, other):
    first = lax.axis_index("mp") == 0
    return [jnp.where(first, own, other), jnp.where(first, other, own)]


def other_part(rows):
    if lax.axis_size("mp") != 2:
        return (lax.psum(rows.astype(f32), "mp") - rows.astype(f32)).astype(bf16)
    return swap(rows, "mp", 1)


def sum_own(sent, kept):
    return kept.astype(f32) + swap(sent, "mp", 1).astype(f32)


class Reduction:
    def __init__(self, halves, bits):
        self.bits = bits
        self.pass_on(halves)

    def pass_on(self, halves):
        bit, *self.bits = self.bits
        sent, self.kept = halves
        self.got = swap(sent, "dp", 1 << bit)


def step(sums, *others):
    sums = [total for total in sums if total.bits]
    if not sums:
        return []
    place = lax.axis_index("dp")
    pairs = [(total.kept, total.got) for total in sums]
    pairs[0] = (after(pairs[0][0], *others), pairs[0][1])
    results = halve(pairs, [lax.shift_right_logical(place, total.bits[0]) & 1 for total in sums])
    for total, halves in zip(sums, results):
        total.pass_on(halves)
    return [total.kept for total in sums]


def sum_all(values):
    for axis in ("dp", "mp"):
        bit = 1
        while bit < lax.axis_size(axis):
            values = values + swap(values, axis, bit)
            bit *= 2
    return values


def per_device(
    inputs,
    cotangent,
    lengths,
    buckets,
    w_qkv,
    w_out,
    w_ffn,
    norm_params,
    rel_bias,
    momentum_qkv,
    momentum_out,
    momentum_ffn,
    momentum_norms,
    momentum_bias,
    average_qkv,
    average_out,
    average_ffn,
    average_norms,
    average_bias,
):
    model_size = lax.axis_size("mp")
    data_size = lax.axis_size("dp")
    data_bits = data_size.bit_length() - 1
    rows_local = inputs.shape[0]
    seq_len = rows_local * model_size
    width_local = w_qkv.shape[2]
    heads_local = width_local // HD
    head_first = lax.axis_index("mp") * heads_local
    own_first = lax.axis_index("mp") * rows_local
    data_index = lax.axis_index("dp")
    low_bit = data_index & 1
    share_rows = momentum_out.shape[0]
    chunks = 2
    chunk_rows = seq_len // chunks

    def chunk_of(rows, chunk):
        return lax.slice_in_dim(rows, chunk * chunk_rows, (chunk + 1) * chunk_rows, axis=0)

    if model_size == 2:
        inputs_other = swap(inputs, "mp", 1)
        cot_other = swap(after(cotangent, inputs_other), "mp", 1)
        x_rows = in_order(inputs, inputs_other)
        cot_rows = in_order(cotangent, cot_other)
    else:
        inputs_all = lax.all_gather(inputs, "mp", axis=0, tiled=True)
        cot_other = lax.all_gather(cotangent, "mp", axis=0, tiled=True)
        x_rows = [chunk_of(inputs_all, chunk) for chunk in range(chunks)]
        cot_rows = [chunk_of(cot_other, chunk) for chunk in range(chunks)]
    weights_qkv = w_qkv.astype(bf16)
    weights_out = w_out.astype(bf16)

    bias_local = lax.dynamic_slice_in_dim(rel_bias, head_first, heads_local, 1)
    bucket_hits = (buckets[:, None] == jnp.arange(rel_bias.shape[0], dtype=jnp.int32)[None, :]).astype(f32)
    bias_table = jnp.dot(bucket_hits, bias_local, precision=highest).T
    skew, skew_back = skew_tables(bias_table)

    normed_one, projected = project(x_rows, norm_params, weights_qkv)

    context, totals, branch = [], [], []
    ahead = projected
    for chunk in range(chunks):
        part, total, sent = attend(ahead, lengths, skew, weights_out, chunk, chunks)
        context.append(part)
        totals.append(total)
        branch.append(sent)
        ahead = after(ahead, sent, *cot_rows)
    branch_other = []
    for sent in branch:
        branch_other.append(other_part(after(sent, *branch_other[-1:])))

    ffn = []
    ahead = after(w_ffn, branch[-1])
    for chunk in range(chunks):
        ffn.append(
            feed_forward(
                x_rows[chunk], branch[chunk], branch_other[chunk], cot_rows[chunk], norm_params, ahead
            )
        )
        ahead = after(ahead, ffn[-1][4])
    middle, normed_two, hidden, pre_grad, two_part, out_part = zip(*ffn)
    two_other = []
    for sent in two_part:
        two_other.append(other_part(after(sent, *(two_other or branch_other)[-1:])))

    core = jnp.reshape(low_bit, (1,))
    orders = [list(range(data_bits)), [0] + list(range(2, data_bits)) + [1]]
    up = Reduction(weight_halves(normed_two, pre_grad, core, orders[0]), orders[0])
    down = Reduction(
        weight_halves(cot_rows, [hidden[0], after(hidden[1], two_other[0], up.kept)], core, orders[1]), orders[1]
    )

    if model_size == 2:
        out_kept, out_sent = in_order(*out_part)
    else:
        out_got = lax.psum_scatter(jnp.concatenate(out_part), "mp", scatter_dimension=0, tiled=True)
    middle_grad, branch_grad, context_grad = [], [], []

    def middle_step(chunk, *others):
        whole, sent, grad, sums = middle_back(
            after(two_part[chunk], *others), two_other[chunk], middle[chunk], cot_rows[chunk], norm_params, weights_out
        )
        middle_grad.append(whole)
        branch_grad.append(sent)
        context_grad.append(grad)
        return sums

    def back(chunk, others, before=(), group=(0, 1)):
        grad = after(context_grad[chunk], *others)
        return attend_back(
            projected, grad, context[chunk], totals[chunk], lengths, skew_back, chunk, chunks, before, group
        )

    groups = 2 if width_local // PAIR % 2 == 0 else 1
    sums_two = [middle_step(0, down.kept)]
    ties = step([up, down], context_grad[0])
    *before, diagonal = back(0, ties)
    diagonals = [diagonal]
    sums_two.append(middle_step(1, diagonal))
    if model_size == 2:
        out_got = swap(after(out_sent, sums_two[-1]), "mp", 1)
    ties = step([up, down], context_grad[1])
    out_halves = weight_halves([branch_grad[0], after(branch_grad[1], *ties)], context, core, orders[1])
    part, diagonal = back(1, [out_halves[1]], before, (0, groups))
    grads = [part]
    diagonals.append(diagonal)
    halves = weight_halves(normed_one, [part], core, orders[0])
    ties = step([up, down], halves[1])
    qkv = [Reduction((after(halves[0], *ties), halves[1]), orders[0])]
    out = Reduction((after(out_halves[0], *ties), out_halves[1]), orders[1])
    if groups == 2:
        part, diagonal = back(1, ties, before, (1, 2))
        grads.append(part)
        diagonals.append(diagonal)
        ties = step([qkv[0], out], part)
        qkv.append(Reduction(weight_halves(normed_one, [after(part, *ties)], core, orders[1]), orders[1]))
    grads[-1] = after(grads[-1], qkv[-1].kept, *ties)

    one = jnp.reshape(own_first * 0, (1,))
    if model_size == 2:
        sent, sums_sent = first_back(grads, weights_qkv, inputs_other, rows_local - own_first)
        got = swap(sent, "mp", 1)
        ties = step([qkv[-1]], sent)
        grads[-1] = after(grads[-1], *ties)
        kept, sums_kept = first_back(grads, weights_qkv, inputs, own_first)
        sums_one = [sums_sent, sums_kept]
        own = one + lax.axis_index("mp")
        output_rows = in_order(*[after(rows, kept) for rows in middle])[0] + out_kept.astype(f32) + out_got.astype(f32)
    else:
        kept, sums_one = first_back(grads, weights_qkv, jnp.concatenate(x_rows), own_first * 0)
        sums_one = [sums_one]
        kept = lax.psum_scatter(kept, "mp", scatter_dimension=0, tiled=True)
        got = jnp.zeros_like(kept)
        own = one
        middle_grad = [lax.dynamic_slice_in_dim(jnp.concatenate(middle_grad), own_first, rows_local, 0)] * 2
        middle_own = lax.dynamic_slice_in_dim(jnp.concatenate(middle), own_first, rows_local, 0)
        output_rows = middle_own + out_got.astype(f32)
    output = output_rows.astype(bf16)

    reversed_buckets = jnp.pad(buckets[::-1], (0, 1), constant_values=-1)[None, :]
    small = pack_small(sums_one, sums_two, diagonals, reversed_buckets, rel_bias.shape[1], head_first, model_size)
    small = sum_all(small)
    step(qkv + [out], kept)
    while any(total.bits for total in qkv + [out, up, down]):
        step(qkv + [out, up, down])

    scale_factor = 1.0 / math.sqrt(float(seq_len * data_size))
    place = one + lax.axis_index("dp")
    ffn_results = ffn_update(
        (up.kept, up.got), (down.kept, down.got), w_ffn, momentum_ffn, average_ffn, place, 0.05 * scale_factor
    )
    attention_results = attention_update(
        [(total.kept, total.got) for total in qkv],
        (out.kept, out.got),
        (w_qkv, momentum_qkv, average_qkv),
        (w_out, momentum_out, average_out),
        place,
        (0.3 * scale_factor, 0.1 * scale_factor),
    )
    input_grad = finish(got, kept, inputs, norm_params, middle_grad, own)
    small_results = small_update(
        small,
        (norm_params, momentum_norms, average_norms),
        (rel_bias.T, momentum_bias.T, average_bias.T),
        0.05 * scale_factor,
    )
    small_results = [*small_results[:4], *[result.T for result in small_results[4:]]]
    return (output, input_grad, *attention_results, *ffn_results, *small_results)


def solution(mesh):
    return jax.shard_map(
        per_device,
        mesh=mesh,
        in_specs=(
            P(("dp", "mp"), None),
            P(("dp", "mp"), None),
            P("dp"),
            P(),
            P(None, None, "mp"),
            P(None, "mp"),
            P(None, None, "mp"),
            P(),
            P(),
            P(None, "dp", "mp"),
            P("dp", "mp"),
            P(None, "dp", "mp"),
            P(),
            P(),
            P(None, "dp", "mp"),
            P("dp", "mp"),
            P(None, "dp", "mp"),
            P(),
            P(),
        ),
        out_specs=(
            P(("dp", "mp"), None),
            P(("dp", "mp"), None),
            P(None, "dp", "mp"),
            P(None, "dp", "mp"),
            P(None, "dp", "mp"),
            P(None, "dp", "mp"),
            P("dp", "mp"),
            P("dp", "mp"),
            P("dp", "mp"),
            P("dp", "mp"),
            P(None, "dp", "mp"),
            P(None, "dp", "mp"),
            P(None, "dp", "mp"),
            P(None, "dp", "mp"),
            P(),
            P(),
            P(),
            P(),
            P(),
            P(),
            P(),
            P(),
        ),
        check_vma=False,
    )
```

```python
import math

import jax
import jax.numpy as jnp
from jax import lax
from jax.experimental import pallas as pl
from jax.experimental.pallas import tpu as pltpu
from jax.sharding import PartitionSpec as P

HD = 64
PAIR = 2 * HD
QB = 128
QUERY_BLOCK = 512
KEY_BLOCK = 512
f32 = jnp.float32
bf16 = jnp.bfloat16
ROWS_BY_ROWS = (((1,), (1,)), ((), ()))
COLS_BY_COLS = (((0,), (0,)), ((), ()))
VMEM_LIMIT = 56 * 2**20

highest = lax.Precision.HIGHEST
momentum_keep = 0.5
average_keep = 0.5
SHARE = 1.1e6


def cost(microseconds):
    return pl.CostEstimate(flops=0, bytes_accessed=int(SHARE * microseconds), transcendentals=0)


def skew_kernel(forward_ref, reverse_ref, forward_out, reverse_out):
    width = forward_ref.shape[2]
    for source, result in ((forward_ref, forward_out), (reverse_ref, reverse_out)):
        rows = jnp.broadcast_to(source[0], (QB, width))
        result[0] = pltpu.roll(rows, width - (QB - 1), 1, stride=1, stride_axis=0)[:, : width - QB]


def skew_tables(table):
    heads, width = table.shape
    forward = jnp.pad(table, ((0, 0), (0, 1)))[:, None, :]
    reverse = jnp.pad(table[:, ::-1], ((0, 0), (0, 1)))[:, None, :]
    width += 1
    row = pl.BlockSpec((1, 1, width), lambda h: (h, 0, 0))
    skewed = pl.BlockSpec((1, QB, width - QB), lambda h: (h, 0, 0))
    shape = jax.ShapeDtypeStruct((heads, QB, width - QB), f32)
    return pl.pallas_call(
        skew_kernel,
        grid=(heads,),
        in_specs=[row, row],
        out_specs=[skewed, skewed],
        out_shape=[shape, shape],
        cost_estimate=cost(8),
        name="skew",
    )(forward, reverse)


def three_parts(values):
    first = values.astype(bf16).astype(f32)
    rest = values - first
    second = rest.astype(bf16).astype(f32)
    return (first, second, rest - second)


def own_lanes(lane, head):
    return (lane >= HD) if head else (lane < HD)


def key_side(keys, mask, lane, head):
    first = 0 if head else HD
    extra = jnp.where(lane == first, mask, jnp.where((lane > first) & (lane < first + 4), 1.0, 0.0))
    return jnp.where(own_lanes(lane, head), keys, extra).astype(bf16)


def forward_kernel(
    first_row,
    length_ref,
    q_ref,
    k_ref,
    v_ref,
    skew_ref,
    weight_ref,
    context_ref,
    total_ref,
    branch_ref,
    key_ref,
    value_ref,
    raised_ref,
    gathered_ref,
):
    seq_len = k_ref.shape[0]
    rows_here = q_ref.shape[0]
    lane = lax.broadcasted_iota(jnp.int32, (seq_len, PAIR), 1)
    place = lax.broadcasted_iota(jnp.int32, (seq_len, PAIR), 0)
    mask = jnp.where(place < length_ref[0], 0.0, -1e9)
    keys = k_ref[...].astype(f32)
    values = v_ref[...].astype(f32)
    for head in range(2):
        key_ref[head] = key_side(keys, mask, lane, head)
        value_ref[head] = jnp.where(own_lanes(lane, head), values, 1.0).astype(bf16)
    here = min(QUERY_BLOCK, rows_here)
    lane = lax.broadcasted_iota(jnp.int32, (here, PAIR), 1)

    def block(index, carry):
        rows = pl.ds(pl.multiple_of(index * here, here), here)
        queries = q_ref[rows, :].astype(f32) * 0.125
        context = []
        totals = []
        for head in range(2):
            own = own_lanes(lane, head)
            first = 0 if head else HD
            query = jnp.where(own, queries, jnp.where(lane == first, 1.0, 0.0)).astype(bf16)
            scores = lax.dot_general(query, key_ref[head], ROWS_BY_ROWS, preferred_element_type=f32)
            tops = []
            for piece in range(0, here, QB):
                start = pl.multiple_of(seq_len - QB - first_row - index * here - piece, QB)
                moved = scores[piece : piece + QB] + skew_ref[head, :, pl.ds(start, seq_len)]
                top = jnp.max(moved, axis=1, keepdims=True)
                raised_ref[head, piece : piece + QB, :] = jnp.exp(moved - top).astype(bf16)
                tops.append(top)
            weighted = jnp.dot(raised_ref[head], value_ref[head], preferred_element_type=f32)
            context.append(weighted / weighted[:, first : first + 1])
            totals.append(jnp.concatenate(tops, axis=0) + jnp.log(jnp.where(own, 1.0, weighted)))
        context_ref[rows, :] = jnp.where(lane < HD, context[0], context[1]).astype(bf16)
        total_ref[rows, :] = jnp.where(lane < HD, totals[1], totals[0])
        return carry

    lax.fori_loop(0, rows_here // here, block, 0, unroll=True)
    step = pl.program_id(0)
    gathered_ref[step] = context_ref[...]

    @pl.when(step == pl.num_programs(0) - 1)
    def _():
        gathered = jnp.concatenate([gathered_ref[p] for p in range(gathered_ref.shape[0])], axis=1)
        branch_ref[...] = lax.dot_general(gathered, weight_ref[...], ROWS_BY_ROWS, preferred_element_type=f32).astype(bf16)


def attend(projected, lengths, skew, weights_out, chunk, chunks):
    _, seq_len, width = projected.shape
    features = weights_out.shape[0]
    rows_here = seq_len // chunks
    whole = [pl.BlockSpec((None, seq_len, PAIR), lambda p, t=t: (t, 0, p)) for t in (1, 2)]
    part = pl.BlockSpec((rows_here, PAIR), lambda p: (0, p))
    return pl.pallas_call(
        lambda *refs: forward_kernel(chunk * rows_here, *refs),
        grid=(width // PAIR,),
        in_specs=[
            pl.BlockSpec(memory_space=pltpu.SMEM),
            pl.BlockSpec((None, rows_here, PAIR), lambda p: (0, chunk, p)),
            *whole,
            pl.BlockSpec((2,) + skew.shape[1:], lambda p: (p, 0, 0)),
            pl.BlockSpec(weights_out.shape, lambda p: (0, 0)),
        ],
        out_specs=[part, part, pl.BlockSpec((rows_here, features), lambda p: (0, 0))],
        out_shape=[
            jax.ShapeDtypeStruct((rows_here, width), bf16),
            jax.ShapeDtypeStruct((rows_here, width), f32),
            jax.ShapeDtypeStruct((rows_here, features), bf16),
        ],
        scratch_shapes=[
            pltpu.VMEM((2, seq_len, PAIR), bf16),
            pltpu.VMEM((2, seq_len, PAIR), bf16),
            pltpu.VMEM((2, min(QUERY_BLOCK, rows_here), seq_len), bf16),
            pltpu.VMEM((width // PAIR, rows_here, PAIR), bf16),
        ],
        compiler_params=pltpu.CompilerParams(vmem_limit_bytes=VMEM_LIMIT),
        cost_estimate=cost(13),
        name="attend",
    )(lengths, projected, projected, projected, skew, weights_out)


def diagonal_sums(skewed):
    width = skewed.shape[1]
    total = pltpu.roll(skewed[:8], QB - 1, 1)
    for group in range(1, QB // 8):
        total = total + pltpu.roll(skewed[8 * group : 8 * group + 8], QB - 1 - 8 * group, 1)
    row = lax.broadcasted_iota(jnp.int32, total.shape, 0)
    for bit in (1, 2, 4):
        total = jnp.where((row & bit) != 0, pltpu.roll(total, width - bit, 1), total)
    return jnp.sum(total, axis=0, keepdims=True)


def backward_kernel(first_row, last, *refs):
    (length_ref, q_ref, k_ref, v_ref, grad_ref, context_ref, total_ref, skew_ref) = refs[:8]
    running = last and first_row > 0
    if running:
        dq_before, dk_before, dv_before = refs[8:11]
    if last:
        grads_ref, diagonal_ref = refs[-8:-6]
        dq_ref = grads_ref.at[0, pl.ds(first_row, q_ref.shape[0]), :]
        dk_ref, dv_ref = grads_ref.at[1], grads_ref.at[2]
    else:
        dq_ref, dk_ref, dv_ref, diagonal_ref = refs[-10:-6]
    (query_ref, back_ref, skewed_ref, dq_sum, soft_ref, slope_ref) = refs[-6:]
    if running:
        grads_ref[0, :first_row, :] = dq_before[...]
    seq_len = k_ref.shape[0]
    rows_here = q_ref.shape[0]
    lane = lax.broadcasted_iota(jnp.int32, (rows_here, PAIR), 1)
    queries = q_ref[...].astype(f32) * 0.125
    back = grad_ref[...].astype(f32)
    dots = back * context_ref[...].astype(f32)
    first_lane = lax.broadcasted_iota(jnp.int32, (PAIR, PAIR), 0) // HD
    cross = jnp.where(first_lane != lax.broadcasted_iota(jnp.int32, (PAIR, PAIR), 1) // HD, 1.0, 0.0).astype(bf16)
    row_dot = sum(jnp.dot(part.astype(bf16), cross, preferred_element_type=f32) for part in three_parts(dots)[:2])
    tops = three_parts(-total_ref[...])
    drops = three_parts(-row_dot)
    for head in range(2):
        own = own_lanes(lane, head)
        first = 0 if head else HD
        query = jnp.where(lane == first, 1.0, 0.0)
        graded = jnp.zeros_like(query)
        for i in range(3):
            query = jnp.where(lane == first + 1 + i, tops[i], query)
            graded = jnp.where(lane == first + 1 + i, drops[i], graded)
        query_ref[head] = jnp.where(own, queries, query).astype(bf16)
        back_ref[head] = jnp.where(own, back, graded).astype(bf16)
    skewed_ref[...] = jnp.zeros_like(skewed_ref)
    keys_here = soft_ref.shape[1]
    small_lane = lax.broadcasted_iota(jnp.int32, (keys_here, PAIR), 1)
    small_row = lax.broadcasted_iota(jnp.int32, (keys_here, PAIR), 0)

    def block(index, carry):
        rows = pl.ds(pl.multiple_of(index * keys_here, keys_here), keys_here)
        keys = k_ref[rows, :].astype(f32)
        values = v_ref[rows, :].astype(f32)
        mask = jnp.where(small_row + index * keys_here < length_ref[0], 0.0, -1e9)
        dq, dk, dv = [], [], []
        for head in range(2):
            key = key_side(keys, mask, small_lane, head)
            value = key_side(values, 0.0, small_lane, head)
            scores = lax.dot_general(key, query_ref[head], ROWS_BY_ROWS, preferred_element_type=f32)
            drop = lax.dot_general(value, back_ref[head], ROWS_BY_ROWS, preferred_element_type=f32)
            for first in range(0, keys_here, QB):
                piece = slice(first, first + QB)
                start = pl.multiple_of(seq_len - QB + first_row - index * keys_here - first, QB)
                soft = jnp.exp(scores[piece] + skew_ref[head, :, pl.ds(start, rows_here)])
                score_grad = soft * drop[piece]
                skewed_ref[head, :, pl.ds(start, rows_here)] += score_grad
                soft_ref[head, piece, :] = soft.astype(bf16)
                slope_ref[head, piece, :] = score_grad.astype(bf16)
            dv.append(jnp.dot(soft_ref[head], back_ref[head], preferred_element_type=f32))
            dk.append(jnp.dot(slope_ref[head], query_ref[head], preferred_element_type=f32))
            dq.append(lax.dot_general(slope_ref[head], key, COLS_BY_COLS, preferred_element_type=f32))
        dk = jnp.where(small_lane < HD, dk[0], dk[1])
        dv = jnp.where(small_lane < HD, dv[0], dv[1])
        if running:
            dk = dk + dk_before[rows, :]
            dv = dv + dv_before[rows, :]
        dk_ref[rows, :] = dk.astype(dk_ref.dtype)
        dv_ref[rows, :] = dv.astype(dv_ref.dtype)
        dq = jnp.where(lane < HD, dq[0], dq[1])

        @pl.when(index == 0)
        def _():
            dq_sum[...] = dq

        @pl.when(index > 0)
        def _():
            dq_sum[...] += dq

        return carry

    lax.fori_loop(0, seq_len // keys_here, block, 0, unroll=True)
    dq_ref[...] = (dq_sum[...] * 0.125).astype(bf16)
    for head in range(2):
        diagonal_ref[head] = diagonal_sums(jnp.concatenate([skewed_ref[head], jnp.zeros((QB, QB), f32)], axis=1))


def attend_back(projected, context_grad, context, totals, lengths, skew, chunk, chunks, before=()):
    _, seq_len, width = projected.shape
    pairs = width // PAIR
    rows_here = seq_len // chunks
    key_block = min(KEY_BLOCK, seq_len)
    skew_width = skew.shape[2]
    whole = [pl.BlockSpec((None, seq_len, PAIR), lambda p, t=t: (t, 0, p)) for t in (1, 2)]
    part = pl.BlockSpec((rows_here, PAIR), lambda p: (0, p))
    full = pl.BlockSpec((seq_len, PAIR), lambda p: (0, p))
    last = chunk == chunks - 1
    if last:
        out_specs = [pl.BlockSpec((3, seq_len, PAIR), lambda p: (0, 0, p))]
        out_shape = [jax.ShapeDtypeStruct((3, seq_len, width), bf16)]
    else:
        out_specs = [part, full, full]
        out_shape = [jax.ShapeDtypeStruct((rows_here, width), bf16)] + [jax.ShapeDtypeStruct((seq_len, width), f32)] * 2
    return pl.pallas_call(
        lambda *refs: backward_kernel(chunk * rows_here, last, *refs),
        grid=(pairs,),
        in_specs=[
            pl.BlockSpec(memory_space=pltpu.SMEM),
            pl.BlockSpec((None, rows_here, PAIR), lambda p: (0, chunk, p)),
            *whole,
            part,
            part,
            part,
            pl.BlockSpec((2, QB, skew_width), lambda p: (p, 0, 0)),
            *[part, full, full][: len(before)],
        ],
        out_specs=out_specs + [pl.BlockSpec((2, 1, skew_width + QB), lambda p: (p, 0, 0))],
        out_shape=out_shape + [jax.ShapeDtypeStruct((width // HD, 1, skew_width + QB), f32)],
        scratch_shapes=[
            pltpu.VMEM((2, rows_here, PAIR), bf16),
            pltpu.VMEM((2, rows_here, PAIR), bf16),
            pltpu.VMEM((2, QB, skew_width), f32),
            pltpu.VMEM((rows_here, PAIR), f32),
            pltpu.VMEM((2, key_block, rows_here), bf16),
            pltpu.VMEM((2, key_block, rows_here), bf16),
        ],
        compiler_params=pltpu.CompilerParams(vmem_limit_bytes=VMEM_LIMIT),
        cost_estimate=cost(18),
        name="attend_back",
    )(lengths, projected, projected, projected, context_grad, context, totals, skew, *before)


def unit(values):
    row_mean = jnp.mean(values, axis=-1, keepdims=True)
    centered = values - row_mean
    spread = jnp.mean(centered * centered, axis=-1, keepdims=True)
    inverse = lax.rsqrt(spread + 1e-05)
    return (centered * inverse, inverse)


def ffn_kernel(x_ref, one_ref, two_ref, cot_ref, norm_ref, up_ref, down_ref, middle_ref, normed_ref, hidden_ref, pre_ref, grad_ref, out_ref, grad_sum, out_sum):
    step = pl.program_id(0)

    @pl.when(step == 0)
    def _():
        middle = x_ref[...].astype(f32) + (one_ref[...].astype(f32) + two_ref[...].astype(f32))
        middle_ref[...] = middle
        normed_ref[...] = (unit(middle)[0] * norm_ref[2:3, :] + norm_ref[3:4, :]).astype(bf16)
        grad_sum[...] = jnp.zeros_like(grad_sum)
        out_sum[...] = jnp.zeros_like(out_sum)

    up = up_ref[...].astype(bf16)
    down = down_ref[...].astype(bf16)
    block = min(512, x_ref.shape[0])
    for first in range(0, x_ref.shape[0], block):
        rows = pl.ds(first, block)
        hidden_pre = jnp.dot(normed_ref[rows, :], up, preferred_element_type=f32)
        hidden_grad = jnp.dot(cot_ref[rows, :], down, preferred_element_type=f32)
        gate = 0.5 + 0.5 * lax.erf(hidden_pre * 0.7071067811865476)
        slope = gate + hidden_pre * (0.3989422804014327 * jnp.exp(-0.5 * hidden_pre * hidden_pre))
        hidden = (hidden_pre * gate).astype(bf16)
        pre_grad = (hidden_grad * slope).astype(bf16)
        hidden_ref[rows, :] = hidden
        pre_ref[rows, :] = pre_grad
        grad_sum[rows, :] += lax.dot_general(pre_grad, up, ROWS_BY_ROWS, preferred_element_type=f32)
        out_sum[rows, :] += lax.dot_general(hidden, down, ROWS_BY_ROWS, preferred_element_type=f32)

    @pl.when(step == pl.num_programs(0) - 1)
    def _():
        grad_ref[...] = grad_sum[...].astype(bf16)
        out_ref[...] = out_sum[...].astype(bf16)


def feed_forward(x_rows, branch_one, branch_two, cot_rows, norm_params, weights_ffn):
    rows, width = x_rows.shape
    units = weights_ffn.shape[2]
    tile = min(512, units)
    whole = pl.BlockSpec((rows, width), lambda f: (0, 0))
    tall = pl.BlockSpec((rows, tile), lambda f: (0, f))
    return pl.pallas_call(
        ffn_kernel,
        grid=(units // tile,),
        in_specs=[
            whole,
            whole,
            whole,
            whole,
            pl.BlockSpec(norm_params.shape, lambda f: (0, 0)),
            pl.BlockSpec((None, width, tile), lambda f: (0, 0, f)),
            pl.BlockSpec((None, width, tile), lambda f: (1, 0, f)),
        ],
        out_specs=[whole, whole, tall, tall, whole, whole],
        out_shape=[
            jax.ShapeDtypeStruct((rows, width), f32),
            jax.ShapeDtypeStruct((rows, width), bf16),
            jax.ShapeDtypeStruct((rows, units), bf16),
            jax.ShapeDtypeStruct((rows, units), bf16),
            jax.ShapeDtypeStruct((rows, width), bf16),
            jax.ShapeDtypeStruct((rows, width), bf16),
        ],
        scratch_shapes=[pltpu.VMEM((rows, width), f32)] * 2,
        compiler_params=pltpu.CompilerParams(vmem_limit_bytes=VMEM_LIMIT),
        cost_estimate=cost(17.5),
        name="feed_forward",
    )(x_rows, branch_one, branch_two, cot_rows, norm_params, weights_ffn, weights_ffn)


def ring_order(size):
    if size % 8:
        return list(range(size))
    rows, columns = 4, size // 8
    chips = [(row, 0) for row in range(rows)]
    for turn, row in enumerate(range(rows - 1, -1, -1)):
        across = [(row, column) for column in range(1, columns)]
        chips += across[::-1] if turn % 2 else across
    cores = [(0, 1) if turn % 2 == 0 else (1, 0) for turn in range(len(chips))]
    return [(row * columns + column) * 2 + core for (row, column), pair in zip(chips, cores) for core in pair]


def weight_kernel(order, chunks, *refs):
    lefts, rights = refs[:chunks], refs[chunks : 2 * chunks]
    result_ref, left_ref = refs[-2:]
    rows, features = lefts[0].shape
    share = features // len(order)

    @pl.when(pl.program_id(0) == 0)
    def _():
        for chunk in range(chunks):
            turned = lefts[chunk][...].T
            for position, block in enumerate(order):
                left_ref[position * share : (position + 1) * share, chunk * rows : (chunk + 1) * rows] = turned[
                    block * share : (block + 1) * share
                ]

    total = 0.0
    for chunk in range(chunks):
        left = left_ref[:, chunk * rows : (chunk + 1) * rows]
        total = total + jnp.dot(left, rights[chunk][...], preferred_element_type=f32)
    result_ref[...] = total.astype(bf16)


def weight_sums(lefts, rights, order, columns, first, before=()):
    chunks = len(lefts)
    rows, features = lefts[0].shape
    if len(rights) == chunks:
        tile = min(512, rights[0].shape[1])
        steps = rights[0].shape[1] // tile
        right_specs = [pl.BlockSpec((rows, tile), lambda c: (0, c))] * chunks
    else:
        steps, _, tile = rights[0].shape
        right_specs = [pl.BlockSpec((None, rows, tile), lambda c, k=k: (c, k, 0)) for k in range(chunks)]
        rights = rights * chunks
    return pl.pallas_call(
        lambda *refs: weight_kernel(order, chunks, *refs),
        grid=(steps,),
        in_specs=[pl.BlockSpec((rows, features), lambda c: (0, 0))] * chunks
        + right_specs
        + [pl.BlockSpec(memory_space=pl.ANY)] * len(before),
        out_specs=pl.BlockSpec((features, tile), lambda c: (0, c + first // tile)),
        out_shape=jax.ShapeDtypeStruct((features, columns), bf16),
        input_output_aliases={2 * chunks: 0} if before else {},
        scratch_shapes=[pltpu.VMEM((features, rows * chunks), bf16)],
        compiler_params=pltpu.CompilerParams(vmem_limit_bytes=VMEM_LIMIT),
        cost_estimate=cost(2 * steps + 1),
        name="weight_sums",
    )(*lefts, *rights, *before)


def middle_kernel(part_ref, other_ref, middle_ref, cot_ref, norm_ref, weight_ref, grad_ref, branch_ref, context_ref, sums_ref):
    grad = part_ref[...].astype(f32) + other_ref[...].astype(f32)
    rows, inverse = unit(middle_ref[...])
    grad_unit = grad * norm_ref[2:3, :]
    first_mean = jnp.mean(grad_unit, axis=-1, keepdims=True)
    second_mean = jnp.mean(grad_unit * rows, axis=-1, keepdims=True)
    whole = cot_ref[...].astype(f32) + inverse * (grad_unit - first_mean - rows * second_mean)
    grad_ref[...] = whole
    branch_ref[...] = whole.astype(bf16)
    context_ref[...] = jnp.dot(branch_ref[...], weight_ref[...], preferred_element_type=f32).astype(bf16)
    gain = jnp.sum(grad * rows, axis=0, keepdims=True)
    shift = jnp.sum(grad, axis=0, keepdims=True)

    @pl.when(pl.program_id(0) == 0)
    def _():
        sums_ref[0:1, :] = gain
        sums_ref[1:2, :] = shift

    @pl.when(pl.program_id(0) > 0)
    def _():
        sums_ref[0:1, :] += gain
        sums_ref[1:2, :] += shift


def middle_back(part, other, middle, cot_rows, norm_params, weights_out):
    rows, width = part.shape
    block = min(256, rows)
    columns = weights_out.shape[1]
    piece = pl.BlockSpec((block, width), lambda r: (r, 0))
    return pl.pallas_call(
        middle_kernel,
        grid=(rows // block,),
        in_specs=[
            piece,
            piece,
            piece,
            piece,
            pl.BlockSpec(norm_params.shape, lambda r: (0, 0)),
            pl.BlockSpec(weights_out.shape, lambda r: (0, 0)),
        ],
        out_specs=[piece, piece, pl.BlockSpec((block, columns), lambda r: (r, 0)), pl.BlockSpec((2, width), lambda r: (0, 0))],
        out_shape=[
            jax.ShapeDtypeStruct((rows, width), f32),
            jax.ShapeDtypeStruct((rows, width), bf16),
            jax.ShapeDtypeStruct((rows, columns), bf16),
            jax.ShapeDtypeStruct((2, width), f32),
        ],
        compiler_params=pltpu.CompilerParams(vmem_limit_bytes=VMEM_LIMIT),
        cost_estimate=cost(6),
        name="middle_back",
    )(part, other, middle, cot_rows, norm_params, weights_out)


def first_kernel(place_ref, grads_ref, weight_ref, x_ref, part_ref, sums_ref):
    left = jnp.concatenate([grads_ref[t] for t in range(3)], axis=1)
    right = jnp.concatenate([weight_ref[t] for t in range(3)], axis=1)
    part = lax.dot_general(left, right, ROWS_BY_ROWS, preferred_element_type=f32)
    part_ref[...] = part.astype(bf16)
    sums_ref[0:1, :] = jnp.sum(part * unit(x_ref[...].astype(f32))[0], axis=0, keepdims=True)
    sums_ref[1:2, :] = jnp.sum(part, axis=0, keepdims=True)


def first_back(grads, weights_qkv, x_rows, first_row):
    rows, width = x_rows.shape
    columns = grads.shape[2]
    return pl.pallas_call(
        first_kernel,
        grid_spec=pltpu.PrefetchScalarGridSpec(
            num_scalar_prefetch=1,
            grid=(1,),
            in_specs=[
                pl.BlockSpec((3, rows, columns), lambda r, place: (0, place[0], 0)),
                pl.BlockSpec(weights_qkv.shape, lambda r, place: (0, 0, 0)),
                pl.BlockSpec((rows, width), lambda r, place: (0, 0)),
            ],
            out_specs=[pl.BlockSpec((rows, width), lambda r, place: (0, 0)), pl.BlockSpec((2, width), lambda r, place: (0, 0))],
        ),
        out_shape=[jax.ShapeDtypeStruct((rows, width), bf16), jax.ShapeDtypeStruct((2, width), f32)],
        compiler_params=pltpu.CompilerParams(vmem_limit_bytes=VMEM_LIMIT),
        cost_estimate=cost(6),
        name="first_back",
    )(jnp.reshape(first_row // rows, (1,)), grads, weights_qkv, x_rows)


def project_kernel(chunks, *refs):
    xs, (norm_ref, weight_ref), normed_refs, result_ref = refs[:chunks], refs[chunks:][:2], refs[chunks + 2 : -1], refs[-1]
    rows = xs[0].shape[0]
    block = min(256, rows)
    for chunk in range(chunks):
        for first in range(0, rows, block):
            at = pl.ds(first, block)
            values = xs[chunk][at, :].astype(f32)
            normed = (unit(values)[0] * norm_ref[0:1, :] + norm_ref[1:2, :]).astype(bf16)
            normed_refs[chunk][at, :] = normed
            for t in range(3):
                product = jnp.dot(normed, weight_ref[t], preferred_element_type=f32)
                result_ref[t, pl.ds(chunk * rows + first, block), :] = product.astype(bf16)


def project(x_rows, norm_params, weights_qkv):
    chunks = len(x_rows)
    rows, width = x_rows[0].shape
    columns = weights_qkv.shape[2]
    *normed, result = pl.pallas_call(
        lambda *refs: project_kernel(chunks, *refs),
        out_shape=[jax.ShapeDtypeStruct((rows, width), bf16)] * chunks
        + [jax.ShapeDtypeStruct((3, rows * chunks, columns), bf16)],
        compiler_params=pltpu.CompilerParams(vmem_limit_bytes=VMEM_LIMIT),
        cost_estimate=cost(8),
        name="project",
    )(*x_rows, norm_params, weights_qkv)
    return (normed, result)


def updated(weight, momentum, average, gradient, step_rate):
    next_moment = momentum_keep * momentum + gradient
    next_weight = weight - step_rate * (gradient + momentum_keep * next_moment)
    next_average = average_keep * average + (1.0 - average_keep) * next_weight
    return (gradient, next_moment, next_weight, next_average)


def update_kernel(counts, rates, place_ref, grad_ref, *refs):
    states, results = refs[: 3 * len(counts)], refs[3 * len(counts) :]
    block = 0
    for i, (count, rate) in enumerate(zip(counts, rates)):
        state, result = states[3 * i : 3 * i + 3], results[4 * i : 4 * i + 4]
        width = state[0].shape[-1]
        for t in range(count):
            at = (t,) if len(state[0].shape) == 3 else ()
            gradient = grad_ref[:, block * width : (block + 1) * width].astype(f32)
            block += 1
            for ref, value in zip(result, updated(*[ref[at + (Ellipsis,)] for ref in state], gradient, rate)):
                ref[at + (Ellipsis,)] = value


def update(gradient, states, place, rates):
    counts, in_specs, out_specs, out_shape = [], [], [], []
    for _, momentum, _ in states:
        shape = momentum.shape
        counts.append(shape[0] if len(shape) == 3 else 1)
        if len(shape) == 3:
            share = pl.BlockSpec(shape, lambda i, place: (0, 0, 0))
            in_specs += [pl.BlockSpec(shape, lambda i, place: (0, place[0], 0)), share, share]
        else:
            share = pl.BlockSpec(shape, lambda i, place: (0, 0))
            in_specs += [pl.BlockSpec(shape, lambda i, place: (place[0], 0)), share, share]
        out_specs += [share] * 4
        out_shape += [jax.ShapeDtypeStruct(shape, f32)] * 4
    return pl.pallas_call(
        lambda *refs: update_kernel(counts, rates, *refs),
        grid_spec=pltpu.PrefetchScalarGridSpec(
            num_scalar_prefetch=1,
            grid=(1,),
            in_specs=[pl.BlockSpec(gradient.shape, lambda i, place: (0, 0))] + in_specs,
            out_specs=out_specs,
        ),
        out_shape=out_shape,
        compiler_params=pltpu.CompilerParams(vmem_limit_bytes=VMEM_LIMIT),
        cost_estimate=cost(4),
        name="update",
    )(place, gradient, *[x for state in states for x in state])


def pack_kernel(shares, counts, head_ref, buckets_ref, *refs):
    result_ref = refs[-1]
    one, two, diagonals = refs[: counts[0]], refs[counts[0] : sum(counts[:2])], refs[sum(counts[:2]) : -1]
    norms = [sum(ref[...] for ref in one), sum(ref[...] for ref in two) * (1.0 / shares)]
    rows = jnp.concatenate(norms, axis=0)
    for i in range(rows.shape[1] // 128):
        result_ref[4 * i : 4 * i + 4, :] = rows[:, 128 * i : 128 * i + 128]
    offsets = sum(ref[:, 0, :] for ref in diagonals)
    first = rows.shape[1] // 32
    heads = result_ref.shape[0] - first
    bins = lax.broadcasted_iota(jnp.int32, (128, offsets.shape[1]), 0)
    hits = (buckets_ref[...] == bins).astype(f32)
    sums = lax.dot_general(offsets, hits, ROWS_BY_ROWS, precision=highest, preferred_element_type=f32)
    if sums.shape[0] < heads:
        sums = jnp.concatenate([sums, jnp.zeros((heads - sums.shape[0], 128), f32)], axis=0)
    result_ref[first:, :] = pltpu.roll(sums, head_ref[0], 0)


def pack_small(one, two, diagonals, buckets, heads, head_first, shares):
    width = one[0].shape[1]
    return pl.pallas_call(
        lambda *refs: pack_kernel(shares, (len(one), len(two)), *refs),
        in_specs=[pl.BlockSpec(memory_space=pltpu.SMEM)]
        + [pl.BlockSpec(memory_space=pltpu.VMEM)] * (1 + len(one) + len(two) + len(diagonals)),
        out_shape=jax.ShapeDtypeStruct((width // 32 + heads, 128), f32),
        cost_estimate=cost(2),
        name="pack_small",
    )(jnp.reshape(head_first, (1,)), buckets, *one, *two, *diagonals)


def small_update_kernel(rate, small_ref, *refs):
    norm_state, bias_state, results = refs[:3], refs[3:6], refs[6:]
    width = norm_state[0].shape[1]
    gradient = jnp.concatenate([small_ref[4 * i : 4 * i + 4, :] for i in range(width // 128)], axis=1)
    for result, value in zip(results[:4], updated(*[ref[...] for ref in norm_state], gradient, rate)):
        result[...] = value
    gradient = small_ref[width // 32 :, : bias_state[0].shape[1]]
    for result, value in zip(results[4:], updated(*[ref[...] for ref in bias_state], gradient, rate)):
        result[...] = value


def small_update(small, norm_state, bias_state, rate):
    return pl.pallas_call(
        lambda *refs: small_update_kernel(rate, *refs),
        out_shape=[jax.ShapeDtypeStruct(norm_state[0].shape, f32)] * 4
        + [jax.ShapeDtypeStruct(bias_state[0].shape, f32)] * 4,
        cost_estimate=cost(1.5),
        name="small_update",
    )(small, *norm_state, *bias_state)


def finish_kernel(place_ref, x_ref, norm_ref, sent_ref, kept_ref, first_ref, second_ref, result_ref):
    chosen = jnp.where(place_ref[0] == 0, first_ref[...], second_ref[...])
    grad = sent_ref[...].astype(f32) + kept_ref[...].astype(f32)
    rows, inverse = unit(x_ref[...].astype(f32))
    grad_unit = grad * norm_ref[0:1, :]
    first_mean = jnp.mean(grad_unit, axis=-1, keepdims=True)
    second_mean = jnp.mean(grad_unit * rows, axis=-1, keepdims=True)
    result_ref[...] = chosen + inverse * (grad_unit - first_mean - rows * second_mean)


def finish(got, kept, x_rows, norm_params, middle_grad, place):
    rows, width = x_rows.shape
    piece = pl.BlockSpec((rows // 2, width), lambda r, place: (r, 0))
    chosen = [
        pl.BlockSpec((rows // 2, width), lambda r, place: (jnp.where(place[0] == 0, r, 0), 0)),
        pl.BlockSpec((rows // 2, width), lambda r, place: (jnp.where(place[0] == 0, 0, r), 0)),
    ]
    return pl.pallas_call(
        finish_kernel,
        grid_spec=pltpu.PrefetchScalarGridSpec(
            num_scalar_prefetch=1,
            grid=(2,),
            in_specs=[piece, pl.BlockSpec(norm_params.shape, lambda r, place: (0, 0)), piece, piece] + chosen,
            out_specs=piece,
        ),
        out_shape=jax.ShapeDtypeStruct((rows, width), f32),
        compiler_params=pltpu.CompilerParams(vmem_limit_bytes=VMEM_LIMIT),
        cost_estimate=cost(5),
        name="finish",
    )(place, x_rows, norm_params, got, kept, *middle_grad)


def after(value, *others):
    return lax.optimization_barrier((value,) + others)[0]


def swap(values, axis, bit):
    size = lax.axis_size(axis)
    return lax.ppermute(values, axis, [(i, i ^ bit) for i in range(size)])


def in_order(own, other):
    first = lax.axis_index("mp") == 0
    return [jnp.where(first, own, other), jnp.where(first, other, own)]


def other_part(rows):
    if lax.axis_size("mp") != 2:
        return (lax.psum(rows.astype(f32), "mp") - rows.astype(f32)).astype(bf16)
    return swap(rows, "mp", 1)


def sum_own(sent, kept):
    return kept.astype(f32) + swap(sent, "mp", 1).astype(f32)


def sum_over_clips(gradient, order):
    return lax.psum_scatter(gradient, "dp", scatter_dimension=0, tiled=True, axis_index_groups=[order])


def per_device(
    inputs,
    cotangent,
    lengths,
    buckets,
    w_qkv,
    w_out,
    w_ffn,
    norm_params,
    rel_bias,
    momentum_qkv,
    momentum_out,
    momentum_ffn,
    momentum_norms,
    momentum_bias,
    average_qkv,
    average_out,
    average_ffn,
    average_norms,
    average_bias,
):
    model_size = lax.axis_size("mp")
    data_size = lax.axis_size("dp")
    rows_local = inputs.shape[0]
    seq_len = rows_local * model_size
    width_local = w_qkv.shape[2]
    heads_local = width_local // HD
    head_first = lax.axis_index("mp") * heads_local
    own_first = lax.axis_index("mp") * rows_local
    share_rows = momentum_out.shape[0]
    chunks = 2
    chunk_rows = seq_len // chunks

    def chunk_of(rows, chunk):
        return lax.slice_in_dim(rows, chunk * chunk_rows, (chunk + 1) * chunk_rows, axis=0)

    if model_size == 2:
        inputs_other = swap(inputs, "mp", 1)
        cot_other = swap(after(cotangent, inputs_other), "mp", 1)
        x_rows = in_order(inputs, inputs_other)
        cot_rows = in_order(cotangent, cot_other)
    else:
        inputs_all = lax.all_gather(inputs, "mp", axis=0, tiled=True)
        cot_other = lax.all_gather(cotangent, "mp", axis=0, tiled=True)
        x_rows = [chunk_of(inputs_all, chunk) for chunk in range(chunks)]
        cot_rows = [chunk_of(cot_other, chunk) for chunk in range(chunks)]
    weights_qkv = w_qkv.astype(bf16)
    weights_out = w_out.astype(bf16)

    bias_local = lax.dynamic_slice_in_dim(rel_bias, head_first, heads_local, 1)
    bucket_hits = (buckets[:, None] == jnp.arange(rel_bias.shape[0], dtype=jnp.int32)[None, :]).astype(f32)
    bias_table = jnp.dot(bucket_hits, bias_local, precision=highest).T
    skew, skew_back = skew_tables(bias_table)

    normed_one, projected = project(x_rows, norm_params, weights_qkv)

    context, totals, branch = [], [], []
    ahead = projected
    for chunk in range(chunks):
        part, total, sent = attend(ahead, lengths, skew, weights_out, chunk, chunks)
        context.append(part)
        totals.append(total)
        branch.append(sent)
        ahead = after(ahead, sent, *cot_rows)
    branch_other = []
    for sent in branch:
        branch_other.append(other_part(after(sent, *branch_other[-1:])))

    ffn = []
    ahead = after(w_ffn, branch[-1])
    for chunk in range(chunks):
        ffn.append(
            feed_forward(
                x_rows[chunk], branch[chunk], branch_other[chunk], cot_rows[chunk], norm_params, ahead
            )
        )
        ahead = after(ahead, ffn[-1][4])
    middle, normed_two, hidden, pre_grad, two_part, out_part = zip(*ffn)
    two_other = [other_part(after(two_part[0], branch_other[-1]))]
    order = ring_order(data_size)
    units = w_ffn.shape[2]
    ffn_grad = weight_sums(normed_two, pre_grad, order, 2 * units, 0)
    ffn_grad, sent, _ = lax.optimization_barrier((ffn_grad, two_part[1], two_other[0]))
    two_other.append(other_part(sent))
    ffn_grad = weight_sums(cot_rows, hidden, order, 2 * units, units, [ffn_grad])
    ffn_share = sum_over_clips(ffn_grad, order)

    if model_size == 2:
        out_kept, out_sent = in_order(*out_part)
    else:
        out_got = lax.psum_scatter(jnp.concatenate(out_part), "mp", scatter_dimension=0, tiled=True)
    middle_grad, branch_grad, context_grad = [], [], []

    def middle_step(chunk, *others):
        whole, sent, grad, sums = middle_back(
            after(two_part[chunk], *others), two_other[chunk], middle[chunk], cot_rows[chunk], norm_params, weights_out
        )
        middle_grad.append(whole)
        branch_grad.append(sent)
        context_grad.append(grad)
        return sums

    def back(chunk, others, before=()):
        grad = after(context_grad[chunk], *others)
        return attend_back(projected, grad, context[chunk], totals[chunk], lengths, skew_back, chunk, chunks, before)

    sums_two = [middle_step(0, ffn_grad)]
    *before, diagonal = back(0, [])
    diagonals = [diagonal]
    sums_two.append(middle_step(1, diagonal))
    if model_size == 2:
        out_got = swap(after(out_sent, sums_two[-1]), "mp", 1)
    attention_grad = weight_sums(branch_grad, context, order, 4 * width_local, 3 * width_local)
    grads, diagonal = back(1, [attention_grad], before)
    diagonals.append(diagonal)
    attention_grad = weight_sums(normed_one, [after(grads, out_got)], order, 4 * width_local, 0, [attention_grad])
    attention_share = sum_over_clips(after(attention_grad, ffn_share), order)
    grads = after(grads, attention_grad)

    one = jnp.reshape(own_first * 0, (1,))
    place = one + lax.axis_index("dp")
    scale_factor = 1.0 / math.sqrt(float(seq_len * data_size))
    if model_size == 2:
        sent, sums_sent = first_back(grads, weights_qkv, inputs_other, rows_local - own_first)
        got = swap(sent, "mp", 1)
        kept, sums_kept = first_back(after(grads, sent), weights_qkv, inputs, own_first)
        sums_one = [sums_sent, sums_kept]
        own = one + lax.axis_index("mp")
        output_rows = in_order(*[after(rows, kept) for rows in middle])[0] + out_kept.astype(f32) + out_got.astype(f32)
    else:
        sent, sums_sent = first_back(grads, weights_qkv, jnp.concatenate(x_rows), own_first * 0)
        sums_one = [sums_sent]
        kept = lax.psum_scatter(sent, "mp", scatter_dimension=0, tiled=True)
        got = jnp.zeros_like(kept)
        own = one
        middle_grad = [lax.dynamic_slice_in_dim(jnp.concatenate(middle_grad), own_first, rows_local, 0)] * 2
        middle_own = lax.dynamic_slice_in_dim(jnp.concatenate(middle), own_first, rows_local, 0)
        output_rows = middle_own + out_got.astype(f32)
    output = output_rows.astype(bf16)

    reversed_buckets = jnp.pad(buckets[::-1], (0, 1), constant_values=-1)[None, :]
    small = pack_small(sums_one, sums_two, diagonals, reversed_buckets, rel_bias.shape[1], head_first, model_size)
    for axis in ("dp", "mp"):
        bit = 1
        while bit < lax.axis_size(axis):
            small = small + swap(small, axis, bit)
            bit *= 2
    ffn_results = update(
        after(ffn_share, kept), [(w_ffn, momentum_ffn, average_ffn)], place, [0.05 * scale_factor]
    )
    attention_results = update(
        attention_share,
        [(w_qkv, momentum_qkv, average_qkv), (w_out, momentum_out, average_out)],
        place,
        [0.3 * scale_factor, 0.1 * scale_factor],
    )
    input_grad = finish(got, kept, inputs, norm_params, middle_grad, own)
    small_results = small_update(
        small,
        (norm_params, momentum_norms, average_norms),
        (rel_bias.T, momentum_bias.T, average_bias.T),
        0.05 * scale_factor,
    )
    small_results = [*small_results[:4], *[result.T for result in small_results[4:]]]
    return (output, input_grad, *attention_results, *ffn_results, *small_results)


def solution(mesh):
    return jax.shard_map(
        per_device,
        mesh=mesh,
        in_specs=(
            P(("dp", "mp"), None),
            P(("dp", "mp"), None),
            P("dp"),
            P(),
            P(None, None, "mp"),
            P(None, "mp"),
            P(None, None, "mp"),
            P(),
            P(),
            P(None, "dp", "mp"),
            P("dp", "mp"),
            P(None, "dp", "mp"),
            P(),
            P(),
            P(None, "dp", "mp"),
            P("dp", "mp"),
            P(None, "dp", "mp"),
            P(),
            P(),
        ),
        out_specs=(
            P(("dp", "mp"), None),
            P(("dp", "mp"), None),
            P(None, "dp", "mp"),
            P(None, "dp", "mp"),
            P(None, "dp", "mp"),
            P(None, "dp", "mp"),
            P("dp", "mp"),
            P("dp", "mp"),
            P("dp", "mp"),
            P("dp", "mp"),
            P(None, "dp", "mp"),
            P(None, "dp", "mp"),
            P(None, "dp", "mp"),
            P(None, "dp", "mp"),
            P(),
            P(),
            P(),
            P(),
            P(),
            P(),
            P(),
            P(),
        ),
        check_vma=False,
    )
```

```python
import math

import jax
import jax.numpy as jnp
from jax import lax
from jax.experimental import pallas as pl
from jax.experimental.pallas import tpu as pltpu
from jax.sharding import PartitionSpec as P

HD = 64
PAIR = 2 * HD
QB = 128
QUERY_BLOCK = 512
KEY_BLOCK = 512
f32 = jnp.float32
bf16 = jnp.bfloat16
ROWS_BY_ROWS = (((1,), (1,)), ((), ()))
COLS_BY_COLS = (((0,), (0,)), ((), ()))
VMEM_LIMIT = 56 * 2**20

highest = lax.Precision.HIGHEST
momentum_keep = 0.5
average_keep = 0.5
SHARE = 1.1e6


def cost(microseconds):
    return pl.CostEstimate(flops=0, bytes_accessed=int(SHARE * microseconds), transcendentals=0)


def in_hbm(*values):
    values = [pltpu.with_memory_space_constraint(value, pltpu.HBM) for value in values]
    return values if len(values) > 1 else values[0]


def skew_kernel(forward_ref, reverse_ref, forward_out, reverse_out):
    width = forward_ref.shape[2]
    for source, result in ((forward_ref, forward_out), (reverse_ref, reverse_out)):
        rows = jnp.broadcast_to(source[0], (QB, width))
        result[0] = pltpu.roll(rows, width - (QB - 1), 1, stride=1, stride_axis=0)[:, : width - QB]


def skew_tables(table):
    heads, width = table.shape
    forward = jnp.pad(table, ((0, 0), (0, 1)))[:, None, :]
    reverse = jnp.pad(table[:, ::-1], ((0, 0), (0, 1)))[:, None, :]
    width += 1
    row = pl.BlockSpec((1, 1, width), lambda h: (h, 0, 0))
    skewed = pl.BlockSpec((1, QB, width - QB), lambda h: (h, 0, 0))
    shape = jax.ShapeDtypeStruct((heads, QB, width - QB), f32)
    return pl.pallas_call(
        skew_kernel,
        grid=(heads,),
        in_specs=[row, row],
        out_specs=[skewed, skewed],
        out_shape=[shape, shape],
        cost_estimate=cost(8),
        name="skew",
    )(forward, reverse)


def three_parts(values):
    first = values.astype(bf16).astype(f32)
    rest = values - first
    second = rest.astype(bf16).astype(f32)
    return (first, second, rest - second)


def own_lanes(lane, head):
    return (lane >= HD) if head else (lane < HD)


def key_side(keys, mask, lane, head):
    first = 0 if head else HD
    extra = jnp.where(lane == first, mask, jnp.where((lane > first) & (lane < first + 4), 1.0, 0.0))
    return jnp.where(own_lanes(lane, head), keys, extra).astype(bf16)


def forward_kernel(
    first_row,
    length_ref,
    q_ref,
    k_ref,
    v_ref,
    skew_ref,
    weight_ref,
    context_ref,
    total_ref,
    branch_ref,
    key_ref,
    value_ref,
    raised_ref,
    gathered_ref,
):
    seq_len = k_ref.shape[0]
    rows_here = q_ref.shape[0]
    lane = lax.broadcasted_iota(jnp.int32, (seq_len, PAIR), 1)
    place = lax.broadcasted_iota(jnp.int32, (seq_len, PAIR), 0)
    mask = jnp.where(place < length_ref[0], 0.0, -1e9)
    keys = k_ref[...].astype(f32)
    values = v_ref[...].astype(f32)
    for head in range(2):
        key_ref[head] = key_side(keys, mask, lane, head)
        value_ref[head] = jnp.where(own_lanes(lane, head), values, 1.0).astype(bf16)
    here = min(QUERY_BLOCK, rows_here)
    lane = lax.broadcasted_iota(jnp.int32, (here, PAIR), 1)

    def block(index, carry):
        rows = pl.ds(pl.multiple_of(index * here, here), here)
        queries = q_ref[rows, :].astype(f32) * 0.125
        context = []
        totals = []
        for head in range(2):
            own = own_lanes(lane, head)
            first = 0 if head else HD
            query = jnp.where(own, queries, jnp.where(lane == first, 1.0, 0.0)).astype(bf16)
            scores = lax.dot_general(query, key_ref[head], ROWS_BY_ROWS, preferred_element_type=f32)
            tops = []
            for piece in range(0, here, QB):
                start = pl.multiple_of(seq_len - QB - first_row - index * here - piece, QB)
                moved = scores[piece : piece + QB] + skew_ref[head, :, pl.ds(start, seq_len)]
                top = jnp.max(moved, axis=1, keepdims=True)
                raised_ref[head, piece : piece + QB, :] = jnp.exp(moved - top).astype(bf16)
                tops.append(top)
            weighted = jnp.dot(raised_ref[head], value_ref[head], preferred_element_type=f32)
            context.append(weighted / weighted[:, first : first + 1])
            totals.append(jnp.concatenate(tops, axis=0) + jnp.log(jnp.where(own, 1.0, weighted)))
        context_ref[rows, :] = jnp.where(lane < HD, context[0], context[1]).astype(bf16)
        total_ref[rows, :] = jnp.where(lane < HD, totals[1], totals[0])
        return carry

    lax.fori_loop(0, rows_here // here, block, 0, unroll=True)
    step = pl.program_id(0)
    gathered_ref[step] = context_ref[...]

    @pl.when(step == pl.num_programs(0) - 1)
    def _():
        gathered = jnp.concatenate([gathered_ref[p] for p in range(gathered_ref.shape[0])], axis=1)
        branch_ref[...] = lax.dot_general(gathered, weight_ref[...], ROWS_BY_ROWS, preferred_element_type=f32).astype(bf16)


def attend(projected, lengths, skew, weights_out, chunk, chunks):
    _, seq_len, width = projected.shape
    features = weights_out.shape[0]
    rows_here = seq_len // chunks
    whole = [pl.BlockSpec((None, seq_len, PAIR), lambda p, t=t: (t, 0, p)) for t in (1, 2)]
    part = pl.BlockSpec((rows_here, PAIR), lambda p: (0, p))
    return pl.pallas_call(
        lambda *refs: forward_kernel(chunk * rows_here, *refs),
        grid=(width // PAIR,),
        in_specs=[
            pl.BlockSpec(memory_space=pltpu.SMEM),
            pl.BlockSpec((None, rows_here, PAIR), lambda p: (0, chunk, p)),
            *whole,
            pl.BlockSpec((2,) + skew.shape[1:], lambda p: (p, 0, 0)),
            pl.BlockSpec(weights_out.shape, lambda p: (0, 0)),
        ],
        out_specs=[part, part, pl.BlockSpec((rows_here, features), lambda p: (0, 0))],
        out_shape=[
            jax.ShapeDtypeStruct((rows_here, width), bf16),
            jax.ShapeDtypeStruct((rows_here, width), f32),
            jax.ShapeDtypeStruct((rows_here, features), bf16),
        ],
        scratch_shapes=[
            pltpu.VMEM((2, seq_len, PAIR), bf16),
            pltpu.VMEM((2, seq_len, PAIR), bf16),
            pltpu.VMEM((2, min(QUERY_BLOCK, rows_here), seq_len), bf16),
            pltpu.VMEM((width // PAIR, rows_here, PAIR), bf16),
        ],
        compiler_params=pltpu.CompilerParams(vmem_limit_bytes=24 * 2**20),
        cost_estimate=cost(13),
        name="attend",
    )(lengths, projected, projected, projected, in_hbm(skew), weights_out)


def diagonal_sums(skewed):
    width = skewed.shape[1]
    total = pltpu.roll(skewed[:8], QB - 1, 1)
    for group in range(1, QB // 8):
        total = total + pltpu.roll(skewed[8 * group : 8 * group + 8], QB - 1 - 8 * group, 1)
    row = lax.broadcasted_iota(jnp.int32, total.shape, 0)
    for bit in (1, 2, 4):
        total = jnp.where((row & bit) != 0, pltpu.roll(total, width - bit, 1), total)
    return jnp.sum(total, axis=0, keepdims=True)


def backward_kernel(first_row, last, *refs):
    (length_ref, q_ref, k_ref, v_ref, grad_ref, context_ref, total_ref, skew_ref) = refs[:8]
    running = last and first_row > 0
    if running:
        dq_before, dk_before, dv_before = refs[8:11]
    if last:
        grads_ref, diagonal_ref = refs[-8:-6]
        dq_ref = grads_ref.at[0, pl.ds(first_row, q_ref.shape[0]), :]
        dk_ref, dv_ref = grads_ref.at[1], grads_ref.at[2]
    else:
        dq_ref, dk_ref, dv_ref, diagonal_ref = refs[-10:-6]
    (query_ref, back_ref, skewed_ref, dq_sum, soft_ref, slope_ref) = refs[-6:]
    if running:
        grads_ref[0, :first_row, :] = dq_before[...]
    seq_len = k_ref.shape[0]
    rows_here = q_ref.shape[0]
    lane = lax.broadcasted_iota(jnp.int32, (rows_here, PAIR), 1)
    queries = q_ref[...].astype(f32) * 0.125
    back = grad_ref[...].astype(f32)
    dots = back * context_ref[...].astype(f32)
    first_lane = lax.broadcasted_iota(jnp.int32, (PAIR, PAIR), 0) // HD
    cross = jnp.where(first_lane != lax.broadcasted_iota(jnp.int32, (PAIR, PAIR), 1) // HD, 1.0, 0.0).astype(bf16)
    row_dot = sum(jnp.dot(part.astype(bf16), cross, preferred_element_type=f32) for part in three_parts(dots)[:2])
    tops = three_parts(-total_ref[...])
    drops = three_parts(-row_dot)
    for head in range(2):
        own = own_lanes(lane, head)
        first = 0 if head else HD
        query = jnp.where(lane == first, 1.0, 0.0)
        graded = jnp.zeros_like(query)
        for i in range(3):
            query = jnp.where(lane == first + 1 + i, tops[i], query)
            graded = jnp.where(lane == first + 1 + i, drops[i], graded)
        query_ref[head] = jnp.where(own, queries, query).astype(bf16)
        back_ref[head] = jnp.where(own, back, graded).astype(bf16)
    skewed_ref[...] = jnp.zeros_like(skewed_ref)
    keys_here = soft_ref.shape[1]
    small_lane = lax.broadcasted_iota(jnp.int32, (keys_here, PAIR), 1)
    small_row = lax.broadcasted_iota(jnp.int32, (keys_here, PAIR), 0)

    def block(index, carry):
        rows = pl.ds(pl.multiple_of(index * keys_here, keys_here), keys_here)
        keys = k_ref[rows, :].astype(f32)
        values = v_ref[rows, :].astype(f32)
        mask = jnp.where(small_row + index * keys_here < length_ref[0], 0.0, -1e9)
        dq, dk, dv = [], [], []
        for head in range(2):
            key = key_side(keys, mask, small_lane, head)
            value = key_side(values, 0.0, small_lane, head)
            scores = lax.dot_general(key, query_ref[head], ROWS_BY_ROWS, preferred_element_type=f32)
            drop = lax.dot_general(value, back_ref[head], ROWS_BY_ROWS, preferred_element_type=f32)
            for first in range(0, keys_here, QB):
                piece = slice(first, first + QB)
                start = pl.multiple_of(seq_len - QB + first_row - index * keys_here - first, QB)
                soft = jnp.exp(scores[piece] + skew_ref[head, :, pl.ds(start, rows_here)])
                score_grad = soft * drop[piece]
                skewed_ref[head, :, pl.ds(start, rows_here)] += score_grad
                soft_ref[head, piece, :] = soft.astype(bf16)
                slope_ref[head, piece, :] = score_grad.astype(bf16)
            dv.append(jnp.dot(soft_ref[head], back_ref[head], preferred_element_type=f32))
            dk.append(jnp.dot(slope_ref[head], query_ref[head], preferred_element_type=f32))
            dq.append(lax.dot_general(slope_ref[head], key, COLS_BY_COLS, preferred_element_type=f32))
        dk = jnp.where(small_lane < HD, dk[0], dk[1])
        dv = jnp.where(small_lane < HD, dv[0], dv[1])
        if running:
            dk = dk + dk_before[rows, :]
            dv = dv + dv_before[rows, :]
        dk_ref[rows, :] = dk.astype(dk_ref.dtype)
        dv_ref[rows, :] = dv.astype(dv_ref.dtype)
        dq = jnp.where(lane < HD, dq[0], dq[1])

        @pl.when(index == 0)
        def _():
            dq_sum[...] = dq

        @pl.when(index > 0)
        def _():
            dq_sum[...] += dq

        return carry

    lax.fori_loop(0, seq_len // keys_here, block, 0, unroll=True)
    dq_ref[...] = (dq_sum[...] * 0.125).astype(bf16)
    for head in range(2):
        diagonal_ref[head] = diagonal_sums(jnp.concatenate([skewed_ref[head], jnp.zeros((QB, QB), f32)], axis=1))


def attend_back(projected, context_grad, context, totals, lengths, skew, chunk, chunks, before=()):
    _, seq_len, width = projected.shape
    pairs = width // PAIR
    rows_here = seq_len // chunks
    key_block = min(KEY_BLOCK, seq_len)
    skew_width = skew.shape[2]
    whole = [pl.BlockSpec((None, seq_len, PAIR), lambda p, t=t: (t, 0, p)) for t in (1, 2)]
    part = pl.BlockSpec((rows_here, PAIR), lambda p: (0, p))
    full = pl.BlockSpec((seq_len, PAIR), lambda p: (0, p))
    last = chunk == chunks - 1
    if last:
        out_specs = [pl.BlockSpec((3, seq_len, PAIR), lambda p: (0, 0, p))]
        out_shape = [pltpu.HBM((3, seq_len, width), bf16)]
    else:
        out_specs = [part, full, full]
        out_shape = [jax.ShapeDtypeStruct((rows_here, width), bf16)] + [jax.ShapeDtypeStruct((seq_len, width), f32)] * 2
    return pl.pallas_call(
        lambda *refs: backward_kernel(chunk * rows_here, last, *refs),
        grid=(pairs,),
        in_specs=[
            pl.BlockSpec(memory_space=pltpu.SMEM),
            pl.BlockSpec((None, rows_here, PAIR), lambda p: (0, chunk, p)),
            *whole,
            part,
            part,
            part,
            pl.BlockSpec((2, QB, skew_width), lambda p: (p, 0, 0)),
            *[part, full, full][: len(before)],
        ],
        out_specs=out_specs + [pl.BlockSpec((2, 1, skew_width + QB), lambda p: (p, 0, 0))],
        out_shape=out_shape + [jax.ShapeDtypeStruct((width // HD, 1, skew_width + QB), f32)],
        scratch_shapes=[
            pltpu.VMEM((2, rows_here, PAIR), bf16),
            pltpu.VMEM((2, rows_here, PAIR), bf16),
            pltpu.VMEM((2, QB, skew_width), f32),
            pltpu.VMEM((rows_here, PAIR), f32),
            pltpu.VMEM((2, key_block, rows_here), bf16),
            pltpu.VMEM((2, key_block, rows_here), bf16),
        ],
        compiler_params=pltpu.CompilerParams(vmem_limit_bytes=28 * 2**20),
        cost_estimate=cost(18),
        name="attend_back",
    )(lengths, *in_hbm(projected, projected, projected, context_grad, context, totals, skew, *before))


def unit(values):
    row_mean = jnp.mean(values, axis=-1, keepdims=True)
    centered = values - row_mean
    spread = jnp.mean(centered * centered, axis=-1, keepdims=True)
    inverse = lax.rsqrt(spread + 1e-05)
    return (centered * inverse, inverse)


def ffn_kernel(x_ref, one_ref, two_ref, cot_ref, norm_ref, up_ref, down_ref, middle_ref, normed_ref, hidden_ref, pre_ref, grad_ref, out_ref, grad_sum, out_sum):
    step = pl.program_id(0)

    @pl.when(step == 0)
    def _():
        middle = x_ref[...].astype(f32) + (one_ref[...].astype(f32) + two_ref[...].astype(f32))
        middle_ref[...] = middle
        normed_ref[...] = (unit(middle)[0] * norm_ref[2:3, :] + norm_ref[3:4, :]).astype(bf16)
        grad_sum[...] = jnp.zeros_like(grad_sum)
        out_sum[...] = jnp.zeros_like(out_sum)

    up = up_ref[...].astype(bf16)
    down = down_ref[...].astype(bf16)
    block = min(512, x_ref.shape[0])
    for first in range(0, x_ref.shape[0], block):
        rows = pl.ds(first, block)
        hidden_pre = jnp.dot(normed_ref[rows, :], up, preferred_element_type=f32)
        hidden_grad = jnp.dot(cot_ref[rows, :], down, preferred_element_type=f32)
        gate = 0.5 + 0.5 * lax.erf(hidden_pre * 0.7071067811865476)
        slope = gate + hidden_pre * (0.3989422804014327 * jnp.exp(-0.5 * hidden_pre * hidden_pre))
        hidden = (hidden_pre * gate).astype(bf16)
        pre_grad = (hidden_grad * slope).astype(bf16)
        hidden_ref[rows, :] = hidden
        pre_ref[rows, :] = pre_grad
        grad_sum[rows, :] += lax.dot_general(pre_grad, up, ROWS_BY_ROWS, preferred_element_type=f32)
        out_sum[rows, :] += lax.dot_general(hidden, down, ROWS_BY_ROWS, preferred_element_type=f32)

    @pl.when(step == pl.num_programs(0) - 1)
    def _():
        grad_ref[...] = grad_sum[...].astype(bf16)
        out_ref[...] = out_sum[...].astype(bf16)


def feed_forward(x_rows, branch_one, branch_two, cot_rows, norm_params, weights_ffn):
    rows, width = x_rows.shape
    units = weights_ffn.shape[2]
    tile = min(512, units)
    whole = pl.BlockSpec((rows, width), lambda f: (0, 0))
    tall = pl.BlockSpec((rows, tile), lambda f: (0, f))
    return pl.pallas_call(
        ffn_kernel,
        grid=(units // tile,),
        in_specs=[
            whole,
            whole,
            whole,
            whole,
            pl.BlockSpec(norm_params.shape, lambda f: (0, 0)),
            pl.BlockSpec((None, width, tile), lambda f: (0, 0, f)),
            pl.BlockSpec((None, width, tile), lambda f: (1, 0, f)),
        ],
        out_specs=[whole, whole, tall, tall, whole, whole],
        out_shape=[
            pltpu.HBM((rows, width), f32),
            jax.ShapeDtypeStruct((rows, width), bf16),
            jax.ShapeDtypeStruct((rows, units), bf16),
            jax.ShapeDtypeStruct((rows, units), bf16),
            jax.ShapeDtypeStruct((rows, width), bf16),
            jax.ShapeDtypeStruct((rows, width), bf16),
        ],
        scratch_shapes=[pltpu.VMEM((rows, width), f32)] * 2,
        compiler_params=pltpu.CompilerParams(vmem_limit_bytes=36 * 2**20),
        cost_estimate=cost(17.5),
        name="feed_forward",
    )(x_rows, branch_one, branch_two, cot_rows, norm_params, weights_ffn, weights_ffn)


def chip_ring(count):
    if count % 4:
        return list(range(count))
    rows, columns = 4, count // 4
    chips = [(row, 0) for row in range(rows)]
    for turn, row in enumerate(range(rows - 1, -1, -1)):
        across = [(row, column) for column in range(1, columns)]
        chips += across[::-1] if turn % 2 else across
    return [row * columns + column for row, column in chips]


def device_ring(size):
    chips = chip_ring(size // 2)
    return [2 * chip + core for turn, chip in enumerate(chips) for core in ((0, 1), (1, 0))[turn % 2]]


def weight_kernel(order, chunks, halves, core_ref, *refs):
    lefts, rights = refs[:chunks], refs[chunks : 2 * chunks]
    results, left_ref = refs[-1 - halves : -1], refs[-1]
    rows, features = lefts[0].shape
    share = features // len(order)
    part = features // halves

    @pl.when(pl.program_id(0) == 0)
    def _():
        for chunk in range(chunks):
            turned = lefts[chunk][...].T
            for position, block in enumerate(order):
                half, first = divmod(position * share, part)
                if halves == 2:
                    half = jnp.where(core_ref[0] == half, 1, 0)
                left_ref[half, first : first + share, chunk * rows : (chunk + 1) * rows] = turned[
                    block * share : (block + 1) * share
                ]

    left = left_ref[...].reshape(features, chunks * rows)
    total = 0.0
    for chunk in range(chunks):
        piece = left[:, chunk * rows : (chunk + 1) * rows]
        total = total + jnp.dot(piece, rights[chunk][...], preferred_element_type=f32)
    for half, result in enumerate(results):
        result[...] = total[half * part : (half + 1) * part].astype(bf16)


def weight_sums(lefts, rights, order, columns, first, before=(), core=None):
    chunks = len(lefts)
    rows, features = lefts[0].shape
    halves = 1 if core is None else 2
    if len(rights) == chunks:
        tile = min(512, rights[0].shape[1])
        steps = rights[0].shape[1] // tile
        right_specs = [pl.BlockSpec((rows, tile), lambda c: (0, c))] * chunks
    else:
        steps, _, tile = rights[0].shape
        right_specs = [pl.BlockSpec((None, rows, tile), lambda c, k=k: (c, k, 0)) for k in range(chunks)]
        rights = rights * chunks
    return pl.pallas_call(
        lambda *refs: weight_kernel(order, chunks, halves, *refs),
        grid=(steps,),
        in_specs=[pl.BlockSpec(memory_space=pltpu.SMEM)]
        + [pl.BlockSpec((rows, features), lambda c: (0, 0))] * chunks
        + right_specs
        + [pl.BlockSpec(memory_space=pl.ANY)] * len(before),
        out_specs=[pl.BlockSpec((features // halves, tile), lambda c: (0, c + first // tile))] * halves,
        out_shape=[pltpu.HBM((features // halves, columns), bf16)] * halves,
        input_output_aliases={1 + 2 * chunks + half: half for half in range(len(before))},
        scratch_shapes=[pltpu.VMEM((halves, features // halves, rows * chunks), bf16)],
        compiler_params=pltpu.CompilerParams(vmem_limit_bytes=20 * 2**20),
        cost_estimate=cost(2 * steps + 1),
        name="weight_sums",
    )(jnp.zeros((1,), jnp.int32) if core is None else core, *lefts, *rights, *before)


def middle_kernel(part_ref, other_ref, middle_ref, cot_ref, norm_ref, weight_ref, grad_ref, branch_ref, context_ref, sums_ref):
    grad = part_ref[...].astype(f32) + other_ref[...].astype(f32)
    rows, inverse = unit(middle_ref[...])
    grad_unit = grad * norm_ref[2:3, :]
    first_mean = jnp.mean(grad_unit, axis=-1, keepdims=True)
    second_mean = jnp.mean(grad_unit * rows, axis=-1, keepdims=True)
    whole = cot_ref[...].astype(f32) + inverse * (grad_unit - first_mean - rows * second_mean)
    grad_ref[...] = whole
    branch_ref[...] = whole.astype(bf16)
    context_ref[...] = jnp.dot(branch_ref[...], weight_ref[...], preferred_element_type=f32).astype(bf16)
    gain = jnp.sum(grad * rows, axis=0, keepdims=True)
    shift = jnp.sum(grad, axis=0, keepdims=True)

    @pl.when(pl.program_id(0) == 0)
    def _():
        sums_ref[0:1, :] = gain
        sums_ref[1:2, :] = shift

    @pl.when(pl.program_id(0) > 0)
    def _():
        sums_ref[0:1, :] += gain
        sums_ref[1:2, :] += shift


def middle_back(part, other, middle, cot_rows, norm_params, weights_out):
    rows, width = part.shape
    block = min(256, rows)
    columns = weights_out.shape[1]
    piece = pl.BlockSpec((block, width), lambda r: (r, 0))
    return pl.pallas_call(
        middle_kernel,
        grid=(rows // block,),
        in_specs=[
            piece,
            piece,
            piece,
            piece,
            pl.BlockSpec(norm_params.shape, lambda r: (0, 0)),
            pl.BlockSpec(weights_out.shape, lambda r: (0, 0)),
        ],
        out_specs=[piece, piece, pl.BlockSpec((block, columns), lambda r: (r, 0)), pl.BlockSpec((2, width), lambda r: (0, 0))],
        out_shape=[
            pltpu.HBM((rows, width), f32),
            jax.ShapeDtypeStruct((rows, width), bf16),
            pltpu.HBM((rows, columns), bf16),
            jax.ShapeDtypeStruct((2, width), f32),
        ],
        compiler_params=pltpu.CompilerParams(vmem_limit_bytes=14 * 2**20),
        cost_estimate=cost(6),
        name="middle_back",
    )(part, other, middle, cot_rows, norm_params, weights_out)


def first_kernel(place_ref, grads_ref, weight_ref, x_ref, part_ref, sums_ref):
    left = jnp.concatenate([grads_ref[t] for t in range(3)], axis=1)
    right = jnp.concatenate([weight_ref[t] for t in range(3)], axis=1)
    part = lax.dot_general(left, right, ROWS_BY_ROWS, preferred_element_type=f32)
    part_ref[...] = part.astype(bf16)
    sums_ref[0:1, :] = jnp.sum(part * unit(x_ref[...].astype(f32))[0], axis=0, keepdims=True)
    sums_ref[1:2, :] = jnp.sum(part, axis=0, keepdims=True)


def first_back(grads, weights_qkv, x_rows, first_row):
    rows, width = x_rows.shape
    columns = grads.shape[2]
    return pl.pallas_call(
        first_kernel,
        grid_spec=pltpu.PrefetchScalarGridSpec(
            num_scalar_prefetch=1,
            grid=(1,),
            in_specs=[
                pl.BlockSpec((3, rows, columns), lambda r, place: (0, place[0], 0)),
                pl.BlockSpec(weights_qkv.shape, lambda r, place: (0, 0, 0)),
                pl.BlockSpec((rows, width), lambda r, place: (0, 0)),
            ],
            out_specs=[pl.BlockSpec((rows, width), lambda r, place: (0, 0)), pl.BlockSpec((2, width), lambda r, place: (0, 0))],
        ),
        out_shape=[jax.ShapeDtypeStruct((rows, width), bf16), jax.ShapeDtypeStruct((2, width), f32)],
        compiler_params=pltpu.CompilerParams(vmem_limit_bytes=20 * 2**20),
        cost_estimate=cost(6),
        name="first_back",
    )(jnp.reshape(first_row // rows, (1,)), *in_hbm(grads, weights_qkv, x_rows))


def project_kernel(chunks, *refs):
    xs, (norm_ref, weight_ref), normed_refs, result_ref = refs[:chunks], refs[chunks:][:2], refs[chunks + 2 : -1], refs[-1]
    rows = xs[0].shape[0]
    block = min(256, rows)
    for chunk in range(chunks):
        for first in range(0, rows, block):
            at = pl.ds(first, block)
            values = xs[chunk][at, :].astype(f32)
            normed = (unit(values)[0] * norm_ref[0:1, :] + norm_ref[1:2, :]).astype(bf16)
            normed_refs[chunk][at, :] = normed
            for t in range(3):
                product = jnp.dot(normed, weight_ref[t], preferred_element_type=f32)
                result_ref[t, pl.ds(chunk * rows + first, block), :] = product.astype(bf16)


def project(x_rows, norm_params, weights_qkv):
    chunks = len(x_rows)
    rows, width = x_rows[0].shape
    columns = weights_qkv.shape[2]
    *normed, result = pl.pallas_call(
        lambda *refs: project_kernel(chunks, *refs),
        out_shape=[jax.ShapeDtypeStruct((rows, width), bf16)] * chunks
        + [jax.ShapeDtypeStruct((3, rows * chunks, columns), bf16)],
        compiler_params=pltpu.CompilerParams(vmem_limit_bytes=24 * 2**20),
        cost_estimate=cost(8),
        name="project",
    )(*x_rows, norm_params, weights_qkv)
    return (normed, result)


def updated(weight, momentum, average, gradient, step_rate):
    next_moment = momentum_keep * momentum + gradient
    next_weight = weight - step_rate * (gradient + momentum_keep * next_moment)
    next_average = average_keep * average + (1.0 - average_keep) * next_weight
    return (gradient, next_moment, next_weight, next_average)


def update_kernel(counts, rates, place_ref, grad_ref, *refs):
    states, results = refs[: 3 * len(counts)], refs[3 * len(counts) :]
    block = 0
    for i, (count, rate) in enumerate(zip(counts, rates)):
        state, result = states[3 * i : 3 * i + 3], results[4 * i : 4 * i + 4]
        width = state[0].shape[-1]
        for t in range(count):
            at = (t,) if len(state[0].shape) == 3 else ()
            gradient = grad_ref[:, block * width : (block + 1) * width].astype(f32)
            block += 1
            for ref, value in zip(result, updated(*[ref[at + (Ellipsis,)] for ref in state], gradient, rate)):
                ref[at + (Ellipsis,)] = value


def update(gradient, states, place, rates):
    counts, in_specs, out_specs, out_shape = [], [], [], []
    for _, momentum, _ in states:
        shape = momentum.shape
        counts.append(shape[0] if len(shape) == 3 else 1)
        if len(shape) == 3:
            share = pl.BlockSpec(shape, lambda i, place: (0, 0, 0))
            in_specs += [pl.BlockSpec(shape, lambda i, place: (0, place[0], 0)), share, share]
        else:
            share = pl.BlockSpec(shape, lambda i, place: (0, 0))
            in_specs += [pl.BlockSpec(shape, lambda i, place: (place[0], 0)), share, share]
        out_specs += [share] * 4
        out_shape += [jax.ShapeDtypeStruct(shape, f32)] * 4
    return pl.pallas_call(
        lambda *refs: update_kernel(counts, rates, *refs),
        grid_spec=pltpu.PrefetchScalarGridSpec(
            num_scalar_prefetch=1,
            grid=(1,),
            in_specs=[pl.BlockSpec(gradient.shape, lambda i, place: (0, 0))] + in_specs,
            out_specs=out_specs,
        ),
        out_shape=out_shape,
        compiler_params=pltpu.CompilerParams(vmem_limit_bytes=20 * 2**20),
        cost_estimate=cost(4),
        name="update",
    )(place, gradient, *[in_hbm(x) for state in states for x in state])


def pack_kernel(shares, counts, head_ref, buckets_ref, *refs):
    result_ref = refs[-1]
    one, two, diagonals = refs[: counts[0]], refs[counts[0] : sum(counts[:2])], refs[sum(counts[:2]) : -1]
    norms = [sum(ref[...] for ref in one), sum(ref[...] for ref in two) * (1.0 / shares)]
    rows = jnp.concatenate(norms, axis=0)
    for i in range(rows.shape[1] // 128):
        result_ref[4 * i : 4 * i + 4, :] = rows[:, 128 * i : 128 * i + 128]
    offsets = sum(ref[:, 0, :] for ref in diagonals)
    first = rows.shape[1] // 32
    heads = result_ref.shape[0] - first
    bins = lax.broadcasted_iota(jnp.int32, (128, offsets.shape[1]), 0)
    hits = (buckets_ref[...] == bins).astype(f32)
    sums = lax.dot_general(offsets, hits, ROWS_BY_ROWS, precision=highest, preferred_element_type=f32)
    if sums.shape[0] < heads:
        sums = jnp.concatenate([sums, jnp.zeros((heads - sums.shape[0], 128), f32)], axis=0)
    result_ref[first:, :] = pltpu.roll(sums, head_ref[0], 0)


def pack_small(one, two, diagonals, buckets, heads, head_first, shares):
    width = one[0].shape[1]
    return pl.pallas_call(
        lambda *refs: pack_kernel(shares, (len(one), len(two)), *refs),
        in_specs=[pl.BlockSpec(memory_space=pltpu.SMEM)]
        + [pl.BlockSpec(memory_space=pltpu.VMEM)] * (1 + len(one) + len(two) + len(diagonals)),
        out_shape=jax.ShapeDtypeStruct((width // 32 + heads, 128), f32),
        cost_estimate=cost(2),
        name="pack_small",
    )(jnp.reshape(head_first, (1,)), buckets, *one, *two, *diagonals)


def small_update_kernel(rate, small_ref, *refs):
    norm_state, bias_state, results = refs[:3], refs[3:6], refs[6:]
    width = norm_state[0].shape[1]
    gradient = jnp.concatenate([small_ref[4 * i : 4 * i + 4, :] for i in range(width // 128)], axis=1)
    for result, value in zip(results[:4], updated(*[ref[...] for ref in norm_state], gradient, rate)):
        result[...] = value
    gradient = small_ref[width // 32 :, : bias_state[0].shape[1]]
    for result, value in zip(results[4:], updated(*[ref[...] for ref in bias_state], gradient, rate)):
        result[...] = value


def small_update(small, norm_state, bias_state, rate):
    return pl.pallas_call(
        lambda *refs: small_update_kernel(rate, *refs),
        out_shape=[jax.ShapeDtypeStruct(norm_state[0].shape, f32)] * 4
        + [jax.ShapeDtypeStruct(bias_state[0].shape, f32)] * 4,
        cost_estimate=cost(1.5),
        name="small_update",
    )(small, *norm_state, *bias_state)


def finish_kernel(place_ref, x_ref, norm_ref, sent_ref, kept_ref, first_ref, second_ref, result_ref):
    chosen = jnp.where(place_ref[0] == 0, first_ref[...], second_ref[...])
    grad = sent_ref[...].astype(f32) + kept_ref[...].astype(f32)
    rows, inverse = unit(x_ref[...].astype(f32))
    grad_unit = grad * norm_ref[0:1, :]
    first_mean = jnp.mean(grad_unit, axis=-1, keepdims=True)
    second_mean = jnp.mean(grad_unit * rows, axis=-1, keepdims=True)
    result_ref[...] = chosen + inverse * (grad_unit - first_mean - rows * second_mean)


def finish(got, kept, x_rows, norm_params, middle_grad, place):
    rows, width = x_rows.shape
    piece = pl.BlockSpec((rows // 2, width), lambda r, place: (r, 0))
    chosen = [
        pl.BlockSpec((rows // 2, width), lambda r, place: (jnp.where(place[0] == 0, r, 0), 0)),
        pl.BlockSpec((rows // 2, width), lambda r, place: (jnp.where(place[0] == 0, 0, r), 0)),
    ]
    return pl.pallas_call(
        finish_kernel,
        grid_spec=pltpu.PrefetchScalarGridSpec(
            num_scalar_prefetch=1,
            grid=(2,),
            in_specs=[piece, pl.BlockSpec(norm_params.shape, lambda r, place: (0, 0)), piece, piece] + chosen,
            out_specs=piece,
        ),
        out_shape=jax.ShapeDtypeStruct((rows, width), f32),
        compiler_params=pltpu.CompilerParams(vmem_limit_bytes=14 * 2**20),
        cost_estimate=cost(5),
        name="finish",
    )(place, in_hbm(x_rows), norm_params, *in_hbm(got, kept, *middle_grad))


def after(value, *others):
    return lax.optimization_barrier((value,) + others)[0]


def swap(values, axis, bit):
    size = lax.axis_size(axis)
    return lax.ppermute(values, axis, [(i, i ^ bit) for i in range(size)])


def in_order(own, other):
    first = lax.axis_index("mp") == 0
    return [jnp.where(first, own, other), jnp.where(first, other, own)]


def other_part(rows):
    if lax.axis_size("mp") != 2:
        return (lax.psum(rows.astype(f32), "mp") - rows.astype(f32)).astype(bf16)
    return swap(rows, "mp", 1)


def sum_own(sent, kept):
    return kept.astype(f32) + swap(sent, "mp", 1).astype(f32)


def sum_over_clips(gradient, groups):
    return lax.psum_scatter(gradient, "dp", scatter_dimension=0, tiled=True, axis_index_groups=groups)


def per_device(
    inputs,
    cotangent,
    lengths,
    buckets,
    w_qkv,
    w_out,
    w_ffn,
    norm_params,
    rel_bias,
    momentum_qkv,
    momentum_out,
    momentum_ffn,
    momentum_norms,
    momentum_bias,
    average_qkv,
    average_out,
    average_ffn,
    average_norms,
    average_bias,
):
    model_size = lax.axis_size("mp")
    data_size = lax.axis_size("dp")
    rows_local = inputs.shape[0]
    seq_len = rows_local * model_size
    width_local = w_qkv.shape[2]
    heads_local = width_local // HD
    head_first = lax.axis_index("mp") * heads_local
    own_first = lax.axis_index("mp") * rows_local
    share_rows = momentum_out.shape[0]
    chunks = 2
    chunk_rows = seq_len // chunks

    def chunk_of(rows, chunk):
        return lax.slice_in_dim(rows, chunk * chunk_rows, (chunk + 1) * chunk_rows, axis=0)

    if model_size == 2:
        inputs_other = swap(inputs, "mp", 1)
        cot_other = swap(after(cotangent, inputs_other), "mp", 1)
        x_rows = in_order(inputs, inputs_other)
        cot_rows = in_order(cotangent, cot_other)
    else:
        inputs_all = lax.all_gather(inputs, "mp", axis=0, tiled=True)
        cot_other = lax.all_gather(cotangent, "mp", axis=0, tiled=True)
        x_rows = [chunk_of(inputs_all, chunk) for chunk in range(chunks)]
        cot_rows = [chunk_of(cot_other, chunk) for chunk in range(chunks)]
    weights_qkv = w_qkv.astype(bf16)
    weights_out = w_out.astype(bf16)

    bias_local = lax.dynamic_slice_in_dim(rel_bias, head_first, heads_local, 1)
    bucket_hits = (buckets[:, None] == jnp.arange(rel_bias.shape[0], dtype=jnp.int32)[None, :]).astype(f32)
    bias_table = jnp.dot(bucket_hits, bias_local, precision=highest).T
    skew, skew_back = skew_tables(bias_table)

    normed_one, projected = project(x_rows, norm_params, weights_qkv)

    context, totals, branch = [], [], []
    ahead = projected
    for chunk in range(chunks):
        part, total, sent = attend(ahead, lengths, skew, weights_out, chunk, chunks)
        context.append(part)
        totals.append(total)
        branch.append(sent)
        ahead = after(ahead, sent, *cot_rows)
    branch_other = []
    for sent in branch:
        branch_other.append(other_part(after(sent, *branch_other[-1:])))

    ffn = []
    ahead = after(w_ffn, branch[-1])
    for chunk in range(chunks):
        ffn.append(
            feed_forward(
                x_rows[chunk], branch[chunk], branch_other[chunk], cot_rows[chunk], norm_params, ahead
            )
        )
        ahead = after(ahead, ffn[-1][4])
    middle, normed_two, hidden, pre_grad, two_part, out_part = zip(*ffn)
    two_other = [other_part(after(two_part[0], branch_other[-1]))]
    core = jnp.reshape(lax.axis_index("dp") & 1, (1,))
    order = device_ring(data_size)
    chips = chip_ring(data_size // 2)
    cores = [[2 * chip + core for chip in chips] for core in range(2)]
    units = w_ffn.shape[2]
    (ffn_grad,) = weight_sums(normed_two, pre_grad, order, 2 * units, 0)
    ffn_grad, sent, _ = lax.optimization_barrier((ffn_grad, two_part[1], two_other[0]))
    two_other.append(other_part(sent))
    (ffn_grad,) = weight_sums(cot_rows, hidden, order, 2 * units, units, [ffn_grad])
    ffn_share = sum_over_clips(ffn_grad, [order])

    if model_size == 2:
        out_kept, out_sent = in_order(*out_part)
    else:
        out_got = lax.psum_scatter(jnp.concatenate(out_part), "mp", scatter_dimension=0, tiled=True)
    middle_grad, branch_grad, context_grad = [], [], []

    def middle_step(chunk, *others):
        whole, sent, grad, sums = middle_back(
            after(two_part[chunk], *others), two_other[chunk], middle[chunk], cot_rows[chunk], norm_params, weights_out
        )
        middle_grad.append(whole)
        branch_grad.append(sent)
        context_grad.append(grad)
        return sums

    def back(chunk, others, before=()):
        grad = after(context_grad[chunk], *others)
        return attend_back(projected, grad, context[chunk], totals[chunk], lengths, skew_back, chunk, chunks, before)

    sums_two = [middle_step(0, ffn_grad)]
    *before, diagonal = back(0, [])
    diagonals = [diagonal]
    sums_two.append(middle_step(1, diagonal))
    if model_size == 2:
        out_got = swap(after(out_sent, sums_two[-1]), "mp", 1)
    halves = weight_sums(branch_grad, in_hbm(*context), cores[0] + cores[1], 4 * width_local, 3 * width_local, core=core)
    context_grad[1], *halves = lax.optimization_barrier((context_grad[1], *halves))
    grads, diagonal = back(1, [], before)
    diagonals.append(diagonal)
    sent, kept = weight_sums(
        in_hbm(*normed_one), [in_hbm(after(grads, out_got))], cores[0] + cores[1], 4 * width_local, 0, halves, core=core
    )
    halves = (kept, swap(after(sent, ffn_share), "dp", 1))
    grads = after(grads, kept)

    one = jnp.reshape(own_first * 0, (1,))
    place = one + lax.axis_index("dp")
    scale_factor = 1.0 / math.sqrt(float(seq_len * data_size))
    def attention_sums(*others):
        total = after(halves[0], *others).astype(f32) + halves[1].astype(f32)
        return sum_over_clips(total.astype(bf16), cores)

    if model_size == 2:
        sent, sums_sent = first_back(grads, weights_qkv, inputs_other, rows_local - own_first)
        got = swap(sent, "mp", 1)
        attention_share = attention_sums(sent)
        kept, sums_kept = first_back(after(grads, sent), weights_qkv, inputs, own_first)
        sums_one = [sums_sent, sums_kept]
        own = one + lax.axis_index("mp")
        output_rows = in_order(*[after(rows, kept) for rows in middle])[0] + out_kept.astype(f32) + out_got.astype(f32)
    else:
        sent, sums_sent = first_back(grads, weights_qkv, jnp.concatenate(x_rows), own_first * 0)
        attention_share = attention_sums(sent)
        sums_one = [sums_sent]
        kept = lax.psum_scatter(sent, "mp", scatter_dimension=0, tiled=True)
        got = jnp.zeros_like(kept)
        own = one
        middle_grad = [lax.dynamic_slice_in_dim(jnp.concatenate(middle_grad), own_first, rows_local, 0)] * 2
        middle_own = lax.dynamic_slice_in_dim(jnp.concatenate(middle), own_first, rows_local, 0)
        output_rows = middle_own + out_got.astype(f32)

    reversed_buckets = jnp.pad(buckets[::-1], (0, 1), constant_values=-1)[None, :]
    small = pack_small(sums_one, sums_two, diagonals, reversed_buckets, rel_bias.shape[1], head_first, model_size)
    exchanged = swap(small, "dp", 1)
    ffn_results = update(after(ffn_share, small), [(w_ffn, momentum_ffn, average_ffn)], place, [0.05 * scale_factor])
    small = after(small, ffn_results[0]) + exchanged
    exchanged = swap(small, "dp", 2)
    output = output_rows.astype(bf16)
    small = after(small, output) + exchanged
    exchanged = swap(small, "dp", 4)
    input_grad = finish(got, after(kept, small), inputs, norm_params, middle_grad, own)
    small = after(small, input_grad) + exchanged
    bit = 8
    while bit < data_size:
        small = small + swap(small, "dp", bit)
        bit *= 2
    attention_results = update(
        attention_share,
        [(w_qkv, momentum_qkv, average_qkv), (w_out, momentum_out, average_out)],
        place,
        [0.3 * scale_factor, 0.1 * scale_factor],
    )
    for bit in range(model_size.bit_length() - 1):
        exchanged = swap(small, "mp", 1 << bit)
        small = after(small, attention_results[0]) + exchanged
    small_results = small_update(
        small,
        (norm_params, momentum_norms, average_norms),
        (rel_bias.T, momentum_bias.T, average_bias.T),
        0.05 * scale_factor,
    )
    small_results = [*small_results[:4], *[result.T for result in small_results[4:]]]
    return (output, input_grad, *attention_results, *ffn_results, *small_results)


def solution(mesh):
    return jax.shard_map(
        per_device,
        mesh=mesh,
        in_specs=(
            P(("dp", "mp"), None),
            P(("dp", "mp"), None),
            P("dp"),
            P(),
            P(None, None, "mp"),
            P(None, "mp"),
            P(None, None, "mp"),
            P(),
            P(),
            P(None, "dp", "mp"),
            P("dp", "mp"),
            P(None, "dp", "mp"),
            P(),
            P(),
            P(None, "dp", "mp"),
            P("dp", "mp"),
            P(None, "dp", "mp"),
            P(),
            P(),
        ),
        out_specs=(
            P(("dp", "mp"), None),
            P(("dp", "mp"), None),
            P(None, "dp", "mp"),
            P(None, "dp", "mp"),
            P(None, "dp", "mp"),
            P(None, "dp", "mp"),
            P("dp", "mp"),
            P("dp", "mp"),
            P("dp", "mp"),
            P("dp", "mp"),
            P(None, "dp", "mp"),
            P(None, "dp", "mp"),
            P(None, "dp", "mp"),
            P(None, "dp", "mp"),
            P(),
            P(),
            P(),
            P(),
            P(),
            P(),
            P(),
            P(),
        ),
        check_vma=False,
    )
```

```python
import math

import jax
import jax.numpy as jnp
from jax import lax
from jax.experimental import pallas as pl
from jax.experimental.pallas import tpu as pltpu
from jax.sharding import PartitionSpec as P

HD = 64
PAIR = 2 * HD
QB = 128
QUERY_BLOCK = 512
KEY_BLOCK = 512
f32 = jnp.float32
bf16 = jnp.bfloat16
ROWS_BY_ROWS = (((1,), (1,)), ((), ()))
COLS_BY_COLS = (((0,), (0,)), ((), ()))
VMEM_LIMIT = 56 * 2**20

highest = lax.Precision.HIGHEST
momentum_keep = 0.5
average_keep = 0.5
SHARE = 1.1e6


def cost(microseconds):
    return pl.CostEstimate(flops=0, bytes_accessed=int(SHARE * microseconds), transcendentals=0)


def in_hbm(*values):
    values = [pltpu.with_memory_space_constraint(value, pltpu.HBM) for value in values]
    return values if len(values) > 1 else values[0]


def skew_kernel(forward_ref, reverse_ref, forward_out, reverse_out):
    width = forward_ref.shape[2]
    for source, result in ((forward_ref, forward_out), (reverse_ref, reverse_out)):
        rows = jnp.broadcast_to(source[0], (QB, width))
        result[0] = pltpu.roll(rows, width - (QB - 1), 1, stride=1, stride_axis=0)[:, : width - QB]


def skew_tables(table):
    heads, width = table.shape
    forward = jnp.pad(table, ((0, 0), (0, 1)))[:, None, :]
    reverse = jnp.pad(table[:, ::-1], ((0, 0), (0, 1)))[:, None, :]
    width += 1
    row = pl.BlockSpec((1, 1, width), lambda h: (h, 0, 0))
    skewed = pl.BlockSpec((1, QB, width - QB), lambda h: (h, 0, 0))
    shape = jax.ShapeDtypeStruct((heads, QB, width - QB), f32)
    return pl.pallas_call(
        skew_kernel,
        grid=(heads,),
        in_specs=[row, row],
        out_specs=[skewed, skewed],
        out_shape=[shape, shape],
        cost_estimate=cost(8),
        name="skew",
    )(forward, reverse)


def three_parts(values):
    first = values.astype(bf16).astype(f32)
    rest = values - first
    second = rest.astype(bf16).astype(f32)
    return (first, second, rest - second)


def own_lanes(lane, head):
    return (lane >= HD) if head else (lane < HD)


def key_side(keys, mask, lane, head):
    first = 0 if head else HD
    extra = jnp.where(lane == first, mask, jnp.where((lane > first) & (lane < first + 4), 1.0, 0.0))
    return jnp.where(own_lanes(lane, head), keys, extra).astype(bf16)


def forward_kernel(
    first_row,
    length_ref,
    q_ref,
    k_ref,
    v_ref,
    skew_ref,
    context_ref,
    total_ref,
    key_ref,
    value_ref,
    raised_ref,
):
    seq_len = k_ref.shape[0]
    rows_here = q_ref.shape[0]
    lane = lax.broadcasted_iota(jnp.int32, (seq_len, PAIR), 1)
    place = lax.broadcasted_iota(jnp.int32, (seq_len, PAIR), 0)
    mask = jnp.where(place < length_ref[0], 0.0, -1e9)
    keys = k_ref[...].astype(f32)
    values = v_ref[...].astype(f32)
    for head in range(2):
        key_ref[head] = key_side(keys, mask, lane, head)
        value_ref[head] = jnp.where(own_lanes(lane, head), values, 1.0).astype(bf16)
    here = min(QUERY_BLOCK, rows_here)
    lane = lax.broadcasted_iota(jnp.int32, (here, PAIR), 1)

    def block(index, carry):
        rows = pl.ds(pl.multiple_of(index * here, here), here)
        queries = q_ref[rows, :].astype(f32) * 0.125
        context = []
        totals = []
        for head in range(2):
            own = own_lanes(lane, head)
            first = 0 if head else HD
            query = jnp.where(own, queries, jnp.where(lane == first, 1.0, 0.0)).astype(bf16)
            scores = lax.dot_general(query, key_ref[head], ROWS_BY_ROWS, preferred_element_type=f32)
            tops = []
            for piece in range(0, here, QB):
                start = pl.multiple_of(seq_len - QB - first_row - index * here - piece, QB)
                moved = scores[piece : piece + QB] + skew_ref[head, :, pl.ds(start, seq_len)]
                top = jnp.max(moved, axis=1, keepdims=True)
                raised_ref[head, piece : piece + QB, :] = jnp.exp(moved - top).astype(bf16)
                tops.append(top)
            weighted = jnp.dot(raised_ref[head], value_ref[head], preferred_element_type=f32)
            context.append(weighted / weighted[:, first : first + 1])
            totals.append(jnp.concatenate(tops, axis=0) + jnp.log(jnp.where(own, 1.0, weighted)))
        context_ref[rows, :] = jnp.where(lane < HD, context[0], context[1]).astype(bf16)
        total_ref[rows, :] = jnp.where(lane < HD, totals[1], totals[0])
        return carry

    lax.fori_loop(0, rows_here // here, block, 0, unroll=True)


def attend(projected, lengths, skew, chunk, chunks):
    _, seq_len, width = projected.shape
    rows_here = seq_len // chunks
    whole = [pl.BlockSpec((None, seq_len, PAIR), lambda p, t=t: (t, 0, p)) for t in (1, 2)]
    part = pl.BlockSpec((rows_here, PAIR), lambda p: (0, p))
    return pl.pallas_call(
        lambda *refs: forward_kernel(chunk * rows_here, *refs),
        grid=(width // PAIR,),
        in_specs=[
            pl.BlockSpec(memory_space=pltpu.SMEM),
            pl.BlockSpec((None, rows_here, PAIR), lambda p: (0, chunk, p)),
            *whole,
            pl.BlockSpec((2,) + skew.shape[1:], lambda p: (p, 0, 0)),
        ],
        out_specs=[part, part],
        out_shape=[
            jax.ShapeDtypeStruct((rows_here, width), bf16),
            jax.ShapeDtypeStruct((rows_here, width), f32),
        ],
        scratch_shapes=[
            pltpu.VMEM((2, seq_len, PAIR), bf16),
            pltpu.VMEM((2, seq_len, PAIR), bf16),
            pltpu.VMEM((2, min(QUERY_BLOCK, rows_here), seq_len), bf16),
        ],
        compiler_params=pltpu.CompilerParams(vmem_limit_bytes=24 * 2**20),
        cost_estimate=cost(13),
        name="attend",
    )(lengths, projected, projected, projected, in_hbm(skew))


def diagonal_sums(skewed):
    width = skewed.shape[1]
    total = pltpu.roll(skewed[:8], QB - 1, 1)
    for group in range(1, QB // 8):
        total = total + pltpu.roll(skewed[8 * group : 8 * group + 8], QB - 1 - 8 * group, 1)
    row = lax.broadcasted_iota(jnp.int32, total.shape, 0)
    for bit in (1, 2, 4):
        total = jnp.where((row & bit) != 0, pltpu.roll(total, width - bit, 1), total)
    return jnp.sum(total, axis=0, keepdims=True)


def backward_kernel(first_row, last, *refs):
    (length_ref, q_ref, k_ref, v_ref, grad_ref, context_ref, total_ref, skew_ref) = refs[:8]
    running = last and first_row > 0
    if running:
        dq_before, dk_before, dv_before = refs[8:11]
    if last:
        grads_ref, diagonal_ref = refs[-8:-6]
        dq_ref = grads_ref.at[0, pl.ds(first_row, q_ref.shape[0]), :]
        dk_ref, dv_ref = grads_ref.at[1], grads_ref.at[2]
    else:
        dq_ref, dk_ref, dv_ref, diagonal_ref = refs[-10:-6]
    (query_ref, back_ref, skewed_ref, dq_sum, soft_ref, slope_ref) = refs[-6:]
    if running:
        grads_ref[0, :first_row, :] = dq_before[...]
    seq_len = k_ref.shape[0]
    rows_here = q_ref.shape[0]
    lane = lax.broadcasted_iota(jnp.int32, (rows_here, PAIR), 1)
    queries = q_ref[...].astype(f32) * 0.125
    back = grad_ref[...].astype(f32)
    dots = back * context_ref[...].astype(f32)
    first_lane = lax.broadcasted_iota(jnp.int32, (PAIR, PAIR), 0) // HD
    cross = jnp.where(first_lane != lax.broadcasted_iota(jnp.int32, (PAIR, PAIR), 1) // HD, 1.0, 0.0).astype(bf16)
    row_dot = sum(jnp.dot(part.astype(bf16), cross, preferred_element_type=f32) for part in three_parts(dots)[:2])
    tops = three_parts(-total_ref[...])
    drops = three_parts(-row_dot)
    for head in range(2):
        own = own_lanes(lane, head)
        first = 0 if head else HD
        query = jnp.where(lane == first, 1.0, 0.0)
        graded = jnp.zeros_like(query)
        for i in range(3):
            query = jnp.where(lane == first + 1 + i, tops[i], query)
            graded = jnp.where(lane == first + 1 + i, drops[i], graded)
        query_ref[head] = jnp.where(own, queries, query).astype(bf16)
        back_ref[head] = jnp.where(own, back, graded).astype(bf16)
    skewed_ref[...] = jnp.zeros_like(skewed_ref)
    keys_here = soft_ref.shape[1]
    small_lane = lax.broadcasted_iota(jnp.int32, (keys_here, PAIR), 1)
    small_row = lax.broadcasted_iota(jnp.int32, (keys_here, PAIR), 0)

    def block(index, carry):
        rows = pl.ds(pl.multiple_of(index * keys_here, keys_here), keys_here)
        keys = k_ref[rows, :].astype(f32)
        values = v_ref[rows, :].astype(f32)
        mask = jnp.where(small_row + index * keys_here < length_ref[0], 0.0, -1e9)
        dq, dk, dv = [], [], []
        for head in range(2):
            key = key_side(keys, mask, small_lane, head)
            value = key_side(values, 0.0, small_lane, head)
            scores = lax.dot_general(key, query_ref[head], ROWS_BY_ROWS, preferred_element_type=f32)
            drop = lax.dot_general(value, back_ref[head], ROWS_BY_ROWS, preferred_element_type=f32)
            for first in range(0, keys_here, QB):
                piece = slice(first, first + QB)
                start = pl.multiple_of(seq_len - QB + first_row - index * keys_here - first, QB)
                soft = jnp.exp(scores[piece] + skew_ref[head, :, pl.ds(start, rows_here)])
                score_grad = soft * drop[piece]
                skewed_ref[head, :, pl.ds(start, rows_here)] += score_grad
                soft_ref[head, piece, :] = soft.astype(bf16)
                slope_ref[head, piece, :] = score_grad.astype(bf16)
            dv.append(jnp.dot(soft_ref[head], back_ref[head], preferred_element_type=f32))
            dk.append(jnp.dot(slope_ref[head], query_ref[head], preferred_element_type=f32))
            dq.append(lax.dot_general(slope_ref[head], key, COLS_BY_COLS, preferred_element_type=f32))
        dk = jnp.where(small_lane < HD, dk[0], dk[1])
        dv = jnp.where(small_lane < HD, dv[0], dv[1])
        if running:
            dk = dk + dk_before[rows, :]
            dv = dv + dv_before[rows, :]
        dk_ref[rows, :] = dk.astype(dk_ref.dtype)
        dv_ref[rows, :] = dv.astype(dv_ref.dtype)
        dq = jnp.where(lane < HD, dq[0], dq[1])

        @pl.when(index == 0)
        def _():
            dq_sum[...] = dq

        @pl.when(index > 0)
        def _():
            dq_sum[...] += dq

        return carry

    lax.fori_loop(0, seq_len // keys_here, block, 0, unroll=True)
    dq_ref[...] = (dq_sum[...] * 0.125).astype(bf16)
    for head in range(2):
        diagonal_ref[head] = diagonal_sums(jnp.concatenate([skewed_ref[head], jnp.zeros((QB, QB), f32)], axis=1))


def attend_back(projected, context_grad, context, totals, lengths, skew, chunk, chunks, before=()):
    _, seq_len, width = projected.shape
    pairs = width // PAIR
    rows_here = seq_len // chunks
    key_block = min(KEY_BLOCK, seq_len)
    skew_width = skew.shape[2]
    whole = [pl.BlockSpec((None, seq_len, PAIR), lambda p, t=t: (t, 0, p)) for t in (1, 2)]
    part = pl.BlockSpec((rows_here, PAIR), lambda p: (0, p))
    full = pl.BlockSpec((seq_len, PAIR), lambda p: (0, p))
    last = chunk == chunks - 1
    if last:
        out_specs = [pl.BlockSpec((3, seq_len, PAIR), lambda p: (0, 0, p))]
        out_shape = [pltpu.HBM((3, seq_len, width), bf16)]
    else:
        out_specs = [part, full, full]
        out_shape = [jax.ShapeDtypeStruct((rows_here, width), bf16)] + [jax.ShapeDtypeStruct((seq_len, width), f32)] * 2
    return pl.pallas_call(
        lambda *refs: backward_kernel(chunk * rows_here, last, *refs),
        grid=(pairs,),
        in_specs=[
            pl.BlockSpec(memory_space=pltpu.SMEM),
            pl.BlockSpec((None, rows_here, PAIR), lambda p: (0, chunk, p)),
            *whole,
            part,
            part,
            part,
            pl.BlockSpec((2, QB, skew_width), lambda p: (p, 0, 0)),
            *[part, full, full][: len(before)],
        ],
        out_specs=out_specs + [pl.BlockSpec((2, 1, skew_width + QB), lambda p: (p, 0, 0))],
        out_shape=out_shape + [jax.ShapeDtypeStruct((width // HD, 1, skew_width + QB), f32)],
        scratch_shapes=[
            pltpu.VMEM((2, rows_here, PAIR), bf16),
            pltpu.VMEM((2, rows_here, PAIR), bf16),
            pltpu.VMEM((2, QB, skew_width), f32),
            pltpu.VMEM((rows_here, PAIR), f32),
            pltpu.VMEM((2, key_block, rows_here), bf16),
            pltpu.VMEM((2, key_block, rows_here), bf16),
        ],
        compiler_params=pltpu.CompilerParams(vmem_limit_bytes=28 * 2**20),
        cost_estimate=cost(18),
        name="attend_back",
    )(lengths, *in_hbm(projected, projected, projected, context_grad, context, totals, skew, *before))


def unit(values):
    row_mean = jnp.mean(values, axis=-1, keepdims=True)
    centered = values - row_mean
    spread = jnp.mean(centered * centered, axis=-1, keepdims=True)
    inverse = lax.rsqrt(spread + 1e-05)
    return (centered * inverse, inverse)


def ffn_kernel(parts, x_ref, *refs):
    contexts, weights, refs = refs[:parts], refs[parts : 2 * parts], refs[2 * parts :]
    (cot_ref, norm_ref, up_ref, down_ref), refs = refs[:4], refs[4:]
    (middle_ref, normed_ref, hidden_ref, pre_ref, grad_ref, out_ref, grad_sum, out_sum) = refs
    step = pl.program_id(0)

    @pl.when(step == 0)
    def _():
        branch = [
            lax.dot_general(context[...], weight[...], ROWS_BY_ROWS, preferred_element_type=f32)
            for context, weight in zip(contexts, weights)
        ]
        middle = x_ref[...].astype(f32) + sum(branch[1:], branch[0])
        middle_ref[...] = middle
        normed_ref[...] = (unit(middle)[0] * norm_ref[2:3, :] + norm_ref[3:4, :]).astype(bf16)
        grad_sum[...] = jnp.zeros_like(grad_sum)
        out_sum[...] = jnp.zeros_like(out_sum)

    up = up_ref[...].astype(bf16)
    down = down_ref[...].astype(bf16)
    block = min(512, x_ref.shape[0])
    for first in range(0, x_ref.shape[0], block):
        rows = pl.ds(first, block)
        hidden_pre = jnp.dot(normed_ref[rows, :], up, preferred_element_type=f32)
        hidden_grad = jnp.dot(cot_ref[rows, :], down, preferred_element_type=f32)
        gate = 0.5 + 0.5 * lax.erf(hidden_pre * 0.7071067811865476)
        slope = gate + hidden_pre * (0.3989422804014327 * jnp.exp(-0.5 * hidden_pre * hidden_pre))
        hidden = (hidden_pre * gate).astype(bf16)
        pre_grad = (hidden_grad * slope).astype(bf16)
        hidden_ref[rows, :] = hidden
        pre_ref[rows, :] = pre_grad
        grad_sum[rows, :] += lax.dot_general(pre_grad, up, ROWS_BY_ROWS, preferred_element_type=f32)
        out_sum[rows, :] += lax.dot_general(hidden, down, ROWS_BY_ROWS, preferred_element_type=f32)

    @pl.when(step == pl.num_programs(0) - 1)
    def _():
        grad_ref[...] = grad_sum[...].astype(bf16)
        out_ref[...] = out_sum[...].astype(bf16)


def feed_forward(x_rows, contexts, weights_out, cot_rows, norm_params, weights_ffn):
    rows, width = x_rows.shape
    units = weights_ffn.shape[2]
    tile = min(512, units)
    whole = pl.BlockSpec((rows, width), lambda f: (0, 0))
    tall = pl.BlockSpec((rows, tile), lambda f: (0, f))
    return pl.pallas_call(
        lambda *refs: ffn_kernel(len(contexts), *refs),
        grid=(units // tile,),
        in_specs=[
            whole,
            *[pl.BlockSpec(x.shape, lambda f: (0, 0)) for x in [*contexts, *weights_out]],
            whole,
            pl.BlockSpec(norm_params.shape, lambda f: (0, 0)),
            pl.BlockSpec((None, width, tile), lambda f: (0, 0, f)),
            pl.BlockSpec((None, width, tile), lambda f: (1, 0, f)),
        ],
        out_specs=[whole, whole, tall, tall, whole, whole],
        out_shape=[
            pltpu.HBM((rows, width), f32),
            jax.ShapeDtypeStruct((rows, width), bf16),
            jax.ShapeDtypeStruct((rows, units), bf16),
            jax.ShapeDtypeStruct((rows, units), bf16),
            jax.ShapeDtypeStruct((rows, width), bf16),
            jax.ShapeDtypeStruct((rows, width), bf16),
        ],
        scratch_shapes=[pltpu.VMEM((rows, width), f32)] * 2,
        compiler_params=pltpu.CompilerParams(vmem_limit_bytes=38 * 2**20),
        cost_estimate=cost(17.5),
        name="feed_forward",
    )(x_rows, *contexts, *weights_out, cot_rows, norm_params, weights_ffn, weights_ffn)


def chip_ring(count):
    if count % 4:
        return list(range(count))
    rows, columns = 4, count // 4
    chips = [(row, 0) for row in range(rows)]
    for turn, row in enumerate(range(rows - 1, -1, -1)):
        across = [(row, column) for column in range(1, columns)]
        chips += across[::-1] if turn % 2 else across
    return [row * columns + column for row, column in chips]


def device_ring(size):
    chips = chip_ring(size // 2)
    return [2 * chip + core for turn, chip in enumerate(chips) for core in ((0, 1), (1, 0))[turn % 2]]


def weight_kernel(order, chunks, halves, core_ref, *refs):
    lefts, rights = refs[:chunks], refs[chunks : 2 * chunks]
    results, left_ref = refs[-1 - halves : -1], refs[-1]
    rows, features = lefts[0].shape
    share = features // len(order)
    part = features // halves

    @pl.when(pl.program_id(0) == 0)
    def _():
        for chunk in range(chunks):
            turned = lefts[chunk][...].T
            for position, block in enumerate(order):
                half, first = divmod(position * share, part)
                if halves == 2:
                    half = jnp.where(core_ref[0] == half, 1, 0)
                left_ref[half, first : first + share, chunk * rows : (chunk + 1) * rows] = turned[
                    block * share : (block + 1) * share
                ]

    left = left_ref[...].reshape(features, chunks * rows)
    total = 0.0
    for chunk in range(chunks):
        piece = left[:, chunk * rows : (chunk + 1) * rows]
        total = total + jnp.dot(piece, rights[chunk][...], preferred_element_type=f32)
    for half, result in enumerate(results):
        result[...] = total[half * part : (half + 1) * part].astype(bf16)


def weight_sums(lefts, rights, order, columns, first, before=(), core=None):
    chunks = len(lefts)
    rows, features = lefts[0].shape
    halves = 1 if core is None else 2
    if len(rights) == chunks:
        tile = min(512, rights[0].shape[1])
        steps = rights[0].shape[1] // tile
        right_specs = [pl.BlockSpec((rows, tile), lambda c: (0, c))] * chunks
    else:
        steps, _, tile = rights[0].shape
        right_specs = [pl.BlockSpec((None, rows, tile), lambda c, k=k: (c, k, 0)) for k in range(chunks)]
        rights = rights * chunks
    return pl.pallas_call(
        lambda *refs: weight_kernel(order, chunks, halves, *refs),
        grid=(steps,),
        in_specs=[pl.BlockSpec(memory_space=pltpu.SMEM)]
        + [pl.BlockSpec((rows, features), lambda c: (0, 0))] * chunks
        + right_specs
        + [pl.BlockSpec(memory_space=pl.ANY)] * len(before),
        out_specs=[pl.BlockSpec((features // halves, tile), lambda c: (0, c + first // tile))] * halves,
        out_shape=[pltpu.HBM((features // halves, columns), bf16)] * halves,
        input_output_aliases={1 + 2 * chunks + half: half for half in range(len(before))},
        scratch_shapes=[pltpu.VMEM((halves, features // halves, rows * chunks), bf16)],
        compiler_params=pltpu.CompilerParams(vmem_limit_bytes=20 * 2**20),
        cost_estimate=cost(2 * steps + 1),
        name="weight_sums",
    )(jnp.zeros((1,), jnp.int32) if core is None else core, *lefts, *rights, *before)


def middle_kernel(part_ref, other_ref, middle_ref, cot_ref, norm_ref, weight_ref, grad_ref, branch_ref, context_ref, sums_ref):
    grad = part_ref[...].astype(f32) + other_ref[...].astype(f32)
    rows, inverse = unit(middle_ref[...])
    grad_unit = grad * norm_ref[2:3, :]
    first_mean = jnp.mean(grad_unit, axis=-1, keepdims=True)
    second_mean = jnp.mean(grad_unit * rows, axis=-1, keepdims=True)
    whole = cot_ref[...].astype(f32) + inverse * (grad_unit - first_mean - rows * second_mean)
    grad_ref[...] = whole
    branch_ref[...] = whole.astype(bf16)
    context_ref[...] = jnp.dot(branch_ref[...], weight_ref[...], preferred_element_type=f32).astype(bf16)
    gain = jnp.sum(grad * rows, axis=0, keepdims=True)
    shift = jnp.sum(grad, axis=0, keepdims=True)

    @pl.when(pl.program_id(0) == 0)
    def _():
        sums_ref[0:1, :] = gain
        sums_ref[1:2, :] = shift

    @pl.when(pl.program_id(0) > 0)
    def _():
        sums_ref[0:1, :] += gain
        sums_ref[1:2, :] += shift


def middle_back(part, other, middle, cot_rows, norm_params, weights_out):
    rows, width = part.shape
    block = min(256, rows)
    columns = weights_out.shape[1]
    piece = pl.BlockSpec((block, width), lambda r: (r, 0))
    return pl.pallas_call(
        middle_kernel,
        grid=(rows // block,),
        in_specs=[
            piece,
            piece,
            piece,
            piece,
            pl.BlockSpec(norm_params.shape, lambda r: (0, 0)),
            pl.BlockSpec(weights_out.shape, lambda r: (0, 0)),
        ],
        out_specs=[piece, piece, pl.BlockSpec((block, columns), lambda r: (r, 0)), pl.BlockSpec((2, width), lambda r: (0, 0))],
        out_shape=[
            pltpu.HBM((rows, width), f32),
            jax.ShapeDtypeStruct((rows, width), bf16),
            pltpu.HBM((rows, columns), bf16),
            jax.ShapeDtypeStruct((2, width), f32),
        ],
        compiler_params=pltpu.CompilerParams(vmem_limit_bytes=14 * 2**20),
        cost_estimate=cost(6),
        name="middle_back",
    )(part, other, middle, cot_rows, norm_params, weights_out)


def first_kernel(place_ref, grads_ref, weight_ref, x_ref, part_ref, sums_ref):
    left = jnp.concatenate([grads_ref[t] for t in range(3)], axis=1)
    right = jnp.concatenate([weight_ref[t] for t in range(3)], axis=1)
    part = lax.dot_general(left, right, ROWS_BY_ROWS, preferred_element_type=f32)
    part_ref[...] = part.astype(bf16)
    sums_ref[0:1, :] = jnp.sum(part * unit(x_ref[...].astype(f32))[0], axis=0, keepdims=True)
    sums_ref[1:2, :] = jnp.sum(part, axis=0, keepdims=True)


def first_back(grads, weights_qkv, x_rows, first_row):
    rows, width = x_rows.shape
    columns = grads.shape[2]
    return pl.pallas_call(
        first_kernel,
        grid_spec=pltpu.PrefetchScalarGridSpec(
            num_scalar_prefetch=1,
            grid=(1,),
            in_specs=[
                pl.BlockSpec((3, rows, columns), lambda r, place: (0, place[0], 0)),
                pl.BlockSpec(weights_qkv.shape, lambda r, place: (0, 0, 0)),
                pl.BlockSpec((rows, width), lambda r, place: (0, 0)),
            ],
            out_specs=[pl.BlockSpec((rows, width), lambda r, place: (0, 0)), pl.BlockSpec((2, width), lambda r, place: (0, 0))],
        ),
        out_shape=[jax.ShapeDtypeStruct((rows, width), bf16), jax.ShapeDtypeStruct((2, width), f32)],
        compiler_params=pltpu.CompilerParams(vmem_limit_bytes=20 * 2**20),
        cost_estimate=cost(6),
        name="first_back",
    )(jnp.reshape(first_row // rows, (1,)), *in_hbm(grads, weights_qkv, x_rows))


def project_kernel(chunks, *refs):
    xs, (norm_ref, weight_ref), normed_refs, result_ref = refs[:chunks], refs[chunks:][:2], refs[chunks + 2 : -1], refs[-1]
    rows = xs[0].shape[0]
    block = min(256, rows)
    for chunk in range(chunks):
        for first in range(0, rows, block):
            at = pl.ds(first, block)
            values = xs[chunk][at, :].astype(f32)
            normed = (unit(values)[0] * norm_ref[0:1, :] + norm_ref[1:2, :]).astype(bf16)
            normed_refs[chunk][at, :] = normed
            for t in range(3):
                product = jnp.dot(normed, weight_ref[t], preferred_element_type=f32)
                result_ref[t, pl.ds(chunk * rows + first, block), :] = product.astype(bf16)


def project(x_rows, norm_params, weights_qkv):
    chunks = len(x_rows)
    rows, width = x_rows[0].shape
    columns = weights_qkv.shape[2]
    *normed, result = pl.pallas_call(
        lambda *refs: project_kernel(chunks, *refs),
        out_shape=[jax.ShapeDtypeStruct((rows, width), bf16)] * chunks
        + [jax.ShapeDtypeStruct((3, rows * chunks, columns), bf16)],
        compiler_params=pltpu.CompilerParams(vmem_limit_bytes=24 * 2**20),
        cost_estimate=cost(8),
        name="project",
    )(*x_rows, norm_params, weights_qkv)
    return (normed, result)


def updated(weight, momentum, average, gradient, step_rate):
    next_moment = momentum_keep * momentum + gradient
    next_weight = weight - step_rate * (gradient + momentum_keep * next_moment)
    next_average = average_keep * average + (1.0 - average_keep) * next_weight
    return (gradient, next_moment, next_weight, next_average)


def update_kernel(counts, rates, place_ref, grad_ref, *refs):
    states, results = refs[: 3 * len(counts)], refs[3 * len(counts) :]
    block = 0
    for i, (count, rate) in enumerate(zip(counts, rates)):
        state, result = states[3 * i : 3 * i + 3], results[4 * i : 4 * i + 4]
        width = state[0].shape[-1]
        for t in range(count):
            at = (t,) if len(state[0].shape) == 3 else ()
            gradient = grad_ref[:, block * width : (block + 1) * width].astype(f32)
            block += 1
            for ref, value in zip(result, updated(*[ref[at + (Ellipsis,)] for ref in state], gradient, rate)):
                ref[at + (Ellipsis,)] = value


def update(gradient, states, place, rates):
    counts, in_specs, out_specs, out_shape = [], [], [], []
    for _, momentum, _ in states:
        shape = momentum.shape
        counts.append(shape[0] if len(shape) == 3 else 1)
        if len(shape) == 3:
            share = pl.BlockSpec(shape, lambda i, place: (0, 0, 0))
            in_specs += [pl.BlockSpec(shape, lambda i, place: (0, place[0], 0)), share, share]
        else:
            share = pl.BlockSpec(shape, lambda i, place: (0, 0))
            in_specs += [pl.BlockSpec(shape, lambda i, place: (place[0], 0)), share, share]
        out_specs += [share] * 4
        out_shape += [jax.ShapeDtypeStruct(shape, f32)] * 4
    return pl.pallas_call(
        lambda *refs: update_kernel(counts, rates, *refs),
        grid_spec=pltpu.PrefetchScalarGridSpec(
            num_scalar_prefetch=1,
            grid=(1,),
            in_specs=[pl.BlockSpec(gradient.shape, lambda i, place: (0, 0))] + in_specs,
            out_specs=out_specs,
        ),
        out_shape=out_shape,
        compiler_params=pltpu.CompilerParams(vmem_limit_bytes=20 * 2**20),
        cost_estimate=cost(4),
        name="update",
    )(place, gradient, *[in_hbm(x) for state in states for x in state])


def pack_kernel(shares, counts, head_ref, buckets_ref, *refs):
    result_ref = refs[-1]
    one, two, diagonals = refs[: counts[0]], refs[counts[0] : sum(counts[:2])], refs[sum(counts[:2]) : -1]
    norms = [sum(ref[...] for ref in one), sum(ref[...] for ref in two) * (1.0 / shares)]
    rows = jnp.concatenate(norms, axis=0)
    for i in range(rows.shape[1] // 128):
        result_ref[4 * i : 4 * i + 4, :] = rows[:, 128 * i : 128 * i + 128]
    offsets = sum(ref[:, 0, :] for ref in diagonals)
    first = rows.shape[1] // 32
    heads = result_ref.shape[0] - first
    bins = lax.broadcasted_iota(jnp.int32, (128, offsets.shape[1]), 0)
    hits = (buckets_ref[...] == bins).astype(f32)
    sums = lax.dot_general(offsets, hits, ROWS_BY_ROWS, precision=highest, preferred_element_type=f32)
    if sums.shape[0] < heads:
        sums = jnp.concatenate([sums, jnp.zeros((heads - sums.shape[0], 128), f32)], axis=0)
    result_ref[first:, :] = pltpu.roll(sums, head_ref[0], 0)


def pack_small(one, two, diagonals, buckets, heads, head_first, shares):
    width = one[0].shape[1]
    return pl.pallas_call(
        lambda *refs: pack_kernel(shares, (len(one), len(two)), *refs),
        in_specs=[pl.BlockSpec(memory_space=pltpu.SMEM)]
        + [pl.BlockSpec(memory_space=pltpu.VMEM)] * (1 + len(one) + len(two) + len(diagonals)),
        out_shape=jax.ShapeDtypeStruct((width // 32 + heads, 128), f32),
        cost_estimate=cost(2),
        name="pack_small",
    )(jnp.reshape(head_first, (1,)), buckets, *one, *two, *diagonals)


def small_update_kernel(rate, small_ref, *refs):
    norm_state, bias_state, results = refs[:3], refs[3:6], refs[6:]
    width = norm_state[0].shape[1]
    gradient = jnp.concatenate([small_ref[4 * i : 4 * i + 4, :] for i in range(width // 128)], axis=1)
    for result, value in zip(results[:4], updated(*[ref[...] for ref in norm_state], gradient, rate)):
        result[...] = value
    gradient = small_ref[width // 32 :, : bias_state[0].shape[1]]
    for result, value in zip(results[4:], updated(*[ref[...] for ref in bias_state], gradient, rate)):
        result[...] = value


def small_update(small, norm_state, bias_state, rate):
    return pl.pallas_call(
        lambda *refs: small_update_kernel(rate, *refs),
        out_shape=[jax.ShapeDtypeStruct(norm_state[0].shape, f32)] * 4
        + [jax.ShapeDtypeStruct(bias_state[0].shape, f32)] * 4,
        cost_estimate=cost(1.5),
        name="small_update",
    )(small, *norm_state, *bias_state)


def finish_kernel(place_ref, x_ref, norm_ref, sent_ref, kept_ref, first_ref, second_ref, result_ref):
    chosen = jnp.where(place_ref[0] == 0, first_ref[...], second_ref[...])
    grad = sent_ref[...].astype(f32) + kept_ref[...].astype(f32)
    rows, inverse = unit(x_ref[...].astype(f32))
    grad_unit = grad * norm_ref[0:1, :]
    first_mean = jnp.mean(grad_unit, axis=-1, keepdims=True)
    second_mean = jnp.mean(grad_unit * rows, axis=-1, keepdims=True)
    result_ref[...] = chosen + inverse * (grad_unit - first_mean - rows * second_mean)


def finish(got, kept, x_rows, norm_params, middle_grad, place):
    rows, width = x_rows.shape
    piece = pl.BlockSpec((rows // 2, width), lambda r, place: (r, 0))
    chosen = [
        pl.BlockSpec((rows // 2, width), lambda r, place: (jnp.where(place[0] == 0, r, 0), 0)),
        pl.BlockSpec((rows // 2, width), lambda r, place: (jnp.where(place[0] == 0, 0, r), 0)),
    ]
    return pl.pallas_call(
        finish_kernel,
        grid_spec=pltpu.PrefetchScalarGridSpec(
            num_scalar_prefetch=1,
            grid=(2,),
            in_specs=[piece, pl.BlockSpec(norm_params.shape, lambda r, place: (0, 0)), piece, piece] + chosen,
            out_specs=piece,
        ),
        out_shape=jax.ShapeDtypeStruct((rows, width), f32),
        compiler_params=pltpu.CompilerParams(vmem_limit_bytes=14 * 2**20),
        cost_estimate=cost(5),
        name="finish",
    )(place, in_hbm(x_rows), norm_params, *in_hbm(got, kept, *middle_grad))


def after(value, *others):
    return lax.optimization_barrier((value,) + others)[0]


def swap(values, axis, bit):
    size = lax.axis_size(axis)
    return lax.ppermute(values, axis, [(i, i ^ bit) for i in range(size)])


def in_order(own, other):
    first = lax.axis_index("mp") == 0
    return [jnp.where(first, own, other), jnp.where(first, other, own)]


def other_part(rows):
    if lax.axis_size("mp") != 2:
        return (lax.psum(rows.astype(f32), "mp") - rows.astype(f32)).astype(bf16)
    return swap(rows, "mp", 1)


def sum_own(sent, kept):
    return kept.astype(f32) + swap(sent, "mp", 1).astype(f32)


def sum_over_clips(gradient, groups):
    return lax.psum_scatter(gradient, "dp", scatter_dimension=0, tiled=True, axis_index_groups=groups)


def per_device(
    inputs,
    cotangent,
    lengths,
    buckets,
    w_qkv,
    w_out,
    w_ffn,
    norm_params,
    rel_bias,
    momentum_qkv,
    momentum_out,
    momentum_ffn,
    momentum_norms,
    momentum_bias,
    average_qkv,
    average_out,
    average_ffn,
    average_norms,
    average_bias,
):
    model_size = lax.axis_size("mp")
    data_size = lax.axis_size("dp")
    rows_local = inputs.shape[0]
    seq_len = rows_local * model_size
    width_local = w_qkv.shape[2]
    heads_local = width_local // HD
    head_first = lax.axis_index("mp") * heads_local
    own_first = lax.axis_index("mp") * rows_local
    share_rows = momentum_out.shape[0]
    chunks = 2
    chunk_rows = seq_len // chunks

    def chunk_of(rows, chunk):
        return lax.slice_in_dim(rows, chunk * chunk_rows, (chunk + 1) * chunk_rows, axis=0)

    if model_size == 2:
        inputs_other = swap(inputs, "mp", 1)
    weights_qkv = w_qkv.astype(bf16)
    weights_out = w_out.astype(bf16)

    bias_local = lax.dynamic_slice_in_dim(rel_bias, head_first, heads_local, 1)
    bucket_hits = (buckets[:, None] == jnp.arange(rel_bias.shape[0], dtype=jnp.int32)[None, :]).astype(f32)
    bias_table = jnp.dot(bucket_hits, bias_local, precision=highest).T
    skew, skew_back = skew_tables(bias_table)

    if model_size == 2:
        inputs_other = after(inputs_other, skew, weights_qkv, weights_out)
        cot_other = swap(after(cotangent, inputs_other), "mp", 1)
        x_rows = in_order(inputs, inputs_other)
        cot_rows = in_order(cotangent, cot_other)
    else:
        inputs_all = lax.all_gather(inputs, "mp", axis=0, tiled=True)
        cot_other = lax.all_gather(cotangent, "mp", axis=0, tiled=True)
        x_rows = [chunk_of(inputs_all, chunk) for chunk in range(chunks)]
        cot_rows = [chunk_of(cot_other, chunk) for chunk in range(chunks)]
    normed_one, projected = project(x_rows, norm_params, weights_qkv)

    if model_size == 2:
        core_here = lax.axis_index("dp") & 1
        rows_half = weights_out.shape[0] // 2
        piece = lax.dynamic_slice_in_dim(weights_out, core_here * rows_half, rows_half, 0)

    context, totals = [], []
    ahead = projected
    for chunk in range(chunks):
        part, total = attend(ahead, lengths, skew, chunk, chunks)
        context.append(part)
        totals.append(total)
        ahead = after(ahead, part, cot_other)
    if model_size == 2:
        piece = swap(after(piece, cot_other, context[0]), "mp", 1)
        paired = swap(after(piece, context[1]), "dp", 1)
        first = core_here == 0
        weights_other = jnp.concatenate([jnp.where(first, piece, paired), jnp.where(first, paired, piece)], axis=0)
        branch_weights = [weights_out, weights_other]
    else:
        branch_weights = [lax.all_gather(weights_out, "mp", axis=1, tiled=True)]
    contexts = []
    for part in context:
        if model_size == 2:
            contexts.append([part, swap(after(part, *[pair[1] for pair in contexts[-1:]]), "mp", 1)])
        else:
            contexts.append([lax.all_gather(part, "mp", axis=1, tiled=True)])

    ffn = []
    ahead = after(w_ffn, context[-1])
    for chunk in range(chunks):
        ffn.append(
            feed_forward(x_rows[chunk], contexts[chunk], branch_weights, cot_rows[chunk], norm_params, ahead)
        )
        ahead = after(ahead, ffn[-1][4])
    middle, normed_two, hidden, pre_grad, two_part, out_part = zip(*ffn)
    two_other = [other_part(after(two_part[0], contexts[-1][-1]))]
    core = jnp.reshape(lax.axis_index("dp") & 1, (1,))
    order = device_ring(data_size)
    chips = chip_ring(data_size // 2)
    cores = [[2 * chip + core for chip in chips] for core in range(2)]
    units = w_ffn.shape[2]
    (ffn_grad,) = weight_sums(normed_two, pre_grad, order, 2 * units, 0)
    ffn_grad, sent, _ = lax.optimization_barrier((ffn_grad, two_part[1], two_other[0]))
    two_other.append(other_part(sent))
    (ffn_grad,) = weight_sums(cot_rows, hidden, order, 2 * units, units, [ffn_grad])
    ffn_share = sum_over_clips(ffn_grad, [order])

    if model_size == 2:
        out_kept, out_sent = in_order(*out_part)
    else:
        out_got = lax.psum_scatter(jnp.concatenate(out_part), "mp", scatter_dimension=0, tiled=True)
    middle_grad, branch_grad, context_grad = [], [], []

    def middle_step(chunk, *others):
        whole, sent, grad, sums = middle_back(
            after(two_part[chunk], *others), two_other[chunk], middle[chunk], cot_rows[chunk], norm_params, weights_out
        )
        middle_grad.append(whole)
        branch_grad.append(sent)
        context_grad.append(grad)
        return sums

    def back(chunk, others, before=()):
        grad = after(context_grad[chunk], *others)
        return attend_back(projected, grad, context[chunk], totals[chunk], lengths, skew_back, chunk, chunks, before)

    sums_two = [middle_step(0, ffn_grad)]
    *before, diagonal = back(0, [])
    diagonals = [diagonal]
    sums_two.append(middle_step(1, diagonal))
    if model_size == 2:
        out_got = swap(after(out_sent, sums_two[-1]), "mp", 1)
    halves = weight_sums(branch_grad, in_hbm(*context), cores[0] + cores[1], 4 * width_local, 3 * width_local, core=core)
    context_grad[1], *halves = lax.optimization_barrier((context_grad[1], *halves))
    grads, diagonal = back(1, [], before)
    diagonals.append(diagonal)
    sent, kept = weight_sums(
        in_hbm(*normed_one), [in_hbm(after(grads, out_got))], cores[0] + cores[1], 4 * width_local, 0, halves, core=core
    )
    halves = (kept, swap(after(sent, ffn_share), "dp", 1))
    grads = after(grads, kept)

    one = jnp.reshape(own_first * 0, (1,))
    place = one + lax.axis_index("dp")
    scale_factor = 1.0 / math.sqrt(float(seq_len * data_size))
    def attention_sums(*others):
        total = after(halves[0], *others).astype(f32) + halves[1].astype(f32)
        return sum_over_clips(total.astype(bf16), cores)

    if model_size == 2:
        sent, sums_sent = first_back(grads, weights_qkv, inputs_other, rows_local - own_first)
        got = swap(sent, "mp", 1)
        attention_share = attention_sums(sent)
        kept, sums_kept = first_back(after(grads, sent), weights_qkv, inputs, own_first)
        sums_one = [sums_sent, sums_kept]
        own = one + lax.axis_index("mp")
        output_rows = in_order(*[after(rows, kept) for rows in middle])[0] + out_kept.astype(f32) + out_got.astype(f32)
    else:
        sent, sums_sent = first_back(grads, weights_qkv, jnp.concatenate(x_rows), own_first * 0)
        attention_share = attention_sums(sent)
        sums_one = [sums_sent]
        kept = lax.psum_scatter(sent, "mp", scatter_dimension=0, tiled=True)
        got = jnp.zeros_like(kept)
        own = one
        middle_grad = [lax.dynamic_slice_in_dim(jnp.concatenate(middle_grad), own_first, rows_local, 0)] * 2
        middle_own = lax.dynamic_slice_in_dim(jnp.concatenate(middle), own_first, rows_local, 0)
        output_rows = middle_own + out_got.astype(f32)

    reversed_buckets = jnp.pad(buckets[::-1], (0, 1), constant_values=-1)[None, :]
    small = pack_small(sums_one, sums_two, diagonals, reversed_buckets, rel_bias.shape[1], head_first, model_size)
    exchanged = swap(small, "dp", 1)
    ffn_results = update(after(ffn_share, small), [(w_ffn, momentum_ffn, average_ffn)], place, [0.05 * scale_factor])
    small = after(small, ffn_results[0]) + exchanged
    exchanged = swap(small, "dp", 2)
    output = output_rows.astype(bf16)
    small = after(small, output) + exchanged
    exchanged = swap(small, "dp", 4)
    input_grad = finish(got, after(kept, small), inputs, norm_params, middle_grad, own)
    small = after(small, input_grad) + exchanged
    bit = 8
    while bit < data_size:
        small = small + swap(small, "dp", bit)
        bit *= 2
    attention_results = update(
        attention_share,
        [(w_qkv, momentum_qkv, average_qkv), (w_out, momentum_out, average_out)],
        place,
        [0.3 * scale_factor, 0.1 * scale_factor],
    )
    for bit in range(model_size.bit_length() - 1):
        exchanged = swap(small, "mp", 1 << bit)
        small = after(small, attention_results[0]) + exchanged
    small_results = small_update(
        small,
        (norm_params, momentum_norms, average_norms),
        (rel_bias.T, momentum_bias.T, average_bias.T),
        0.05 * scale_factor,
    )
    small_results = [*small_results[:4], *[result.T for result in small_results[4:]]]
    return (output, input_grad, *attention_results, *ffn_results, *small_results)


def solution(mesh):
    return jax.shard_map(
        per_device,
        mesh=mesh,
        in_specs=(
            P(("dp", "mp"), None),
            P(("dp", "mp"), None),
            P("dp"),
            P(),
            P(None, None, "mp"),
            P(None, "mp"),
            P(None, None, "mp"),
            P(),
            P(),
            P(None, "dp", "mp"),
            P("dp", "mp"),
            P(None, "dp", "mp"),
            P(),
            P(),
            P(None, "dp", "mp"),
            P("dp", "mp"),
            P(None, "dp", "mp"),
            P(),
            P(),
        ),
        out_specs=(
            P(("dp", "mp"), None),
            P(("dp", "mp"), None),
            P(None, "dp", "mp"),
            P(None, "dp", "mp"),
            P(None, "dp", "mp"),
            P(None, "dp", "mp"),
            P("dp", "mp"),
            P("dp", "mp"),
            P("dp", "mp"),
            P("dp", "mp"),
            P(None, "dp", "mp"),
            P(None, "dp", "mp"),
            P(None, "dp", "mp"),
            P(None, "dp", "mp"),
            P(),
            P(),
            P(),
            P(),
            P(),
            P(),
            P(),
            P(),
        ),
        check_vma=False,
    )
```

```python
import math

import jax
import jax.numpy as jnp
from jax import lax
from jax.experimental import pallas as pl
from jax.experimental.pallas import tpu as pltpu
from jax.sharding import PartitionSpec as P

HD = 64
PAIR = 2 * HD
QB = 128
QUERY_BLOCK = 512
KEY_BLOCK = 512
f32 = jnp.float32
bf16 = jnp.bfloat16
ROWS_BY_ROWS = (((1,), (1,)), ((), ()))
COLS_BY_COLS = (((0,), (0,)), ((), ()))
VMEM_LIMIT = 56 * 2**20

highest = lax.Precision.HIGHEST
momentum_keep = 0.5
average_keep = 0.5
SHARE = 1.1e6


def cost(microseconds):
    return pl.CostEstimate(flops=0, bytes_accessed=int(SHARE * microseconds), transcendentals=0)


def in_hbm(*values):
    values = [pltpu.with_memory_space_constraint(value, pltpu.HBM) for value in values]
    return values if len(values) > 1 else values[0]


def skew_kernel(forward_ref, reverse_ref, forward_out, reverse_out):
    width = forward_ref.shape[2]
    for source, result in ((forward_ref, forward_out), (reverse_ref, reverse_out)):
        rows = jnp.broadcast_to(source[0], (QB, width))
        result[0] = pltpu.roll(rows, width - (QB - 1), 1, stride=1, stride_axis=0)[:, : width - QB]


def skew_tables(table):
    heads, width = table.shape
    forward = jnp.pad(table, ((0, 0), (0, 1)))[:, None, :]
    reverse = jnp.pad(table[:, ::-1], ((0, 0), (0, 1)))[:, None, :]
    width += 1
    row = pl.BlockSpec((1, 1, width), lambda h: (h, 0, 0))
    skewed = pl.BlockSpec((1, QB, width - QB), lambda h: (h, 0, 0))
    shape = jax.ShapeDtypeStruct((heads, QB, width - QB), f32)
    return pl.pallas_call(
        skew_kernel,
        grid=(heads,),
        in_specs=[row, row],
        out_specs=[skewed, skewed],
        out_shape=[shape, shape],
        cost_estimate=cost(8),
        name="skew",
    )(forward, reverse)


def three_parts(values):
    first = values.astype(bf16).astype(f32)
    rest = values - first
    second = rest.astype(bf16).astype(f32)
    return (first, second, rest - second)


def own_lanes(lane, head):
    return (lane >= HD) if head else (lane < HD)


def key_side(keys, mask, lane, head):
    first = 0 if head else HD
    extra = jnp.where(lane == first, mask, jnp.where((lane > first) & (lane < first + 4), 1.0, 0.0))
    return jnp.where(own_lanes(lane, head), keys, extra).astype(bf16)


def forward_kernel(
    first_row,
    length_ref,
    q_ref,
    k_ref,
    v_ref,
    skew_ref,
    context_ref,
    total_ref,
    key_ref,
    value_ref,
    raised_ref,
):
    seq_len = k_ref.shape[0]
    rows_here = q_ref.shape[0]
    lane = lax.broadcasted_iota(jnp.int32, (seq_len, PAIR), 1)
    place = lax.broadcasted_iota(jnp.int32, (seq_len, PAIR), 0)
    mask = jnp.where(place < length_ref[0], 0.0, -1e9)
    keys = k_ref[...].astype(f32)
    values = v_ref[...].astype(f32)
    for head in range(2):
        key_ref[head] = key_side(keys, mask, lane, head)
        value_ref[head] = jnp.where(own_lanes(lane, head), values, 1.0).astype(bf16)
    here = min(QUERY_BLOCK, rows_here)
    lane = lax.broadcasted_iota(jnp.int32, (here, PAIR), 1)

    def block(index, carry):
        rows = pl.ds(pl.multiple_of(index * here, here), here)
        queries = q_ref[rows, :].astype(f32) * 0.125
        context = []
        totals = []
        for head in range(2):
            own = own_lanes(lane, head)
            first = 0 if head else HD
            query = jnp.where(own, queries, jnp.where(lane == first, 1.0, 0.0)).astype(bf16)
            scores = lax.dot_general(query, key_ref[head], ROWS_BY_ROWS, preferred_element_type=f32)
            tops = []
            for piece in range(0, here, QB):
                start = pl.multiple_of(seq_len - QB - first_row - index * here - piece, QB)
                moved = scores[piece : piece + QB] + skew_ref[head, :, pl.ds(start, seq_len)]
                top = jnp.max(moved, axis=1, keepdims=True)
                raised_ref[head, piece : piece + QB, :] = jnp.exp(moved - top).astype(bf16)
                tops.append(top)
            weighted = jnp.dot(raised_ref[head], value_ref[head], preferred_element_type=f32)
            context.append(weighted / weighted[:, first : first + 1])
            totals.append(jnp.concatenate(tops, axis=0) + jnp.log(jnp.where(own, 1.0, weighted)))
        context_ref[rows, :] = jnp.where(lane < HD, context[0], context[1]).astype(bf16)
        total_ref[rows, :] = jnp.where(lane < HD, totals[1], totals[0])
        return carry

    lax.fori_loop(0, rows_here // here, block, 0, unroll=True)


def attend(projected, lengths, skew, chunk, chunks):
    _, seq_len, width = projected.shape
    rows_here = seq_len // chunks
    whole = [pl.BlockSpec((None, seq_len, PAIR), lambda p, t=t: (t, 0, p)) for t in (1, 2)]
    part = pl.BlockSpec((rows_here, PAIR), lambda p: (0, p))
    return pl.pallas_call(
        lambda *refs: forward_kernel(chunk * rows_here, *refs),
        grid=(width // PAIR,),
        in_specs=[
            pl.BlockSpec(memory_space=pltpu.SMEM),
            pl.BlockSpec((None, rows_here, PAIR), lambda p: (0, chunk, p)),
            *whole,
            pl.BlockSpec((2,) + skew.shape[1:], lambda p: (p, 0, 0)),
        ],
        out_specs=[part, part],
        out_shape=[
            jax.ShapeDtypeStruct((rows_here, width), bf16),
            jax.ShapeDtypeStruct((rows_here, width), f32),
        ],
        scratch_shapes=[
            pltpu.VMEM((2, seq_len, PAIR), bf16),
            pltpu.VMEM((2, seq_len, PAIR), bf16),
            pltpu.VMEM((2, min(QUERY_BLOCK, rows_here), seq_len), bf16),
        ],
        compiler_params=pltpu.CompilerParams(vmem_limit_bytes=24 * 2**20),
        cost_estimate=cost(13),
        name="attend",
    )(lengths, projected, projected, projected, in_hbm(skew))


def diagonal_sums(skewed):
    width = skewed.shape[1]
    total = pltpu.roll(skewed[:8], QB - 1, 1)
    for group in range(1, QB // 8):
        total = total + pltpu.roll(skewed[8 * group : 8 * group + 8], QB - 1 - 8 * group, 1)
    row = lax.broadcasted_iota(jnp.int32, total.shape, 0)
    for bit in (1, 2, 4):
        total = jnp.where((row & bit) != 0, pltpu.roll(total, width - bit, 1), total)
    return jnp.sum(total, axis=0, keepdims=True)


def backward_kernel(first_row, last, *refs):
    (length_ref, q_ref, k_ref, v_ref, grad_ref, context_ref, total_ref, skew_ref) = refs[:8]
    running = last and first_row > 0
    if running:
        dq_before, dk_before, dv_before = refs[8:11]
    if last:
        grads_ref, diagonal_ref = refs[-8:-6]
        dq_ref = grads_ref.at[0, pl.ds(first_row, q_ref.shape[0]), :]
        dk_ref, dv_ref = grads_ref.at[1], grads_ref.at[2]
    else:
        dq_ref, dk_ref, dv_ref, diagonal_ref = refs[-10:-6]
    (query_ref, back_ref, skewed_ref, dq_sum, soft_ref, slope_ref) = refs[-6:]
    if running:
        grads_ref[0, :first_row, :] = dq_before[...]
    seq_len = k_ref.shape[0]
    rows_here = q_ref.shape[0]
    lane = lax.broadcasted_iota(jnp.int32, (rows_here, PAIR), 1)
    queries = q_ref[...].astype(f32) * 0.125
    back = grad_ref[...].astype(f32)
    dots = back * context_ref[...].astype(f32)
    first_lane = lax.broadcasted_iota(jnp.int32, (PAIR, PAIR), 0) // HD
    cross = jnp.where(first_lane != lax.broadcasted_iota(jnp.int32, (PAIR, PAIR), 1) // HD, 1.0, 0.0).astype(bf16)
    row_dot = sum(jnp.dot(part.astype(bf16), cross, preferred_element_type=f32) for part in three_parts(dots)[:2])
    tops = three_parts(-total_ref[...])
    drops = three_parts(-row_dot)
    for head in range(2):
        own = own_lanes(lane, head)
        first = 0 if head else HD
        query = jnp.where(lane == first, 1.0, 0.0)
        graded = jnp.zeros_like(query)
        for i in range(3):
            query = jnp.where(lane == first + 1 + i, tops[i], query)
            graded = jnp.where(lane == first + 1 + i, drops[i], graded)
        query_ref[head] = jnp.where(own, queries, query).astype(bf16)
        back_ref[head] = jnp.where(own, back, graded).astype(bf16)
    skewed_ref[...] = jnp.zeros_like(skewed_ref)
    keys_here = soft_ref.shape[1]
    small_lane = lax.broadcasted_iota(jnp.int32, (keys_here, PAIR), 1)
    small_row = lax.broadcasted_iota(jnp.int32, (keys_here, PAIR), 0)

    def block(index, carry):
        rows = pl.ds(pl.multiple_of(index * keys_here, keys_here), keys_here)
        keys = k_ref[rows, :].astype(f32)
        values = v_ref[rows, :].astype(f32)
        mask = jnp.where(small_row + index * keys_here < length_ref[0], 0.0, -1e9)
        dq, dk, dv = [], [], []
        for head in range(2):
            key = key_side(keys, mask, small_lane, head)
            value = key_side(values, 0.0, small_lane, head)
            scores = lax.dot_general(key, query_ref[head], ROWS_BY_ROWS, preferred_element_type=f32)
            drop = lax.dot_general(value, back_ref[head], ROWS_BY_ROWS, preferred_element_type=f32)
            for first in range(0, keys_here, QB):
                piece = slice(first, first + QB)
                start = pl.multiple_of(seq_len - QB + first_row - index * keys_here - first, QB)
                soft = jnp.exp(scores[piece] + skew_ref[head, :, pl.ds(start, rows_here)])
                score_grad = soft * drop[piece]
                skewed_ref[head, :, pl.ds(start, rows_here)] += score_grad
                soft_ref[head, piece, :] = soft.astype(bf16)
                slope_ref[head, piece, :] = score_grad.astype(bf16)
            dv.append(jnp.dot(soft_ref[head], back_ref[head], preferred_element_type=f32))
            dk.append(jnp.dot(slope_ref[head], query_ref[head], preferred_element_type=f32))
            dq.append(lax.dot_general(slope_ref[head], key, COLS_BY_COLS, preferred_element_type=f32))
        dk = jnp.where(small_lane < HD, dk[0], dk[1])
        dv = jnp.where(small_lane < HD, dv[0], dv[1])
        if running:
            dk = dk + dk_before[rows, :]
            dv = dv + dv_before[rows, :]
        dk_ref[rows, :] = dk.astype(dk_ref.dtype)
        dv_ref[rows, :] = dv.astype(dv_ref.dtype)
        dq = jnp.where(lane < HD, dq[0], dq[1])

        @pl.when(index == 0)
        def _():
            dq_sum[...] = dq

        @pl.when(index > 0)
        def _():
            dq_sum[...] += dq

        return carry

    lax.fori_loop(0, seq_len // keys_here, block, 0, unroll=True)
    dq_ref[...] = (dq_sum[...] * 0.125).astype(bf16)
    for head in range(2):
        diagonal_ref[head] = diagonal_sums(jnp.concatenate([skewed_ref[head], jnp.zeros((QB, QB), f32)], axis=1))


def attend_back(projected, context_grad, context, totals, lengths, skew, chunk, chunks, before=()):
    _, seq_len, width = projected.shape
    pairs = width // PAIR
    rows_here = seq_len // chunks
    key_block = min(KEY_BLOCK, seq_len)
    skew_width = skew.shape[2]
    whole = [pl.BlockSpec((None, seq_len, PAIR), lambda p, t=t: (t, 0, p)) for t in (1, 2)]
    part = pl.BlockSpec((rows_here, PAIR), lambda p: (0, p))
    full = pl.BlockSpec((seq_len, PAIR), lambda p: (0, p))
    last = chunk == chunks - 1
    if last:
        out_specs = [pl.BlockSpec((3, seq_len, PAIR), lambda p: (0, 0, p))]
        out_shape = [pltpu.HBM((3, seq_len, width), bf16)]
    else:
        out_specs = [part, full, full]
        out_shape = [jax.ShapeDtypeStruct((rows_here, width), bf16)] + [jax.ShapeDtypeStruct((seq_len, width), f32)] * 2
    return pl.pallas_call(
        lambda *refs: backward_kernel(chunk * rows_here, last, *refs),
        grid=(pairs,),
        in_specs=[
            pl.BlockSpec(memory_space=pltpu.SMEM),
            pl.BlockSpec((None, rows_here, PAIR), lambda p: (0, chunk, p)),
            *whole,
            part,
            part,
            part,
            pl.BlockSpec((2, QB, skew_width), lambda p: (p, 0, 0)),
            *[part, full, full][: len(before)],
        ],
        out_specs=out_specs + [pl.BlockSpec((2, 1, skew_width + QB), lambda p: (p, 0, 0))],
        out_shape=out_shape + [jax.ShapeDtypeStruct((width // HD, 1, skew_width + QB), f32)],
        scratch_shapes=[
            pltpu.VMEM((2, rows_here, PAIR), bf16),
            pltpu.VMEM((2, rows_here, PAIR), bf16),
            pltpu.VMEM((2, QB, skew_width), f32),
            pltpu.VMEM((rows_here, PAIR), f32),
            pltpu.VMEM((2, key_block, rows_here), bf16),
            pltpu.VMEM((2, key_block, rows_here), bf16),
        ],
        compiler_params=pltpu.CompilerParams(vmem_limit_bytes=28 * 2**20),
        cost_estimate=cost(18),
        name="attend_back",
    )(lengths, *in_hbm(projected, projected, projected, context_grad, context, totals, skew, *before))


def unit(values):
    row_mean = jnp.mean(values, axis=-1, keepdims=True)
    centered = values - row_mean
    spread = jnp.mean(centered * centered, axis=-1, keepdims=True)
    inverse = lax.rsqrt(spread + 1e-05)
    return (centered * inverse, inverse)


def ffn_kernel(parts, pieces, core_ref, x_ref, *refs):
    contexts, weights, refs = refs[:parts], refs[parts : parts + pieces], refs[parts + pieces :]
    (cot_ref, norm_ref, up_ref, down_ref), refs = refs[:4], refs[4:]
    (middle_ref, normed_ref, hidden_ref, pre_ref, grad_ref, out_ref, grad_sum, out_sum) = refs
    step = pl.program_id(0)

    @pl.when(step == 0)
    def _():
        whole = [weight[...] for weight in weights]
        if pieces > parts:
            first = core_ref[0] == 0
            here, there = whole[-2:]
            whole[-2:] = [jnp.concatenate([jnp.where(first, here, there), jnp.where(first, there, here)], axis=0)]
        branch = [
            lax.dot_general(context[...], weight, ROWS_BY_ROWS, preferred_element_type=f32)
            for context, weight in zip(contexts, whole)
        ]
        middle = x_ref[...].astype(f32) + sum(branch[1:], branch[0])
        middle_ref[...] = middle
        normed_ref[...] = (unit(middle)[0] * norm_ref[2:3, :] + norm_ref[3:4, :]).astype(bf16)
        grad_sum[...] = jnp.zeros_like(grad_sum)
        out_sum[...] = jnp.zeros_like(out_sum)

    up = up_ref[...].astype(bf16)
    down = down_ref[...].astype(bf16)
    block = min(512, x_ref.shape[0])
    for first in range(0, x_ref.shape[0], block):
        rows = pl.ds(first, block)
        hidden_pre = jnp.dot(normed_ref[rows, :], up, preferred_element_type=f32)
        hidden_grad = jnp.dot(cot_ref[rows, :], down, preferred_element_type=f32)
        gate = 0.5 + 0.5 * lax.erf(hidden_pre * 0.7071067811865476)
        slope = gate + hidden_pre * (0.3989422804014327 * jnp.exp(-0.5 * hidden_pre * hidden_pre))
        hidden = (hidden_pre * gate).astype(bf16)
        pre_grad = (hidden_grad * slope).astype(bf16)
        hidden_ref[rows, :] = hidden
        pre_ref[rows, :] = pre_grad
        grad_sum[rows, :] += lax.dot_general(pre_grad, up, ROWS_BY_ROWS, preferred_element_type=f32)
        out_sum[rows, :] += lax.dot_general(hidden, down, ROWS_BY_ROWS, preferred_element_type=f32)

    @pl.when(step == pl.num_programs(0) - 1)
    def _():
        grad_ref[...] = grad_sum[...].astype(bf16)
        out_ref[...] = out_sum[...].astype(bf16)


def feed_forward(x_rows, contexts, weights_out, cot_rows, norm_params, weights_ffn, core):
    rows, width = x_rows.shape
    units = weights_ffn.shape[2]
    tile = min(512, units)
    whole = pl.BlockSpec((rows, width), lambda f: (0, 0))
    tall = pl.BlockSpec((rows, tile), lambda f: (0, f))
    return pl.pallas_call(
        lambda *refs: ffn_kernel(len(contexts), len(weights_out), *refs),
        grid=(units // tile,),
        in_specs=[
            pl.BlockSpec(memory_space=pltpu.SMEM),
            whole,
            *[pl.BlockSpec(x.shape, lambda f: (0, 0)) for x in [*contexts, *weights_out]],
            whole,
            pl.BlockSpec(norm_params.shape, lambda f: (0, 0)),
            pl.BlockSpec((None, width, tile), lambda f: (0, 0, f)),
            pl.BlockSpec((None, width, tile), lambda f: (1, 0, f)),
        ],
        out_specs=[whole, whole, tall, tall, whole, whole],
        out_shape=[
            pltpu.HBM((rows, width), f32),
            jax.ShapeDtypeStruct((rows, width), bf16),
            jax.ShapeDtypeStruct((rows, units), bf16),
            jax.ShapeDtypeStruct((rows, units), bf16),
            jax.ShapeDtypeStruct((rows, width), bf16),
            jax.ShapeDtypeStruct((rows, width), bf16),
        ],
        scratch_shapes=[pltpu.VMEM((rows, width), f32)] * 2,
        compiler_params=pltpu.CompilerParams(vmem_limit_bytes=38 * 2**20),
        cost_estimate=cost(17.5),
        name="feed_forward",
    )(core, x_rows, *contexts, *weights_out, cot_rows, norm_params, weights_ffn, weights_ffn)


def chip_ring(count):
    if count % 4:
        return list(range(count))
    rows, columns = 4, count // 4
    chips = [(row, 0) for row in range(rows)]
    for turn, row in enumerate(range(rows - 1, -1, -1)):
        across = [(row, column) for column in range(1, columns)]
        chips += across[::-1] if turn % 2 else across
    return [row * columns + column for row, column in chips]


def device_ring(size):
    chips = chip_ring(size // 2)
    return [2 * chip + core for turn, chip in enumerate(chips) for core in ((0, 1), (1, 0))[turn % 2]]


def weight_kernel(order, chunks, halves, core_ref, *refs):
    lefts, rights = refs[:chunks], refs[chunks : 2 * chunks]
    results, left_ref = refs[-1 - halves : -1], refs[-1]
    rows, features = lefts[0].shape
    share = features // len(order)
    part = features // halves

    @pl.when(pl.program_id(0) == 0)
    def _():
        for chunk in range(chunks):
            turned = lefts[chunk][...].T
            for position, block in enumerate(order):
                half, first = divmod(position * share, part)
                if halves == 2:
                    half = jnp.where(core_ref[0] == half, 1, 0)
                left_ref[half, first : first + share, chunk * rows : (chunk + 1) * rows] = turned[
                    block * share : (block + 1) * share
                ]

    left = left_ref[...].reshape(features, chunks * rows)
    total = 0.0
    for chunk in range(chunks):
        piece = left[:, chunk * rows : (chunk + 1) * rows]
        total = total + jnp.dot(piece, rights[chunk][...], preferred_element_type=f32)
    for half, result in enumerate(results):
        result[...] = total[half * part : (half + 1) * part].astype(bf16)


def weight_sums(lefts, rights, order, columns, first, before=(), core=None):
    chunks = len(lefts)
    rows, features = lefts[0].shape
    halves = 1 if core is None else 2
    if len(rights) == chunks:
        tile = min(512, rights[0].shape[1])
        steps = rights[0].shape[1] // tile
        right_specs = [pl.BlockSpec((rows, tile), lambda c: (0, c))] * chunks
    else:
        steps, _, tile = rights[0].shape
        right_specs = [pl.BlockSpec((None, rows, tile), lambda c, k=k: (c, k, 0)) for k in range(chunks)]
        rights = rights * chunks
    return pl.pallas_call(
        lambda *refs: weight_kernel(order, chunks, halves, *refs),
        grid=(steps,),
        in_specs=[pl.BlockSpec(memory_space=pltpu.SMEM)]
        + [pl.BlockSpec((rows, features), lambda c: (0, 0))] * chunks
        + right_specs
        + [pl.BlockSpec(memory_space=pl.ANY)] * len(before),
        out_specs=[pl.BlockSpec((features // halves, tile), lambda c: (0, c + first // tile))] * halves,
        out_shape=[pltpu.HBM((features // halves, columns), bf16)] * halves,
        input_output_aliases={1 + 2 * chunks + half: half for half in range(len(before))},
        scratch_shapes=[pltpu.VMEM((halves, features // halves, rows * chunks), bf16)],
        compiler_params=pltpu.CompilerParams(vmem_limit_bytes=20 * 2**20),
        cost_estimate=cost(2 * steps + 1),
        name="weight_sums",
    )(jnp.zeros((1,), jnp.int32) if core is None else core, *lefts, *rights, *before)


def middle_kernel(part_ref, other_ref, middle_ref, cot_ref, norm_ref, weight_ref, grad_ref, branch_ref, context_ref, sums_ref):
    grad = part_ref[...].astype(f32) + other_ref[...].astype(f32)
    rows, inverse = unit(middle_ref[...])
    grad_unit = grad * norm_ref[2:3, :]
    first_mean = jnp.mean(grad_unit, axis=-1, keepdims=True)
    second_mean = jnp.mean(grad_unit * rows, axis=-1, keepdims=True)
    whole = cot_ref[...].astype(f32) + inverse * (grad_unit - first_mean - rows * second_mean)
    grad_ref[...] = whole
    branch_ref[...] = whole.astype(bf16)
    context_ref[...] = jnp.dot(branch_ref[...], weight_ref[...], preferred_element_type=f32).astype(bf16)
    gain = jnp.sum(grad * rows, axis=0, keepdims=True)
    shift = jnp.sum(grad, axis=0, keepdims=True)

    @pl.when(pl.program_id(0) == 0)
    def _():
        sums_ref[0:1, :] = gain
        sums_ref[1:2, :] = shift

    @pl.when(pl.program_id(0) > 0)
    def _():
        sums_ref[0:1, :] += gain
        sums_ref[1:2, :] += shift


def middle_back(part, other, middle, cot_rows, norm_params, weights_out):
    rows, width = part.shape
    block = min(256, rows)
    columns = weights_out.shape[1]
    piece = pl.BlockSpec((block, width), lambda r: (r, 0))
    return pl.pallas_call(
        middle_kernel,
        grid=(rows // block,),
        in_specs=[
            piece,
            piece,
            piece,
            piece,
            pl.BlockSpec(norm_params.shape, lambda r: (0, 0)),
            pl.BlockSpec(weights_out.shape, lambda r: (0, 0)),
        ],
        out_specs=[piece, piece, pl.BlockSpec((block, columns), lambda r: (r, 0)), pl.BlockSpec((2, width), lambda r: (0, 0))],
        out_shape=[
            pltpu.HBM((rows, width), f32),
            jax.ShapeDtypeStruct((rows, width), bf16),
            pltpu.HBM((rows, columns), bf16),
            jax.ShapeDtypeStruct((2, width), f32),
        ],
        compiler_params=pltpu.CompilerParams(vmem_limit_bytes=14 * 2**20),
        cost_estimate=cost(6),
        name="middle_back",
    )(part, other, middle, cot_rows, norm_params, weights_out)


def first_kernel(place_ref, grads_ref, weight_ref, x_ref, part_ref, sums_ref):
    left = jnp.concatenate([grads_ref[t] for t in range(3)], axis=1)
    right = jnp.concatenate([weight_ref[t] for t in range(3)], axis=1)
    part = lax.dot_general(left, right, ROWS_BY_ROWS, preferred_element_type=f32)
    part_ref[...] = part.astype(bf16)
    sums_ref[0:1, :] = jnp.sum(part * unit(x_ref[...].astype(f32))[0], axis=0, keepdims=True)
    sums_ref[1:2, :] = jnp.sum(part, axis=0, keepdims=True)


def first_back(grads, weights_qkv, x_rows, first_row):
    rows, width = x_rows.shape
    columns = grads.shape[2]
    return pl.pallas_call(
        first_kernel,
        grid_spec=pltpu.PrefetchScalarGridSpec(
            num_scalar_prefetch=1,
            grid=(1,),
            in_specs=[
                pl.BlockSpec((3, rows, columns), lambda r, place: (0, place[0], 0)),
                pl.BlockSpec(weights_qkv.shape, lambda r, place: (0, 0, 0)),
                pl.BlockSpec((rows, width), lambda r, place: (0, 0)),
            ],
            out_specs=[pl.BlockSpec((rows, width), lambda r, place: (0, 0)), pl.BlockSpec((2, width), lambda r, place: (0, 0))],
        ),
        out_shape=[jax.ShapeDtypeStruct((rows, width), bf16), jax.ShapeDtypeStruct((2, width), f32)],
        compiler_params=pltpu.CompilerParams(vmem_limit_bytes=20 * 2**20),
        cost_estimate=cost(6),
        name="first_back",
    )(jnp.reshape(first_row // rows, (1,)), *in_hbm(grads, weights_qkv, x_rows))


def project_kernel(chunks, *refs):
    xs, (norm_ref, weight_ref), normed_refs, result_ref = refs[:chunks], refs[chunks:][:2], refs[chunks + 2 : -1], refs[-1]
    rows = xs[0].shape[0]
    block = min(256, rows)
    for chunk in range(chunks):
        for first in range(0, rows, block):
            at = pl.ds(first, block)
            values = xs[chunk][at, :].astype(f32)
            normed = (unit(values)[0] * norm_ref[0:1, :] + norm_ref[1:2, :]).astype(bf16)
            normed_refs[chunk][at, :] = normed
            for t in range(3):
                product = jnp.dot(normed, weight_ref[t], preferred_element_type=f32)
                result_ref[t, pl.ds(chunk * rows + first, block), :] = product.astype(bf16)


def project(x_rows, norm_params, weights_qkv):
    chunks = len(x_rows)
    rows, width = x_rows[0].shape
    columns = weights_qkv.shape[2]
    *normed, result = pl.pallas_call(
        lambda *refs: project_kernel(chunks, *refs),
        out_shape=[jax.ShapeDtypeStruct((rows, width), bf16)] * chunks
        + [jax.ShapeDtypeStruct((3, rows * chunks, columns), bf16)],
        compiler_params=pltpu.CompilerParams(vmem_limit_bytes=24 * 2**20),
        cost_estimate=cost(8),
        name="project",
    )(*x_rows, norm_params, weights_qkv)
    return (normed, result)


def updated(weight, momentum, average, gradient, step_rate):
    next_moment = momentum_keep * momentum + gradient
    next_weight = weight - step_rate * (gradient + momentum_keep * next_moment)
    next_average = average_keep * average + (1.0 - average_keep) * next_weight
    return (gradient, next_moment, next_weight, next_average)


def update_kernel(counts, rates, place_ref, grad_ref, *refs):
    states, results = refs[: 3 * len(counts)], refs[3 * len(counts) :]
    block = 0
    for i, (count, rate) in enumerate(zip(counts, rates)):
        state, result = states[3 * i : 3 * i + 3], results[4 * i : 4 * i + 4]
        width = state[0].shape[-1]
        for t in range(count):
            at = (t,) if len(state[0].shape) == 3 else ()
            gradient = grad_ref[:, block * width : (block + 1) * width].astype(f32)
            block += 1
            for ref, value in zip(result, updated(*[ref[at + (Ellipsis,)] for ref in state], gradient, rate)):
                ref[at + (Ellipsis,)] = value


def update(gradient, states, place, rates):
    counts, in_specs, out_specs, out_shape = [], [], [], []
    for _, momentum, _ in states:
        shape = momentum.shape
        counts.append(shape[0] if len(shape) == 3 else 1)
        if len(shape) == 3:
            share = pl.BlockSpec(shape, lambda i, place: (0, 0, 0))
            in_specs += [pl.BlockSpec(shape, lambda i, place: (0, place[0], 0)), share, share]
        else:
            share = pl.BlockSpec(shape, lambda i, place: (0, 0))
            in_specs += [pl.BlockSpec(shape, lambda i, place: (place[0], 0)), share, share]
        out_specs += [share] * 4
        out_shape += [jax.ShapeDtypeStruct(shape, f32)] * 4
    return pl.pallas_call(
        lambda *refs: update_kernel(counts, rates, *refs),
        grid_spec=pltpu.PrefetchScalarGridSpec(
            num_scalar_prefetch=1,
            grid=(1,),
            in_specs=[pl.BlockSpec(gradient.shape, lambda i, place: (0, 0))] + in_specs,
            out_specs=out_specs,
        ),
        out_shape=out_shape,
        compiler_params=pltpu.CompilerParams(vmem_limit_bytes=20 * 2**20),
        cost_estimate=cost(4),
        name="update",
    )(place, gradient, *[in_hbm(x) for state in states for x in state])


def pack_kernel(shares, counts, head_ref, buckets_ref, *refs):
    result_ref = refs[-1]
    one, two, diagonals = refs[: counts[0]], refs[counts[0] : sum(counts[:2])], refs[sum(counts[:2]) : -1]
    norms = [sum(ref[...] for ref in one), sum(ref[...] for ref in two) * (1.0 / shares)]
    rows = jnp.concatenate(norms, axis=0)
    for i in range(rows.shape[1] // 128):
        result_ref[4 * i : 4 * i + 4, :] = rows[:, 128 * i : 128 * i + 128]
    offsets = sum(ref[:, 0, :] for ref in diagonals)
    first = rows.shape[1] // 32
    heads = result_ref.shape[0] - first
    bins = lax.broadcasted_iota(jnp.int32, (128, offsets.shape[1]), 0)
    hits = (buckets_ref[...] == bins).astype(f32)
    sums = lax.dot_general(offsets, hits, ROWS_BY_ROWS, precision=highest, preferred_element_type=f32)
    if sums.shape[0] < heads:
        sums = jnp.concatenate([sums, jnp.zeros((heads - sums.shape[0], 128), f32)], axis=0)
    result_ref[first:, :] = pltpu.roll(sums, head_ref[0], 0)


def pack_small(one, two, diagonals, buckets, heads, head_first, shares):
    width = one[0].shape[1]
    return pl.pallas_call(
        lambda *refs: pack_kernel(shares, (len(one), len(two)), *refs),
        in_specs=[pl.BlockSpec(memory_space=pltpu.SMEM)]
        + [pl.BlockSpec(memory_space=pltpu.VMEM)] * (1 + len(one) + len(two) + len(diagonals)),
        out_shape=jax.ShapeDtypeStruct((width // 32 + heads, 128), f32),
        cost_estimate=cost(2),
        name="pack_small",
    )(jnp.reshape(head_first, (1,)), buckets, *one, *two, *diagonals)


def small_update_kernel(rate, small_ref, *refs):
    norm_state, bias_state, results = refs[:3], refs[3:6], refs[6:]
    width = norm_state[0].shape[1]
    gradient = jnp.concatenate([small_ref[4 * i : 4 * i + 4, :] for i in range(width // 128)], axis=1)
    for result, value in zip(results[:4], updated(*[ref[...] for ref in norm_state], gradient, rate)):
        result[...] = value
    gradient = small_ref[width // 32 :, : bias_state[0].shape[1]]
    for result, value in zip(results[4:], updated(*[ref[...] for ref in bias_state], gradient, rate)):
        result[...] = value


def small_update(small, norm_state, bias_state, rate):
    return pl.pallas_call(
        lambda *refs: small_update_kernel(rate, *refs),
        out_shape=[jax.ShapeDtypeStruct(norm_state[0].shape, f32)] * 4
        + [jax.ShapeDtypeStruct(bias_state[0].shape, f32)] * 4,
        cost_estimate=cost(1.5),
        name="small_update",
    )(small, *norm_state, *bias_state)


def finish_kernel(place_ref, x_ref, norm_ref, sent_ref, kept_ref, first_ref, second_ref, result_ref):
    chosen = jnp.where(place_ref[0] == 0, first_ref[...], second_ref[...])
    grad = sent_ref[...].astype(f32) + kept_ref[...].astype(f32)
    rows, inverse = unit(x_ref[...].astype(f32))
    grad_unit = grad * norm_ref[0:1, :]
    first_mean = jnp.mean(grad_unit, axis=-1, keepdims=True)
    second_mean = jnp.mean(grad_unit * rows, axis=-1, keepdims=True)
    result_ref[...] = chosen + inverse * (grad_unit - first_mean - rows * second_mean)


def finish(got, kept, x_rows, norm_params, middle_grad, place):
    rows, width = x_rows.shape
    piece = pl.BlockSpec((rows // 2, width), lambda r, place: (r, 0))
    chosen = [
        pl.BlockSpec((rows // 2, width), lambda r, place: (jnp.where(place[0] == 0, r, 0), 0)),
        pl.BlockSpec((rows // 2, width), lambda r, place: (jnp.where(place[0] == 0, 0, r), 0)),
    ]
    return pl.pallas_call(
        finish_kernel,
        grid_spec=pltpu.PrefetchScalarGridSpec(
            num_scalar_prefetch=1,
            grid=(2,),
            in_specs=[piece, pl.BlockSpec(norm_params.shape, lambda r, place: (0, 0)), piece, piece] + chosen,
            out_specs=piece,
        ),
        out_shape=jax.ShapeDtypeStruct((rows, width), f32),
        compiler_params=pltpu.CompilerParams(vmem_limit_bytes=14 * 2**20),
        cost_estimate=cost(5),
        name="finish",
    )(place, in_hbm(x_rows), norm_params, *in_hbm(got, kept, *middle_grad))


def after(value, *others):
    return lax.optimization_barrier((value,) + others)[0]


def swap(values, axis, bit):
    size = lax.axis_size(axis)
    return lax.ppermute(values, axis, [(i, i ^ bit) for i in range(size)])


def in_order(own, other):
    first = lax.axis_index("mp") == 0
    return [jnp.where(first, own, other), jnp.where(first, other, own)]


def other_part(rows):
    if lax.axis_size("mp") != 2:
        return (lax.psum(rows.astype(f32), "mp") - rows.astype(f32)).astype(bf16)
    return swap(rows, "mp", 1)


def sum_own(sent, kept):
    return kept.astype(f32) + swap(sent, "mp", 1).astype(f32)


def sum_over_clips(gradient, groups):
    return lax.psum_scatter(gradient, "dp", scatter_dimension=0, tiled=True, axis_index_groups=groups)


def per_device(
    inputs,
    cotangent,
    lengths,
    buckets,
    w_qkv,
    w_out,
    w_ffn,
    norm_params,
    rel_bias,
    momentum_qkv,
    momentum_out,
    momentum_ffn,
    momentum_norms,
    momentum_bias,
    average_qkv,
    average_out,
    average_ffn,
    average_norms,
    average_bias,
):
    model_size = lax.axis_size("mp")
    data_size = lax.axis_size("dp")
    rows_local = inputs.shape[0]
    seq_len = rows_local * model_size
    width_local = w_qkv.shape[2]
    heads_local = width_local // HD
    head_first = lax.axis_index("mp") * heads_local
    own_first = lax.axis_index("mp") * rows_local
    share_rows = momentum_out.shape[0]
    chunks = 2
    chunk_rows = seq_len // chunks

    def chunk_of(rows, chunk):
        return lax.slice_in_dim(rows, chunk * chunk_rows, (chunk + 1) * chunk_rows, axis=0)

    if model_size == 2:
        inputs_other = swap(inputs, "mp", 1)
    weights_qkv = w_qkv.astype(bf16)
    weights_out = w_out.astype(bf16)

    bias_local = lax.dynamic_slice_in_dim(rel_bias, head_first, heads_local, 1)
    bucket_hits = (buckets[:, None] == jnp.arange(rel_bias.shape[0], dtype=jnp.int32)[None, :]).astype(f32)
    bias_table = jnp.dot(bucket_hits, bias_local, precision=highest).T
    skew, skew_back = skew_tables(bias_table)

    if model_size == 2:
        inputs_other = after(inputs_other, skew, weights_qkv, weights_out)
        cot_other = swap(after(cotangent, inputs_other), "mp", 1)
        x_rows = in_order(inputs, inputs_other)
        cot_rows = in_order(cotangent, cot_other)
    else:
        inputs_all = lax.all_gather(inputs, "mp", axis=0, tiled=True)
        cot_other = lax.all_gather(cotangent, "mp", axis=0, tiled=True)
        x_rows = [chunk_of(inputs_all, chunk) for chunk in range(chunks)]
        cot_rows = [chunk_of(cot_other, chunk) for chunk in range(chunks)]
    normed_one, projected = project(x_rows, norm_params, weights_qkv)

    if model_size == 2:
        core_here = lax.axis_index("dp") & 1
        rows_half = weights_out.shape[0] // 2
        piece = lax.dynamic_slice_in_dim(weights_out, core_here * rows_half, rows_half, 0)

    context, totals = [], []
    ahead = projected
    for chunk in range(chunks):
        part, total = attend(ahead, lengths, skew, chunk, chunks)
        context.append(part)
        totals.append(total)
        ahead = after(ahead, part, cot_other)
    if model_size == 2:
        piece = swap(after(piece, cot_other, context[0]), "mp", 1)
        paired = swap(after(piece, context[1], *cot_rows), "dp", 1)
        branch_weights = [weights_out, piece, paired]
    else:
        branch_weights = [lax.all_gather(weights_out, "mp", axis=1, tiled=True)]
    contexts = []
    for part in context:
        if model_size == 2:
            contexts.append([part, swap(after(part, *[pair[1] for pair in contexts[-1:]]), "mp", 1)])
        else:
            contexts.append([lax.all_gather(part, "mp", axis=1, tiled=True)])

    core = jnp.reshape(lax.axis_index("dp") & 1, (1,))
    ffn = []
    ahead = after(w_ffn, context[-1])
    for chunk in range(chunks):
        ffn.append(
            feed_forward(x_rows[chunk], contexts[chunk], branch_weights, cot_rows[chunk], norm_params, ahead, core)
        )
        ahead = after(ahead, ffn[-1][4])
    middle, normed_two, hidden, pre_grad, two_part, out_part = zip(*ffn)
    two_other = [other_part(after(two_part[0], contexts[-1][-1]))]
    order = device_ring(data_size)
    chips = chip_ring(data_size // 2)
    cores = [[2 * chip + core for chip in chips] for core in range(2)]
    units = w_ffn.shape[2]
    (ffn_grad,) = weight_sums(normed_two, pre_grad, order, 2 * units, 0)
    ffn_grad, sent, _ = lax.optimization_barrier((ffn_grad, two_part[1], two_other[0]))
    two_other.append(other_part(sent))
    (ffn_grad,) = weight_sums(cot_rows, hidden, order, 2 * units, units, [ffn_grad])
    ffn_share = sum_over_clips(ffn_grad, [order])

    if model_size == 2:
        out_kept, out_sent = in_order(*out_part)
    else:
        out_got = lax.psum_scatter(jnp.concatenate(out_part), "mp", scatter_dimension=0, tiled=True)
    middle_grad, branch_grad, context_grad = [], [], []

    def middle_step(chunk, *others):
        whole, sent, grad, sums = middle_back(
            after(two_part[chunk], *others), two_other[chunk], middle[chunk], cot_rows[chunk], norm_params, weights_out
        )
        middle_grad.append(whole)
        branch_grad.append(sent)
        context_grad.append(grad)
        return sums

    def back(chunk, others, before=()):
        grad = after(context_grad[chunk], *others)
        return attend_back(projected, grad, context[chunk], totals[chunk], lengths, skew_back, chunk, chunks, before)

    sums_two = [middle_step(0, ffn_grad)]
    *before, diagonal = back(0, [])
    diagonals = [diagonal]
    sums_two.append(middle_step(1, diagonal))
    if model_size == 2:
        out_got = swap(after(out_sent, sums_two[-1]), "mp", 1)
    halves = weight_sums(branch_grad, in_hbm(*context), cores[0] + cores[1], 4 * width_local, 3 * width_local, core=core)
    context_grad[1], *halves = lax.optimization_barrier((context_grad[1], *halves))
    grads, diagonal = back(1, [], before)
    diagonals.append(diagonal)
    sent, kept = weight_sums(
        in_hbm(*normed_one), [in_hbm(after(grads, out_got))], cores[0] + cores[1], 4 * width_local, 0, halves, core=core
    )
    halves = (kept, swap(after(sent, ffn_share), "dp", 1))
    grads = after(grads, kept)

    one = jnp.reshape(own_first * 0, (1,))
    place = one + lax.axis_index("dp")
    scale_factor = 1.0 / math.sqrt(float(seq_len * data_size))
    def attention_sums(*others):
        total = after(halves[0], *others).astype(f32) + halves[1].astype(f32)
        return sum_over_clips(total.astype(bf16), cores)

    if model_size == 2:
        sent, sums_sent = first_back(grads, weights_qkv, inputs_other, rows_local - own_first)
        got = swap(sent, "mp", 1)
        attention_share = attention_sums(sent)
        kept, sums_kept = first_back(after(grads, sent), weights_qkv, inputs, own_first)
        sums_one = [sums_sent, sums_kept]
        own = one + lax.axis_index("mp")
        output_rows = in_order(*[after(rows, kept) for rows in middle])[0] + out_kept.astype(f32) + out_got.astype(f32)
    else:
        sent, sums_sent = first_back(grads, weights_qkv, jnp.concatenate(x_rows), own_first * 0)
        attention_share = attention_sums(sent)
        sums_one = [sums_sent]
        kept = lax.psum_scatter(sent, "mp", scatter_dimension=0, tiled=True)
        got = jnp.zeros_like(kept)
        own = one
        middle_grad = [lax.dynamic_slice_in_dim(jnp.concatenate(middle_grad), own_first, rows_local, 0)] * 2
        middle_own = lax.dynamic_slice_in_dim(jnp.concatenate(middle), own_first, rows_local, 0)
        output_rows = middle_own + out_got.astype(f32)

    reversed_buckets = jnp.pad(buckets[::-1], (0, 1), constant_values=-1)[None, :]
    small = pack_small(sums_one, sums_two, diagonals, reversed_buckets, rel_bias.shape[1], head_first, model_size)
    exchanged = swap(small, "dp", 1)
    ffn_results = update(after(ffn_share, small), [(w_ffn, momentum_ffn, average_ffn)], place, [0.05 * scale_factor])
    small = after(small, ffn_results[0]) + exchanged
    exchanged = swap(small, "dp", 2)
    output = output_rows.astype(bf16)
    small = after(small, output) + exchanged
    exchanged = swap(small, "dp", 4)
    input_grad = finish(got, after(kept, small), inputs, norm_params, middle_grad, own)
    small = after(small, input_grad) + exchanged
    bit = 8
    while bit < data_size:
        small = small + swap(small, "dp", bit)
        bit *= 2
    attention_results = update(
        attention_share,
        [(w_qkv, momentum_qkv, average_qkv), (w_out, momentum_out, average_out)],
        place,
        [0.3 * scale_factor, 0.1 * scale_factor],
    )
    for bit in range(model_size.bit_length() - 1):
        exchanged = swap(small, "mp", 1 << bit)
        small = after(small, attention_results[0]) + exchanged
    small_results = small_update(
        small,
        (norm_params, momentum_norms, average_norms),
        (rel_bias.T, momentum_bias.T, average_bias.T),
        0.05 * scale_factor,
    )
    small_results = [*small_results[:4], *[result.T for result in small_results[4:]]]
    return (output, input_grad, *attention_results, *ffn_results, *small_results)


def solution(mesh):
    return jax.shard_map(
        per_device,
        mesh=mesh,
        in_specs=(
            P(("dp", "mp"), None),
            P(("dp", "mp"), None),
            P("dp"),
            P(),
            P(None, None, "mp"),
            P(None, "mp"),
            P(None, None, "mp"),
            P(),
            P(),
            P(None, "dp", "mp"),
            P("dp", "mp"),
            P(None, "dp", "mp"),
            P(),
            P(),
            P(None, "dp", "mp"),
            P("dp", "mp"),
            P(None, "dp", "mp"),
            P(),
            P(),
        ),
        out_specs=(
            P(("dp", "mp"), None),
            P(("dp", "mp"), None),
            P(None, "dp", "mp"),
            P(None, "dp", "mp"),
            P(None, "dp", "mp"),
            P(None, "dp", "mp"),
            P("dp", "mp"),
            P("dp", "mp"),
            P("dp", "mp"),
            P("dp", "mp"),
            P(None, "dp", "mp"),
            P(None, "dp", "mp"),
            P(None, "dp", "mp"),
            P(None, "dp", "mp"),
            P(),
            P(),
            P(),
            P(),
            P(),
            P(),
            P(),
            P(),
        ),
        check_vma=False,
    )
```
